32 devices in a mesh: dp: 8 (over z, y), blk: 4 (over x, core).
Axes of the slice: x: 2, y: 2, z: 4, core: 2. Of those that a mesh axis runs over, the one named last changes fastest.
Arguments:
- hidden: bfloat16 [1024, 16, 768], P('blk', 'dp'), may hold values from -6 to 6
- side_state: bfloat16 [1024, 16, 96], P('blk', 'dp'), may hold values from -6 to 6
- doc_lengths: int32 [16, 8], P('dp'), may hold values from 1 to 832, 1024 in all within a row
- norm_in: bfloat16 [768], replicated, may hold values from 0.099609375 to 1.8984375
- w_query: bfloat16 [768, 768], replicated, may hold values from -0.21875 to 0.21875
- w_key: bfloat16 [768, 768], replicated, may hold values from -0.21875 to 0.21875
- w_value: bfloat16 [768, 768], replicated, may hold values from -0.21875 to 0.21875
- w_out: bfloat16 [768, 768], replicated, may hold values from -0.875 to 0.875
- norm_mid: bfloat16 [768], replicated, may hold values from 0.099609375 to 1.8984375
- w_inner: bfloat16 [768, 3072], replicated, may hold values from -0.21875 to 0.21875
- w_outer: bfloat16 [3072, 768], replicated, may hold values from -0.109375 to 0.109375
- w_down: bfloat16 [768, 96], replicated, may hold values from -0.21875 to 0.21875
- gate: float32 [96], replicated, may hold values from -4 to 4
- side_norm_in: float32 [96], replicated, may hold values from 0.1 to 1.9
- s_query: bfloat16 [96, 96], replicated, may hold values from -0.625 to 0.625
- s_key: bfloat16 [96, 96], replicated, may hold values from -0.625 to 0.625
- s_value: bfloat16 [96, 96], replicated, may hold values from -0.625 to 0.625
- s_out: bfloat16 [96, 96], replicated, may hold values from -1.75 to 1.75
- side_norm_mid: float32 [96], replicated, may hold values from 0.1 to 1.9
- s_inner: bfloat16 [96, 384], replicated, may hold values from -0.625 to 0.625
- s_outer: bfloat16 [384, 96], replicated, may hold values from -0.3125 to 0.3125
- cotangent: bfloat16 [1024, 16, 96], P('blk', 'dp'), may hold values from -6 to 6
Outputs:
- backbone_out: bfloat16 [1024, 16, 768], P('blk', 'dp')
- side_out: bfloat16 [1024, 16, 96], P('blk', 'dp')
- state_grad: float32 [1024, 16, 96], P('blk', 'dp')
- grad_down: float32 [768, 96], replicated
- grad_gate: float32 [96], replicated
- grad_norm_in: float32 [96], replicated
- grad_query: float32 [96, 96], replicated
- grad_key: float32 [96, 96], replicated
- grad_value: float32 [96, 96], replicated
- grad_out: float32 [96, 96], replicated
- grad_norm_mid: float32 [96], replicated
- grad_inner: float32 [96, 384], replicated
- grad_outer: float32 [384, 96], replicated
The draws below stay inside these ranges and needn't reach their ends.
Inputs may be any that keep to these rules, and one draw needn't show every extreme that they name: `doc_lengths`: each row's 8 lengths sum to 1024, and each row has one document of exactly 832 tokens.
All inputs are finite; a program needn't handle non-finite values.
Results may differ from the reference program's by a relative error of at most 0.034.
Values may be sent and summed in bfloat16 or wider, within the bound.
No kernel may reach another device: no remote copies, remote signals or barrier semaphores. Data moves between devices by JAX's collectives and lax.ppermute only.
A program may use at most 128 MiB of HBM per device.

```python
import math
import jax
import jax.numpy as jnp
import numpy as np
from jax import lax

D = 768
HEADS = 12
FF = 3072
FS = 96
SHEADS = 12
SFF = 384
DOCS = 8
ROW_LEN = 1024
LONGEST = 832
ROWS_ALL = 16


def shard_levels(stream_key, extent, shards, least, high):
    level = 1.0
    for position, blocks in shards:
        heights = jax.random.uniform(jax.random.fold_in(jax.random.fold_in(stream_key, 6), position), (blocks,), jnp.float32, least / len(shards), high / len(shards))
        level = level * jnp.repeat(jnp.exp(heights), extent[position] // blocks).reshape((-1,) + (1,) * (len(extent) - 1 - position))
    return level


def length_profile(amount, total, reach, skew):
    loads = [(1 << 20) // math.isqrt(rank ** skew) + 1 for rank in range(2, amount + 1)]
    surplus, counts = total - reach - (amount - 1), [1] * (amount - 1)
    while surplus > 0:
        movable = [i for i in range(amount - 1) if counts[i] < reach]
        mass, left = sum([loads[i] for i in movable]), surplus
        for i in movable:
            more = min(reach - counts[i], max(1, left * loads[i] // mass), surplus)
            counts[i] = counts[i] + more
            surplus = surplus - more
    return np.array([reach] + counts)


def uneven_parts(stream_key, amount, total, bound, lean):
    if amount == 2:
        one = jax.random.randint(stream_key, (), max(1, total - bound), min(bound, total - 1) + 1)
        return jnp.stack([one, total - one])
    sizes = jnp.asarray(length_profile(amount, total, bound, lean), jnp.int32)
    pairs = (amount - 1) // 2
    giver, receiver = sizes[1:1 + 2 * pairs:2], sizes[2:2 + 2 * pairs:2]
    margin = jnp.minimum(giver - 1, bound - receiver)
    passed = jax.random.randint(jax.random.fold_in(stream_key, 1), (pairs,), 0, 1 << 20) % (margin + 1)
    sizes = sizes.at[1:1 + 2 * pairs:2].set(giver - passed).at[2:2 + 2 * pairs:2].set(receiver + passed)
    return sizes[jax.random.permutation(jax.random.fold_in(stream_key, 2), amount)]


def normal_values(key, shape, deviation, most, pieces=(), kind=jnp.bfloat16):
    factor_of = shard_levels(key, shape, pieces, -0.22, 0.18) if pieces else 1.0
    result = jax.random.normal(key, shape, jnp.float32) * deviation * factor_of
    return jnp.minimum(jnp.maximum(result, -most), most).astype(kind)


def setup_inputs(seed: int = 0) -> dict:
    key_list = jax.random.split(jax.random.key(seed), 23)
    hidden = normal_values(key_list[0], (ROW_LEN, ROWS_ALL, D), 1.0, 6.0, ((0, 4), (1, 8)))
    side_state = normal_values(key_list[1], (ROW_LEN, ROWS_ALL, FS), 1.0, 6.0, ((0, 4), (1, 8)))
    doc_lengths = jax.vmap(lambda own: uneven_parts(own, DOCS, ROW_LEN, LONGEST, 2))(jax.random.split(key_list[2], ROWS_ALL)).reshape((ROWS_ALL, DOCS)).astype(jnp.int32)
    norm_in = jnp.clip(1.0 + 0.18 * jax.random.normal(key_list[3], (D,), jnp.float32), 0.099609375, 1.8984375).astype(jnp.bfloat16)
    w_query = normal_values(key_list[4], (D, D), D ** -0.5, 0.21875)
    w_key = normal_values(key_list[5], (D, D), D ** -0.5, 0.21875)
    w_value = normal_values(key_list[6], (D, D), D ** -0.5, 0.21875)
    w_out = normal_values(key_list[7], (D, D), (D // 16) ** -0.5, 0.875)
    norm_mid = jnp.clip(1.0 + 0.18 * jax.random.normal(key_list[8], (D,), jnp.float32), 0.099609375, 1.8984375).astype(jnp.bfloat16)
    w_inner = normal_values(key_list[9], (D, FF), D ** -0.5, 0.21875)
    w_outer = normal_values(key_list[10], (FF, D), FF ** -0.5, 0.109375)
    w_down = normal_values(key_list[11], (D, FS), D ** -0.5, 0.21875)
    gate = normal_values(key_list[12], (FS,), 1.0, 4.0, (), jnp.float32)
    side_norm_in = jnp.clip(1.0 + 0.18 * jax.random.normal(key_list[13], (FS,), jnp.float32), 0.1, 1.9)
    s_query = normal_values(key_list[14], (FS, FS), FS ** -0.5, 0.625)
    s_key = normal_values(key_list[15], (FS, FS), FS ** -0.5, 0.625)
    s_value = normal_values(key_list[16], (FS, FS), FS ** -0.5, 0.625)
    s_out = normal_values(key_list[17], (FS, FS), (FS // 8) ** -0.5, 1.75)
    side_norm_mid = jnp.clip(1.0 + 0.18 * jax.random.normal(key_list[18], (FS,), jnp.float32), 0.1, 1.9)
    s_inner = normal_values(key_list[19], (FS, SFF), FS ** -0.5, 0.625)
    s_outer = normal_values(key_list[20], (SFF, FS), SFF ** -0.5, 0.3125)
    cotangent = normal_values(key_list[21], (ROW_LEN, ROWS_ALL, FS), 1.0, 6.0, ((0, 4), (1, 8)))
    return {"hidden": hidden, "side_state": side_state, "doc_lengths": doc_lengths, "norm_in": norm_in, "w_query": w_query, "w_key": w_key, "w_value": w_value, "w_out": w_out, "norm_mid": norm_mid, "w_inner": w_inner, "w_outer": w_outer, "w_down": w_down, "gate": gate, "side_norm_in": side_norm_in, "s_query": s_query, "s_key": s_key, "s_value": s_value, "s_out": s_out, "side_norm_mid": side_norm_mid, "s_inner": s_inner, "s_outer": s_outer, "cotangent": cotangent}


@jax.custom_vjp
def low(v):
    return lax.optimization_barrier(v.astype(jnp.bfloat16)).astype(jnp.float32)

@jax.custom_vjp
def low_back(v):
    return v

def low_keep(v):
    return (low(v), None)

def low_pass(kept, grad):
    return (grad,)

def back_keep(v):
    return (v, None)

def back_low(kept, grad):
    return (low(grad),)
low.defvjp(low_keep, low_pass)
low_back.defvjp(back_keep, back_low)
highest = lax.Precision.HIGHEST
eps_value = 1e-06
neg_fill = -1e+30

def matmul_hi(left_mat, right_mat):
    return jnp.dot(left_mat, right_mat, precision=highest)

def rms_norm(vector, gain_vec):
    return vector * lax.rsqrt(lax.optimization_barrier(jnp.mean(vector * vector, axis=-1, keepdims=True)) + eps_value) * gain_vec

def segment_ids(lengths_row, seq_len):
    doc_ends = jnp.cumsum(lengths_row, dtype=jnp.int32)
    positions = jnp.arange(seq_len, dtype=jnp.int32)
    return lax.optimization_barrier(jnp.sum((positions[:, None] >= doc_ends[None, :]).astype(jnp.int32), axis=1, dtype=jnp.int32))

def attend(queries, key_rows, value_rows, same_doc, head_count):
    seq_len = queries.shape[0]
    query_heads = queries.reshape(seq_len, head_count, -1)
    key_heads = key_rows.reshape(seq_len, head_count, -1)
    value_heads = value_rows.reshape(seq_len, head_count, -1)
    score_scale = query_heads.shape[-1] ** (-0.5)
    scores = low_back(jnp.einsum('qhe,khe->hqk', query_heads, key_heads, precision=highest) * score_scale)
    scores = jnp.where(same_doc[None], scores, neg_fill)
    row_max = lax.optimization_barrier(jnp.max(scores, axis=-1, keepdims=True))
    weights_exp = jnp.exp(scores - row_max)
    probs = weights_exp / lax.optimization_barrier(jnp.sum(weights_exp, axis=-1, keepdims=True))
    attended = jnp.einsum('hqk,khe->qhe', low(probs), value_heads, precision=highest)
    return attended.reshape(seq_len, -1)

def backbone_row(row_input, doc_row, frozen):
    norm_in, w_query, w_key, w_value, w_out, norm_mid, w_inner, w_outer = frozen
    normed = low(rms_norm(row_input, norm_in))
    queries = low(matmul_hi(normed, w_query))
    key_rows = low(matmul_hi(normed, w_key))
    value_rows = low(matmul_hi(normed, w_value))
    same_doc = doc_row[:, None] == doc_row[None, :]
    attended = low(attend(queries, key_rows, value_rows, same_doc, HEADS))
    after_attn = row_input + matmul_hi(attended, w_out)
    mid_normed = low(rms_norm(after_attn, norm_mid))
    inner_act = low(jax.nn.gelu(matmul_hi(mid_normed, w_inner), approximate=False))
    return (after_attn + matmul_hi(inner_act, w_outer)).astype(jnp.bfloat16)

def side_row(params, backbone_row_out, state_row, doc_row):
    w_down, gate, side_norm_in, s_query, s_key, s_value, s_out, side_norm_mid, s_inner, s_outer = params
    downed = low_back(matmul_hi(backbone_row_out, w_down))
    gate_open = jax.nn.sigmoid(gate)
    mixed = gate_open * downed + (1.0 - gate_open) * state_row
    side_normed = low(rms_norm(mixed, side_norm_in))
    queries = low_back(low(matmul_hi(side_normed, s_query)))
    key_rows = low_back(low(matmul_hi(side_normed, s_key)))
    value_rows = low_back(low(matmul_hi(side_normed, s_value)))
    same_doc = doc_row[:, None] == doc_row[None, :]
    attended = low_back(low(attend(queries, key_rows, value_rows, same_doc, SHEADS)))
    side_mid = mixed + low_back(matmul_hi(attended, s_out))
    mid_normed = low(rms_norm(side_mid, side_norm_mid))
    inner_pre = low_back(matmul_hi(mid_normed, s_inner))
    inner_act = low(jax.nn.gelu(inner_pre, approximate=False))
    return side_mid + low_back(matmul_hi(inner_act, s_outer))

def reference(hidden, side_state, doc_lengths, norm_in, w_query, w_key, w_value, w_out, norm_mid, w_inner, w_outer, w_down, gate, side_norm_in, s_query, s_key, s_value, s_out, side_norm_mid, s_inner, s_outer, cotangent):
    rows_input = jnp.transpose(hidden, (1, 0, 2)).astype(jnp.float32)
    doc_rows = jax.vmap(lambda lengths_row: segment_ids(lengths_row, ROW_LEN))(doc_lengths)
    frozen = tuple((weight.astype(jnp.float32) for weight in (norm_in, w_query, w_key, w_value, w_out, norm_mid, w_inner, w_outer)))
    backbone_rows = lax.map(lambda inputs_row: backbone_row(inputs_row[0], inputs_row[1], frozen), (rows_input, doc_rows))
    backbone_float = backbone_rows.astype(jnp.float32)
    params = tuple((weight.astype(jnp.float32) for weight in (w_down, gate, side_norm_in, s_query, s_key, s_value, s_out, side_norm_mid, s_inner, s_outer)))
    state_rows = jnp.transpose(side_state, (1, 0, 2)).astype(jnp.float32)

    def forward(params, states):
        row_function = jax.checkpoint(side_row)

        def scan_step(running, inputs_row):
            return (running, row_function(params, inputs_row[0], inputs_row[1], inputs_row[2]))
        _, outputs = lax.scan(scan_step, None, (backbone_float, states, doc_rows))
        return outputs
    side_rows, pullback = jax.vjp(forward, params, state_rows)
    grad_params, grad_states = pullback(jnp.transpose(cotangent, (1, 0, 2)).astype(jnp.float32))
    backbone_out = jnp.transpose(backbone_rows, (1, 0, 2))
    side_out = jnp.transpose(side_rows, (1, 0, 2)).astype(jnp.bfloat16)
    state_grad = jnp.transpose(grad_states, (1, 0, 2))
    grad_down, grad_gate, grad_norm_in, grad_query, grad_key, grad_value, grad_out, grad_norm_mid, grad_inner, grad_outer = grad_params
    return (backbone_out, side_out, state_grad, grad_down, grad_gate, grad_norm_in, grad_query, grad_key, grad_value, grad_out, grad_norm_mid, grad_inner, grad_outer)
```

```python
from functools import partial

import jax
import jax.numpy as jnp
from jax import lax
from jax.sharding import PartitionSpec as P

HEADS = 12
SHEADS = 12


eps_value = 1e-06
neg_fill = -1e30


def product(left_mat, right_mat):
    return jnp.dot(left_mat, right_mat, preferred_element_type=jnp.float32)


def over_tokens(left_mat, right_mat):
    return lax.dot_general(
        left_mat, right_mat, (((0,), (0,)), ((), ())), preferred_element_type=jnp.float32
    )


def times_transposed(left_mat, right_mat):
    return lax.dot_general(
        left_mat, right_mat, (((1,), (1,)), ((), ())), preferred_element_type=jnp.float32
    )


def norm_rows(vector, gain_vec):
    return (
        vector * lax.rsqrt(jnp.mean(vector * vector, axis=-1, keepdims=True) + eps_value) * gain_vec
    )


def doc_ids(lengths, first_pos, span_len):
    doc_ends = jnp.cumsum(lengths, axis=1, dtype=jnp.int32)
    positions = first_pos + jnp.arange(span_len, dtype=jnp.int32)
    return jnp.sum(
        (positions[None, :, None] >= doc_ends[:, None, :]).astype(jnp.int32),
        axis=2,
        dtype=jnp.int32,
    )


def sum_everywhere(parts):
    flat = jnp.concatenate([part.reshape(-1) for part in parts])
    count = flat.shape[0]
    lanes = 128
    rows = -(-count // (lanes * 32)) * 32
    low = jnp.pad(flat, (0, rows * lanes - count)).reshape(2, rows // 2, lanes).astype(jnp.bfloat16)
    place = lax.axis_index("blk")
    keep = lax.dynamic_index_in_dim(low, place % 2, 0, keepdims=False)
    send = lax.dynamic_index_in_dim(low, 1 - place % 2, 0, keepdims=False)
    blk_size, dp_size = lax.axis_size("blk"), lax.axis_size("dp")

    def swap(value, axis, size, hop):
        return lax.ppermute(value, axis, [(i, i ^ hop) for i in range(size)])

    def add(left, right):
        return (left.astype(jnp.float32) + right.astype(jnp.float32)).astype(jnp.bfloat16)

    half = add(keep, swap(send, "blk", blk_size, 1))
    for axis, size, start in (("blk", blk_size, 2), ("dp", dp_size, 1)):
        hop = start
        while hop < size:
            half = add(half, swap(half, axis, size, hop))
            hop *= 2
    other = swap(half, "blk", blk_size, 1)
    first = place % 2 == 0
    whole = jnp.concatenate([jnp.where(first, half, other), jnp.where(first, other, half)])
    whole = whole.reshape(-1).astype(jnp.float32)
    out, at = [], 0
    for part in parts:
        out.append(whole[at : at + part.size].reshape(part.shape))
        at += part.size
    return out


def per_device(
    hidden,
    side_state,
    doc_lengths,
    norm_in,
    w_query,
    w_key,
    w_value,
    w_out,
    norm_mid,
    w_inner,
    w_outer,
    w_down,
    gate,
    side_norm_in,
    s_query,
    s_key,
    s_value,
    s_out,
    side_norm_mid,
    s_inner,
    s_outer,
    cotangent,
):
    shard_len, row_count, model_width = hidden.shape
    side_width = side_state.shape[2]
    tokens = shard_len * row_count
    first_pos = lax.axis_index("blk") * shard_len
    doc_here = doc_ids(doc_lengths, first_pos, shard_len)
    inputs_flat = hidden.reshape(tokens, model_width).astype(jnp.float32)
    normed = norm_rows(inputs_flat, norm_in.astype(jnp.float32)).astype(jnp.bfloat16)
    queries = product(normed, w_query).astype(jnp.bfloat16).reshape(shard_len, row_count, HEADS, -1)
    score_scale = queries.shape[-1] ** (-0.5)
    key_local = (
        product(normed, w_key).astype(jnp.bfloat16).reshape(shard_len, row_count, model_width)
    )
    value_local = (
        product(normed, w_value).astype(jnp.bfloat16).reshape(shard_len, row_count, model_width)
    )
    key_rows = lax.all_gather(key_local, "blk", axis=0, tiled=True)
    span_len = key_rows.shape[0]
    key_heads = key_rows.reshape(span_len, row_count, HEADS, -1)
    value_heads = lax.all_gather(value_local, "blk", axis=0, tiled=True).reshape(
        span_len, row_count, HEADS, -1
    )
    doc_there = doc_ids(doc_lengths, jnp.int32(0), span_len)
    same_doc = doc_here[:, None, :, None] == doc_there[:, None, None, :]
    scores = (
        jnp.einsum("qrhe,krhe->rhqk", queries, key_heads, preferred_element_type=jnp.float32)
        * score_scale
    )
    scores = jnp.where(same_doc, scores, neg_fill)
    max_old = jnp.full((row_count, HEADS, shard_len), neg_fill, jnp.float32)
    max_new = jnp.maximum(max_old, jnp.max(scores, axis=-1))
    weights_exp = jnp.where(same_doc, jnp.exp(scores - max_new[..., None]), 0.0)
    total_new = jnp.sum(weights_exp, axis=-1)
    accum_new = jnp.einsum(
        "rhqk,krhe->rhqe",
        weights_exp.astype(jnp.bfloat16),
        value_heads,
        preferred_element_type=jnp.float32,
    )
    attended = accum_new / total_new[..., None]
    attended = (
        jnp.transpose(attended, (2, 0, 1, 3)).reshape(tokens, model_width).astype(jnp.bfloat16)
    )
    after_attn = inputs_flat + product(attended, w_out)
    mid_normed = norm_rows(after_attn, norm_mid.astype(jnp.float32)).astype(jnp.bfloat16)
    inner_act = jax.nn.gelu(product(mid_normed, w_inner), approximate=False).astype(jnp.bfloat16)
    backbone_flat = (after_attn + product(inner_act, w_outer)).astype(jnp.bfloat16)
    downed = product(backbone_flat, w_down)
    gate_open = jax.nn.sigmoid(gate)
    state_flat = side_state.reshape(tokens, side_width).astype(jnp.float32)
    mixed = gate_open * downed + (1.0 - gate_open) * state_flat
    side_normed = norm_rows(mixed, side_norm_in).astype(jnp.bfloat16)
    side_query = product(side_normed, s_query).astype(jnp.bfloat16)
    side_key = product(side_normed, s_key).astype(jnp.bfloat16)
    side_value = product(side_normed, s_value).astype(jnp.bfloat16)
    all_keys, all_values = (
        lax.all_gather(
            side_key.reshape(shard_len, row_count * side_width), "blk", axis=0, tiled=True
        ),
        lax.all_gather(
            side_value.reshape(shard_len, row_count * side_width), "blk", axis=0, tiled=True
        ),
    )
    seq_len = all_keys.shape[0]
    query_heads = side_query.reshape(shard_len, row_count, SHEADS, -1)
    key_heads = all_keys.reshape(seq_len, row_count, SHEADS, -1)
    value_heads = all_values.reshape(seq_len, row_count, SHEADS, -1)
    side_scale = query_heads.shape[-1] ** (-0.5)
    doc_all = doc_ids(doc_lengths, 0, seq_len)
    same_doc = doc_here[:, None, :, None] == doc_all[:, None, None, :]
    scores = (
        jnp.einsum("qrhe,krhe->rhqk", query_heads, key_heads, preferred_element_type=jnp.float32)
        * side_scale
    )
    scores = jnp.where(same_doc, scores, neg_fill)
    row_max = jnp.max(scores, axis=-1, keepdims=True)
    weights_exp = jnp.exp(scores - row_max)
    row_total = jnp.sum(weights_exp, axis=-1, keepdims=True)
    probs = weights_exp / row_total
    probs_low = probs.astype(jnp.bfloat16)
    side_attn = jnp.einsum(
        "rhqk,krhe->qrhe", probs_low, value_heads, preferred_element_type=jnp.float32
    )
    side_attn = side_attn.reshape(tokens, side_width).astype(jnp.bfloat16)
    side_mid = mixed + product(side_attn, s_out)
    side_mid_normed = norm_rows(side_mid, side_norm_mid).astype(jnp.bfloat16)
    inner_pre = product(side_mid_normed, s_inner)
    gelu_exact = partial(jax.nn.gelu, approximate=False)
    side_act = gelu_exact(inner_pre).astype(jnp.bfloat16)
    side_flat = side_mid + product(side_act, s_outer)
    grad_flat = cotangent.reshape(tokens, side_width).astype(jnp.float32)
    grad_low = cotangent.reshape(tokens, side_width)
    grad_outer = over_tokens(side_act, grad_low)
    grad_act = times_transposed(grad_low, s_outer)
    grad_pre = jax.vjp(gelu_exact, inner_pre)[1](grad_act)[0].astype(jnp.bfloat16)
    grad_inner = over_tokens(side_mid_normed, grad_pre)
    grad_mid_normed = times_transposed(grad_pre, s_inner)
    mid_pull = jax.vjp(norm_rows, side_mid, side_norm_mid)[1]
    grad_mid_part, grad_norm_mid = mid_pull(grad_mid_normed)
    grad_mid = grad_flat + grad_mid_part
    grad_mid_low = grad_mid.astype(jnp.bfloat16)
    grad_out = over_tokens(side_attn, grad_mid_low)
    grad_attn = (
        times_transposed(grad_mid_low, s_out)
        .astype(jnp.bfloat16)
        .reshape(shard_len, row_count, SHEADS, -1)
    )
    grad_probs = jnp.einsum(
        "qrhe,krhe->rhqk", grad_attn, value_heads, preferred_element_type=jnp.float32
    )
    row_terms = jnp.sum(probs * grad_probs, axis=-1, keepdims=True)
    grad_scores = (probs * (grad_probs - row_terms)).astype(jnp.bfloat16)
    grad_query_rows = (
        jnp.einsum("rhqk,krhe->qrhe", grad_scores, key_heads, preferred_element_type=jnp.float32)
        * side_scale
    )
    grad_query_rows = grad_query_rows.reshape(tokens, side_width).astype(jnp.bfloat16)
    grad_key_all = (
        jnp.einsum("rhqk,qrhe->krhe", grad_scores, query_heads, preferred_element_type=jnp.float32)
        * side_scale
    )
    grad_value_all = jnp.einsum(
        "rhqk,qrhe->krhe", probs_low, grad_attn, preferred_element_type=jnp.float32
    )
    stacked = jnp.concatenate(
        [
            grad_key_all.reshape(seq_len, row_count * side_width),
            grad_value_all.reshape(seq_len, row_count * side_width),
        ],
        axis=1,
    )
    mine = lax.psum_scatter(
        stacked.astype(jnp.bfloat16), "blk", scatter_dimension=0, tiled=True
    ).astype(jnp.float32)
    grad_key_rows = (
        mine[:, : row_count * side_width].reshape(tokens, side_width).astype(jnp.bfloat16)
    )
    grad_value_rows = (
        mine[:, row_count * side_width :].reshape(tokens, side_width).astype(jnp.bfloat16)
    )
    grad_query = over_tokens(side_normed, grad_query_rows)
    grad_key = over_tokens(side_normed, grad_key_rows)
    grad_value = over_tokens(side_normed, grad_value_rows)
    grad_normed = (
        times_transposed(grad_query_rows, s_query)
        + times_transposed(grad_key_rows, s_key)
        + times_transposed(grad_value_rows, s_value)
    )
    in_pull = jax.vjp(norm_rows, mixed, side_norm_in)[1]
    grad_mixed_part, grad_norm_in = in_pull(grad_normed)
    grad_mixed = grad_mid + grad_mixed_part
    state_grad = (1.0 - gate_open) * grad_mixed
    grad_downed = (gate_open * grad_mixed).astype(jnp.bfloat16)
    grad_down = over_tokens(backbone_flat, grad_downed)
    grad_gate = jnp.sum(grad_mixed * (downed - state_flat), axis=0) * gate_open * (1.0 - gate_open)
    parts = (
        grad_down,
        grad_gate,
        grad_norm_in,
        grad_query,
        grad_key,
        grad_value,
        grad_out,
        grad_norm_mid,
        grad_inner,
        grad_outer,
    )
    summed = sum_everywhere(parts)
    backbone_out = backbone_flat.reshape(shard_len, row_count, model_width)
    side_out = side_flat.astype(jnp.bfloat16).reshape(shard_len, row_count, side_width)
    state_out = state_grad.reshape(shard_len, row_count, side_width)
    return (
        backbone_out,
        side_out,
        state_out,
        summed[0],
        summed[1],
        summed[2],
        summed[3],
        summed[4],
        summed[5],
        summed[6],
        summed[7],
        summed[8],
        summed[9],
    )


def solution(mesh):
    return jax.shard_map(
        per_device,
        mesh=mesh,
        in_specs=(
            P("blk", "dp", None),
            P("blk", "dp", None),
            P("dp", None),
            P(),
            P(),
            P(),
            P(),
            P(),
            P(),
            P(),
            P(),
            P(),
            P(),
            P(),
            P(),
            P(),
            P(),
            P(),
            P(),
            P(),
            P(),
            P("blk", "dp", None),
        ),
        out_specs=(
            P("blk", "dp", None),
            P("blk", "dp", None),
            P("blk", "dp", None),
            P(),
            P(),
            P(),
            P(),
            P(),
            P(),
            P(),
            P(),
            P(),
            P(),
        ),
        check_vma=False,
    )
```

```python
import math

import jax
import jax.numpy as jnp
from jax import lax
from jax.experimental import pallas as pl
from jax.experimental.pallas import tpu as pltpu
from jax.sharding import PartitionSpec as P

HEADS = 12
SHEADS = 12
EPS = 1e-06
LOG2E = math.log2(math.e)
FAR = 2.0**100
LOW_TOTAL, HIGH_TOTAL = 2.0**-80, 2.0**100
VMEM_BYTES = 60 * 2**20

f32, bf16, i32 = jnp.float32, jnp.bfloat16, jnp.int32


def nn(left, right):
    return jnp.dot(left, right, preferred_element_type=f32)


def nt(left, right):
    return lax.dot_general(left, right, (((1,), (1,)), ((), ())), preferred_element_type=f32)


def ones_where(condition):
    return jnp.where(condition, 1.0, 0.0).astype(bf16)


def iota(shape, dim):
    return lax.broadcasted_iota(i32, shape, dim)


def eye(size):
    return ones_where(iota((size, size), 0) == iota((size, size), 1))


def norm_lanes(value, gain):
    return value * lax.rsqrt(jnp.mean(value * value, axis=1, keepdims=True) + EPS) * gain


def gelu(value):
    return 0.5 * value * (1.0 + lax.erf(value * math.sqrt(0.5)))


def gelu_slope(value):
    bell = jnp.exp2(value * value * (-0.5 * LOG2E)) * (1.0 / math.sqrt(2.0 * math.pi))
    return 0.5 * (1.0 + lax.erf(value * math.sqrt(0.5))) + value * bell


def kernel_call(body, outs, ins, *, scratch=(), whole=(), scalars=(), cost=(0, 0, 0)):
    specs = [
        pl.BlockSpec(
            memory_space=pl.ANY if i in whole else pltpu.SMEM if i in scalars else pltpu.VMEM
        )
        for i in range(len(ins))
    ]
    return pl.pallas_call(
        body,
        out_shape=[jax.ShapeDtypeStruct(shape, kind) for shape, kind in outs],
        in_specs=specs,
        out_specs=[pl.BlockSpec(memory_space=pltpu.VMEM)] * len(outs),
        scratch_shapes=list(scratch),
        compiler_params=pltpu.CompilerParams(vmem_limit_bytes=VMEM_BYTES),
        cost_estimate=pl.CostEstimate(flops=cost[0], bytes_accessed=cost[1], transcendentals=cost[2]),
    )(*ins)


def doubled(rows, columns, feature, transposed):
    wide, thin = iota((rows, columns), 0), iota((rows, columns), 1)
    if not transposed:
        wide, thin = thin, wide
    source = (wide // (2 * feature)) * feature + wide % feature
    return ones_where(source == thin)


def prepare_body(
    w_value, w_down, s_query, s_key, s_value, s_out, s_inner, s_outer, value_t, dup, dup_t, tall_t, wide_t
):
    width, side = w_down.shape
    feature = side // SHEADS
    hidden = s_inner.shape[1]
    value_t[...] = nt(eye(width), w_value[...]).astype(bf16)
    spread = doubled(side, dup.shape[1], feature, False)
    dup[0:side] = nn(s_key[...], spread).astype(bf16)
    dup[side : 2 * side] = nn(s_value[...], spread).astype(bf16)
    spread_t = doubled(2 * side, side, feature, True)
    for i, weight in enumerate((s_query, s_key, s_value)):
        dup_t[2 * side * i : 2 * side * (i + 1)] = nt(spread_t, weight[...]).astype(bf16)
    one = eye(side)
    tall_t[0:side] = nt(one, s_out[...]).astype(bf16)
    tall_t[side : side + hidden] = nt(eye(hidden), s_inner[...]).astype(bf16)
    wide_t[:, 0:hidden] = nt(one, s_outer[...]).astype(bf16)
    wide_t[:, hidden : hidden + width] = nt(one, w_down[...]).astype(bf16)


def project(tokens, gain, w_query, w_key, value_t, scale, queries):
    normed = norm_lanes(tokens.astype(f32), gain.astype(f32)).astype(bf16)
    query = (nn(normed[0:queries], w_query[...]) * scale).astype(bf16)
    return query, nn(normed, w_key[...]).astype(bf16), nt(value_t[...], normed).astype(bf16)


def first_body(own, mate, norm_in, w_query, w_key, value_t, query, key, value):
    span, width = own.shape
    scale = LOG2E * (width // HEADS) ** -0.5
    tokens = jnp.concatenate([own[...], mate[...]], axis=0)
    query[...], key[...], value[...] = project(
        tokens, norm_in[...], w_query, w_key, value_t, scale, span
    )


def bounds(doc_lengths, row):
    starts, ends, at = [], [], jnp.int32(0)
    for d in range(doc_lengths.shape[1]):
        starts.append(at)
        at = at + doc_lengths[row, d]
        ends.append(at)
    return starts, ends


def in_doc(doc_lengths, row, blocks, span, shape, token_dim):
    starts, ends = bounds(doc_lengths, row)
    parts = []
    part_shape = list(shape)
    part_shape[token_dim] = span
    number = iota(tuple(part_shape), 1 - token_dim)
    first = jnp.zeros(tuple(part_shape), i32)
    last = first
    for d, (start, end) in enumerate(zip(starts, ends)):
        first = jnp.where(number == d, start, first)
        last = jnp.where(number == d, end, last)
    for block in blocks:
        position = iota(tuple(part_shape), token_dim) + block * span
        parts.append(jnp.where((position >= first) & (position < last), 1.0, 0.0))
    return jnp.concatenate(parts, axis=token_dim)


def out_of_range(totals):
    lowest, highest = jnp.min(totals), jnp.max(totals)
    return jnp.logical_not((lowest > LOW_TOTAL) & (highest < HIGH_TOTAL))


def backbone_body(
    doc_lengths,
    own,
    far,
    far_mate,
    query_own,
    key_near,
    value_near,
    norm_in,
    w_query,
    w_key,
    value_t,
    norm_mid,
    wide_t,
    columns,
    state_own,
    side_far,
    w_out_hbm,
    w_inner_hbm,
    w_outer_hbm,
    out_own,
    out_far,
    sn_rows,
    sn_t,
    mixed_t,
    lead_t,
    query,
    key,
    value,
    key_doc,
    query_doc,
    totals,
    attended,
    after,
    w_out,
    w_inner,
    w_outer,
    sems,
):
    copies = [
        pltpu.make_async_copy(source, target, sems.at[i])
        for i, (source, target) in enumerate(
            ((w_out_hbm, w_out), (w_inner_hbm, w_inner), (w_outer_hbm, w_outer))
        )
    ]
    for copy in copies:
        copy.start()
    span, width = own.shape
    head = width // HEADS
    stride = value.shape[0] // HEADS
    place = lax.axis_index("blk")
    half = lax.axis_size("blk") // 2
    row = place // half
    near, opposite = place ^ 1, place ^ half
    opposite_near = opposite ^ 1

    tokens = jnp.concatenate([far[...], far_mate[...]], axis=0)
    query_far, key_far, value_far = project(
        tokens, norm_in[...], w_query, w_key, value_t, LOG2E * head**-0.5, span
    )
    query[0:span] = query_own[...]
    query[span : 2 * span] = query_far
    key[0 : 2 * span] = key_near[...]
    key[2 * span : 4 * span] = key_far
    for h in range(HEADS):
        base = h * stride
        value[base : base + head, 0 : 2 * span] = value_near[h * head : (h + 1) * head]
        value[base : base + head, 2 * span : 4 * span] = value_far[h * head : (h + 1) * head]
        value[base + head : base + stride] = jnp.ones((stride - head, 4 * span), bf16)
    keys_in = in_doc(doc_lengths, row, (place, near, opposite, opposite_near), span, (4 * span, 128), 0)
    key_doc[...] = (keys_in - 1.0).astype(bf16)
    query_doc[...] = (
        in_doc(doc_lengths, row, (place, opposite), span, (2 * span, 128), 0) * FAR
    ).astype(bf16)

    def attend(shifted):
        def pair(j, carry):
            lanes = pl.ds(pl.multiple_of(j * 128, 128), 128)
            keys = jnp.concatenate([key[:, lanes], key_doc[...]], axis=1)
            results = []
            for side in range(128 // head):
                mine = ones_where(iota((1, 128), 1) // head == side)
                queries = jnp.concatenate([query[:, lanes] * mine, query_doc[...]], axis=1)
                scores = nt(keys, queries)
                if shifted:
                    scores = scores - jnp.max(scores, axis=0, keepdims=True)
                weights = jnp.exp2(scores).astype(bf16)
                at = (j * (128 // head) + side) * stride
                summed = nn(value[pl.ds(pl.multiple_of(at, 16), stride), :], weights)
                total = summed[head : head + 1]
                slot = pl.multiple_of((j * (128 // head) + side) * 8, 8)
                totals[pl.ds(slot, 8), :] = summed[head : head + 8]
                results.append(summed[0:head] * (1.0 / total))
            joined = jnp.concatenate(results, axis=0)
            attended[:, lanes] = joined.T.astype(bf16)
            return carry

        lax.fori_loop(0, width // 128, pair, 0)

    attend(False)

    @pl.when(out_of_range(totals[...]))
    def _():
        attend(True)

    copies[0].wait()
    after[0:span] = own[...].astype(f32) + nn(attended[0:span], w_out[...])
    after[span : 2 * span] = far[...].astype(f32) + nn(attended[span : 2 * span], w_out[...])
    middle = norm_lanes(after[...], norm_mid[...].astype(f32)).astype(bf16)
    copies[1].wait()
    copies[2].wait()
    hidden = w_inner.shape[1]
    step = width
    result = after[...]
    for at in range(0, hidden, step):
        act = gelu(nn(middle, w_inner[:, at : at + step])).astype(bf16)
        result = result + nn(act, w_outer[at : at + step, :])
    out = result.astype(bf16)
    out_own[...] = out[0:span]
    out_far[...] = out[span : 2 * span]

    side = state_own.shape[1]
    skip = wide_t.shape[1] - width
    down_t = nt(wide_t[:, skip : skip + width], out)
    state_t = jnp.concatenate(
        [
            nt(eye(side), state_own[...]),
            nt(ones_where(iota((side, 2 * side), 0) == iota((side, 2 * side), 1)), side_far[...]),
        ],
        axis=1,
    )
    gate_open = jax.nn.sigmoid(columns[:, 0:1])
    mixed = gate_open * down_t + (1.0 - gate_open) * state_t
    normed = (
        mixed * lax.rsqrt(jnp.mean(mixed * mixed, axis=0, keepdims=True) + EPS) * columns[:, 1:2]
    )
    mixed_t[...] = mixed
    lead_t[...] = down_t - state_t
    sn_t[...] = normed.astype(bf16)
    sn_rows[...] = normed.T.astype(bf16)


def side_body(
    doc_lengths,
    sn_own,
    sn_mate,
    mixed_t,
    cot_own,
    side_far,
    dup,
    dup_t,
    tall_t,
    wide_t,
    s_out,
    s_inner,
    s_outer,
    columns,
    out_own,
    out_far,
    dquery,
    dkv_own,
    dkv_mate,
    dmid_t,
    early,
    weights,
    keys,
    values,
    key_t,
    value_t,
    query_t,
    query_s,
    query_h,
    attn_t,
    inverse,
    totals,
    dattn_s,
    dterm_s,
    dattn_h,
    dkv_t,
):
    tokens, side = sn_own.shape
    span = tokens // 2
    feature = side // SHEADS
    hidden = s_inner.shape[1]
    wide = 2 * side
    place = lax.axis_index("blk")
    half = lax.axis_size("blk") // 2
    row = place // half
    near, opposite = place ^ 1, place ^ half
    opposite_near = opposite ^ 1
    scale = feature**-0.5

    sn = jnp.concatenate([sn_own[...], sn_mate[...]], axis=0)
    lane = iota((2 * tokens, keys.shape[1]), 1)
    docs = in_doc(
        doc_lengths, row, (place, opposite, near, opposite_near), span, (2 * tokens, 128), 0
    )
    shift = wide % 128
    docs = pltpu.roll(docs, shift, 1)
    projected = nn(sn, dup[0:side]).astype(bf16)
    low_lane = iota((2 * tokens, 128), 1) < shift
    keys[:, 0:128] = projected[:, 0:128]
    keys[:, 128:256] = jnp.where(low_lane, projected[:, 128:256].astype(f32), docs - 1.0).astype(bf16)
    projected = nn(sn, dup[side : 2 * side]).astype(bf16)
    values[:, 0:128] = projected[:, 0:128]
    values[:, 128:256] = jnp.where(low_lane, projected[:, 128:256].astype(f32), 1.0).astype(bf16)
    key_t[...] = nt(dup_t[wide : 2 * wide], sn).astype(bf16)
    second = iota((wide, 2 * tokens), 0) % (2 * feature) >= feature
    value_t[...] = jnp.where(second, 1.0, nt(dup_t[2 * wide : 3 * wide], sn)).astype(bf16)
    query = nt(dup_t[0:wide], sn_own[...]).astype(bf16)
    query_t[...] = query
    scaled = query.astype(f32) * (scale * LOG2E)
    high = scaled.astype(bf16).astype(f32)
    second = iota((wide, tokens), 0) % (2 * feature) >= feature
    query_s[...] = jnp.where(second, scaled - high, high).astype(bf16)
    query_docs = in_doc(doc_lengths, row, (place, opposite), span, (16, tokens), 1) * FAR
    for i in range(2):
        query_h[i] = jnp.zeros(query_h.shape[1:], bf16)
        query_h[i, wide : wide + 16] = query_docs.astype(bf16)

    def attend(shifted):
        def pair(j, carry):
            for i in range(2):
                h = 2 * j + i
                rows = pl.ds(pl.multiple_of(h * 16, 16), 16)
                eight = pl.ds(pl.multiple_of(h * 8, 8), 8)
                query_h[i, rows, :] = query_s[rows, :]
                scores = nn(keys[...], query_h[i])
                query_h[i, rows, :] = jnp.zeros((16, tokens), bf16)
                if shifted:
                    scores = scores - jnp.max(scores, axis=0, keepdims=True)
                weight = jnp.exp2(scores).astype(bf16)
                weights[h] = weight
                summed = nn(value_t[rows, :], weight)
                total = summed[feature : 2 * feature]
                totals[eight, :] = total
                invert = 1.0 / total
                inverse[eight, :] = invert
                attn_t[eight, :] = summed[0:feature] * invert
            return carry

        lax.fori_loop(0, SHEADS // 2, pair, 0)

    attend(False)

    @pl.when(out_of_range(totals[...]))
    def _():
        attend(True)

    attn = attn_t[...]
    attn_low = attn.astype(bf16)
    mid = mixed_t[...] + nn(tall_t[0:side], attn_low)
    mid_scale = lax.rsqrt(jnp.mean(mid * mid, axis=0, keepdims=True) + EPS)
    gain = columns[:, 2:3]
    unit = mid * mid_scale
    normed = (unit * gain).astype(bf16)
    inner = nn(tall_t[side : side + hidden], normed)
    act = gelu(inner).astype(bf16)
    out = (mid + nn(wide_t[:, 0:hidden], act)).T.astype(bf16)
    out_own[...] = out[0:span]
    out_far[...] = out[span : 2 * span]

    pick = ones_where(iota((side, 2 * side), 0) + side == iota((side, 2 * side), 1))
    dy = jnp.concatenate([nt(eye(side), cot_own[...]), nt(pick, side_far[...])], axis=1)
    dy_low = dy.astype(bf16)
    early[:, hidden : 2 * hidden] = nt(dy_low, act)
    dinner = (gelu_slope(inner) * nn(s_outer[...], dy_low)).astype(bf16)
    early[:, 0:hidden] = nt(normed, dinner)
    dnormed = nn(s_inner[...], dinner)
    grad_gain = jnp.sum(dnormed * unit, axis=1, keepdims=True)
    scaled = dnormed * gain
    dmid = dy + mid_scale * (scaled - unit * jnp.mean(scaled * unit, axis=0, keepdims=True))
    dmid_t[...] = dmid
    dmid_low = dmid.astype(bf16)
    last = jnp.concatenate(
        [nt(attn_low, dmid_low), jnp.zeros((side, 128 - side), f32)], axis=1
    )
    early[:, 2 * hidden : 2 * hidden + 128] = jnp.where(
        iota((side, 128), 1) == side, grad_gain, last
    )
    dattn = nn(s_out[...], dmid_low).astype(bf16).astype(f32)

    number = iota((feature, tokens), 0)
    for h in range(SHEADS):
        eight = slice(h * feature, (h + 1) * feature)
        invert = inverse[eight, :]
        part = dattn[eight] * invert
        high = part.astype(bf16).astype(f32)
        dattn_s[h * 16 : (h + 1) * 16] = jnp.concatenate([high, part - high], axis=0).astype(bf16)
        term = -jnp.sum(dattn[eight] * attn[eight], axis=0, keepdims=True) * invert
        first = term.astype(bf16).astype(f32)
        rest = term - first
        middle = rest.astype(bf16).astype(f32)
        piece = jnp.where(
            number == 0, first, jnp.where(number == 1, middle, jnp.where(number == 2, rest - middle, 0.0))
        )
        dterm_s[h * 16 : (h + 1) * 16] = jnp.concatenate(
            [piece, jnp.zeros_like(piece)], axis=0
        ).astype(bf16)
    for i in range(2):
        dattn_h[i] = jnp.zeros(dattn_h.shape[1:], bf16)

    def back(j, carry):
        for i in range(2):
            h = 2 * j + i
            rows = pl.ds(pl.multiple_of(h * 16, 16), 16)
            eight = pl.ds(pl.multiple_of(h * 8, 8), 8)
            eight_v = pl.ds(pl.multiple_of(side + h * 8, 8), 8)
            dattn_h[i, rows, :] = dattn_s[rows, :]
            dattn_h[i, wide : wide + 16] = dterm_s[rows, :]
            slope = nn(values[...], dattn_h[i])
            dattn_h[i, rows, :] = jnp.zeros((16, tokens), bf16)
            weight = weights[h]
            dscores = (weight.astype(f32) * slope).astype(bf16)
            dquery[eight, :] = nn(key_t[rows, :], dscores)[0:feature] * scale
            dkv_t[eight, :] = nt(query_t[rows, :], dscores)[0:feature] * scale
            both = nt(dattn_s[rows, :], weight)
            dkv_t[eight_v, :] = both[0:feature] + both[feature : 2 * feature]
        return carry

    lax.fori_loop(0, SHEADS // 2, back, 0)
    dkv_own[...] = dkv_t[:, 0:tokens]
    dkv_mate[...] = dkv_t[:, tokens : 2 * tokens].astype(bf16)


def last_body(
    dquery,
    dkv_own,
    dkv_back,
    sn_t,
    dmid_t,
    mixed_t,
    lead_t,
    out_own,
    out_far,
    s_query,
    s_key,
    s_value,
    columns,
    early,
    state_own,
    state_far,
    keep,
    send,
    pack,
):
    side, tokens = sn_t.shape
    span = tokens // 2
    width = out_own.shape[1]
    dq = dquery[...].astype(bf16)
    dkv = (dkv_own[...].astype(bf16).astype(f32) + dkv_back[...].astype(f32)).astype(bf16)
    dk, dv = dkv[0:side], dkv[side : 2 * side]
    sn = sn_t[...]
    dnormed = nn(s_query[...], dq) + nn(s_key[...], dk) + nn(s_value[...], dv)
    mixed = mixed_t[...]
    mixed_scale = lax.rsqrt(jnp.mean(mixed * mixed, axis=0, keepdims=True) + EPS)
    unit = mixed * mixed_scale
    scaled = dnormed * columns[:, 1:2]
    dmixed = dmid_t[...] + mixed_scale * (
        scaled - unit * jnp.mean(scaled * unit, axis=0, keepdims=True)
    )
    gate_open = jax.nn.sigmoid(columns[:, 0:1])
    grad_gain = jnp.sum(dnormed * unit, axis=1, keepdims=True)
    grad_gate = jnp.sum(dmixed * lead_t[...], axis=1, keepdims=True) * gate_open * (1.0 - gate_open)
    state = ((1.0 - gate_open) * dmixed).T
    state_own[...] = state[0:span]
    state_far[...] = state[span : 2 * span]
    ddown = (gate_open * dmixed).astype(bf16)
    pack[:, 0:width] = nn(ddown[:, 0:span], out_own[...]) + nn(ddown[:, span:tokens], out_far[...])
    at = width
    blank = jnp.zeros((side, 128 - side), f32)
    for grad in (dq, dk, dv):
        pack[:, at : at + 128] = jnp.concatenate([nt(sn, grad), blank], axis=1)
        at += 128
    lane = iota((side, 128), 1)
    inner = early.shape[1] - 128
    vectors = early[:, inner : inner + 128]
    vectors = jnp.where(lane == side + 1, grad_gain, vectors)
    pack[:, at : at + 128] = jnp.where(lane == side + 2, grad_gate, vectors)
    pack[:, at + 128 : at + 128 + inner] = early[:, 0:inner]
    size = keep.shape[1]
    core = lax.axis_index("blk") % 2
    keep[...] = pack[:, pl.ds(pl.multiple_of(core * size, 128), size)].astype(bf16)
    send[...] = pack[:, pl.ds(pl.multiple_of((1 - core) * size, 128), size)].astype(bf16)


def spread_body(
    half, other, grad_down, grad_gate, gain_in, grad_query, grad_key, grad_value, grad_out, gain_mid, grad_inner, grad_outer
):
    side = grad_query.shape[0]
    width = grad_down.shape[0]
    hidden = grad_inner.shape[1]
    even = lax.axis_index("blk") % 2 == 0
    first = jnp.where(even, half[...].astype(f32), other[...].astype(f32))
    second = jnp.where(even, other[...].astype(f32), half[...].astype(f32))
    whole = jnp.concatenate([first, second], axis=1)
    grad_down[...] = whole[:, 0:width].T
    at = width
    for target in (grad_query, grad_key, grad_value):
        target[...] = whole[:, at : at + side]
        at += 128
    block = whole[:, at : at + 128]
    grad_out[...] = block[:, 0:side]
    rows = block.T
    gain_mid[...] = rows[side : side + 1]
    gain_in[...] = rows[side + 1 : side + 2]
    grad_gate[...] = rows[side + 2 : side + 3]
    at += 128
    grad_inner[...] = whole[:, at : at + hidden]
    grad_outer[...] = whole[:, at + hidden : at + 2 * hidden].T


def per_device(
    hidden,
    side_state,
    doc_lengths,
    norm_in,
    w_query,
    w_key,
    w_value,
    w_out,
    norm_mid,
    w_inner,
    w_outer,
    w_down,
    gate,
    side_norm_in,
    s_query,
    s_key,
    s_value,
    s_out,
    side_norm_mid,
    s_inner,
    s_outer,
    cotangent,
):
    span, rows, width = hidden.shape
    side = side_state.shape[2]
    ff = w_inner.shape[1]
    sff = s_inner.shape[1]
    tokens = 2 * span
    blk_size, dp_size = lax.axis_size("blk"), lax.axis_size("dp")
    half = blk_size // 2
    place = lax.axis_index("blk")
    row = place // half

    def swap(value, axis, size, hop):
        return lax.ppermute(value, axis, [(i, i ^ hop) for i in range(size)])

    def across(value):
        return swap(value, "blk", blk_size, half)

    def beside(value):
        return swap(value, "blk", blk_size, 1)

    def of_row(array, which):
        return lax.dynamic_index_in_dim(array, which, 1, keepdims=False)

    hidden_far = across(of_row(hidden, 1 - row))
    side_far = across(
        jnp.concatenate([of_row(side_state, 1 - row), of_row(cotangent, 1 - row)], axis=1)
    )
    hidden_own = of_row(hidden, row)
    hidden_mate = beside(hidden_own)
    state_own, cot_own = of_row(side_state, row), of_row(cotangent, row)
    columns = jnp.stack([gate, side_norm_in, side_norm_mid], axis=1)
    gain_in, gain_mid = norm_in.reshape(1, width), norm_mid.reshape(1, width)

    value_t, dup, dup_t, tall_t, wide_t = kernel_call(
        prepare_body,
        [
            ((width, width), bf16),
            ((2 * side, 256), bf16),
            ((6 * side, side), bf16),
            ((side + sff, side), bf16),
            ((side, sff + width), bf16),
        ],
        [w_value, w_down, s_query, s_key, s_value, s_out, s_inner, s_outer],
        cost=(2 * width**3, 4 * width * width, 0),
    )
    query_own, key_near, value_near = kernel_call(
        first_body,
        [((span, width), bf16), ((tokens, width), bf16), ((width, tokens), bf16)],
        [hidden_own, hidden_mate, gain_in, w_query, w_key, value_t],
        cost=(5 * tokens * width * width, 8 * width * width, 0),
    )
    far_mate = beside(hidden_far)
    stride = width // HEADS + 16
    out_own, out_far, sn_rows, sn_t, mixed_t, lead_t = kernel_call(
        backbone_body,
        [
            ((span, width), bf16),
            ((span, width), bf16),
            ((tokens, side), bf16),
            ((side, tokens), bf16),
            ((side, tokens), f32),
            ((side, tokens), f32),
        ],
        [
            doc_lengths,
            hidden_own,
            hidden_far,
            far_mate,
            query_own,
            key_near,
            value_near,
            gain_in,
            w_query,
            w_key,
            value_t,
            gain_mid,
            wide_t,
            columns,
            state_own,
            side_far,
            w_out,
            w_inner,
            w_outer,
        ],
        scalars=(0,),
        whole=(16, 17, 18),
        scratch=[
            pltpu.VMEM((tokens, width), bf16),
            pltpu.VMEM((2 * tokens, width), bf16),
            pltpu.VMEM((HEADS * stride, 2 * tokens), bf16),
            pltpu.VMEM((2 * tokens, 128), bf16),
            pltpu.VMEM((tokens, 128), bf16),
            pltpu.VMEM((HEADS * 8, tokens), f32),
            pltpu.VMEM((tokens, width), bf16),
            pltpu.VMEM((tokens, width), f32),
            pltpu.VMEM((width, width), bf16),
            pltpu.VMEM((width, ff), bf16),
            pltpu.VMEM((ff, width), bf16),
            pltpu.SemaphoreType.DMA((3,)),
        ],
        cost=(20 * 10**9, 16 * 10**6, 0),
    )
    sn_mate = beside(sn_rows)
    side_own, side_back, dquery, dkv_own, dkv_mate, dmid_t, early = kernel_call(
        side_body,
        [
            ((span, side), bf16),
            ((span, side), bf16),
            ((side, tokens), f32),
            ((2 * side, tokens), f32),
            ((2 * side, tokens), bf16),
            ((side, tokens), f32),
            ((side, 2 * sff + 128), f32),
        ],
        [
            doc_lengths,
            sn_rows,
            sn_mate,
            mixed_t,
            cot_own,
            side_far,
            dup,
            dup_t,
            tall_t,
            wide_t,
            s_out,
            s_inner,
            s_outer,
            columns,
        ],
        scalars=(0,),
        scratch=[
            pltpu.VMEM((SHEADS, 2 * tokens, tokens), bf16),
            pltpu.VMEM((2 * tokens, 256), bf16),
            pltpu.VMEM((2 * tokens, 256), bf16),
            pltpu.VMEM((2 * side, 2 * tokens), bf16),
            pltpu.VMEM((2 * side, 2 * tokens), bf16),
            pltpu.VMEM((2 * side, tokens), bf16),
            pltpu.VMEM((2 * side, tokens), bf16),
            pltpu.VMEM((2, 256, tokens), bf16),
            pltpu.VMEM((side, tokens), f32),
            pltpu.VMEM((side, tokens), f32),
            pltpu.VMEM((side, tokens), f32),
            pltpu.VMEM((2 * side, tokens), bf16),
            pltpu.VMEM((2 * side, tokens), bf16),
            pltpu.VMEM((2, 256, tokens), bf16),
            pltpu.VMEM((2 * side, 2 * tokens), f32),
        ],
        cost=(30 * 10**9, 3 * 10**6, 0),
    )
    dkv_back = beside(dkv_mate)
    packed = width + 4 * 128 + 2 * sff
    grad_own, grad_far, keep, send = kernel_call(
        last_body,
        [
            ((span, side), f32),
            ((span, side), f32),
            ((side, packed // 2), bf16),
            ((side, packed // 2), bf16),
        ],
        [
            dquery,
            dkv_own,
            dkv_back,
            sn_t,
            dmid_t,
            mixed_t,
            lead_t,
            out_own,
            out_far,
            s_query,
            s_key,
            s_value,
            columns,
            early,
        ],
        scratch=[pltpu.VMEM((side, packed), f32)],
        cost=(10**9, 3 * 10**6, 0),
    )

    def add(left, right):
        return (left.astype(f32) + right.astype(f32)).astype(bf16)

    total = add(keep, beside(send))
    for axis, size, hop in (("blk", blk_size, 2), ("dp", dp_size, 1)):
        while hop < size:
            total = add(total, swap(total, axis, size, hop))
            hop *= 2
    other = beside(total)
    vector = ((1, side), f32)
    square = ((side, side), f32)
    grads = kernel_call(
        spread_body,
        [
            ((width, side), f32),
            vector,
            vector,
            square,
            square,
            square,
            square,
            vector,
            ((side, sff), f32),
            ((sff, side), f32),
        ],
        [total, other],
        cost=(0, 2 * 10**6, 0),
    )
    grads = [grad.reshape(side) if grad.shape[0] == 1 else grad for grad in grads]

    def both_rows(own, far):
        first = jnp.where(row == 0, own, far)
        second = jnp.where(row == 0, far, own)
        return jnp.stack([first, second], axis=1)

    return (
        both_rows(out_own, across(out_far)),
        both_rows(side_own, across(side_back)),
        both_rows(grad_own, across(grad_far)),
        *grads,
    )


def solution(mesh):
    split = P("blk", "dp", None)
    return jax.shard_map(
        per_device,
        mesh=mesh,
        in_specs=(split, split, P("dp", None)) + (P(),) * 18 + (split,),
        out_specs=(split,) * 3 + (P(),) * 10,
        check_vma=False,
    )
```

```python
import math

import jax
import jax.numpy as jnp
from jax import lax
from jax.experimental import pallas as pl
from jax.experimental.pallas import tpu as pltpu
from jax.sharding import PartitionSpec as P

HEADS = 12
SHEADS = 12
EPS = 1e-06
LOG2E = math.log2(math.e)
FAR = 2.0**100
LOW_TOTAL, HIGH_TOTAL = 2.0**-80, 2.0**100

f32, bf16, i32 = jnp.float32, jnp.bfloat16, jnp.int32


def nn(left, right):
    return jnp.dot(left, right, preferred_element_type=f32)


def nt(left, right):
    return lax.dot_general(left, right, (((1,), (1,)), ((), ())), preferred_element_type=f32)


def tn(left, right):
    return lax.dot_general(left, right, (((0,), (0,)), ((), ())), preferred_element_type=f32)


def ones_where(condition):
    return jnp.where(condition, 1.0, 0.0).astype(bf16)


def iota(shape, dim):
    return lax.broadcasted_iota(i32, shape, dim)


def eye(size):
    return ones_where(iota((size, size), 0) == iota((size, size), 1))


def norm_lanes(value, gain):
    return value * lax.rsqrt(jnp.mean(value * value, axis=1, keepdims=True) + EPS) * gain


def gelu(value):
    return 0.5 * value * (1.0 + lax.erf(value * math.sqrt(0.5)))


def gelu_slope(value):
    bell = jnp.exp2(value * value * (-0.5 * LOG2E)) * (1.0 / math.sqrt(2.0 * math.pi))
    return 0.5 * (1.0 + lax.erf(value * math.sqrt(0.5))) + value * bell


def kernel_call(body, outs, ins, *, vmem, scratch=(), whole=(), scalars=(), cost=(0, 0, 0)):
    specs = [
        pl.BlockSpec(
            memory_space=pl.ANY if i in whole else pltpu.SMEM if i in scalars else pltpu.VMEM
        )
        for i in range(len(ins))
    ]
    return pl.pallas_call(
        body,
        out_shape=[jax.ShapeDtypeStruct(shape, kind) for shape, kind in outs],
        in_specs=specs,
        out_specs=[pl.BlockSpec(memory_space=pltpu.VMEM)] * len(outs),
        scratch_shapes=list(scratch),
        compiler_params=pltpu.CompilerParams(vmem_limit_bytes=vmem * 2**20),
        cost_estimate=pl.CostEstimate(flops=cost[0], bytes_accessed=cost[1], transcendentals=cost[2]),
    )(*ins)


def doubled(rows, columns, feature, transposed):
    wide, thin = iota((rows, columns), 0), iota((rows, columns), 1)
    if not transposed:
        wide, thin = thin, wide
    source = (wide // (2 * feature)) * feature + wide % feature
    return ones_where(source == thin)


def prepare_body(
    w_value, s_query, s_key, s_value, s_out, s_inner, gate, gain_in, gain_mid, value_t, dup, dup_t, tall_t, columns, lines
):
    side = s_out.shape[0]
    feature = side // SHEADS
    hidden = s_inner.shape[1]
    value_t[...] = nt(eye(w_value.shape[0]), w_value[...]).astype(bf16)
    spread = doubled(side, dup.shape[1], feature, False)
    dup[0:side] = nn(s_key[...], spread).astype(bf16)
    dup[side : 2 * side] = nn(s_value[...], spread).astype(bf16)
    spread_t = doubled(2 * side, side, feature, True)
    for i, weight in enumerate((s_query, s_key, s_value)):
        dup_t[2 * side * i : 2 * side * (i + 1)] = nt(spread_t, weight[...]).astype(bf16)
    tall_t[0:side] = nt(eye(side), s_out[...]).astype(bf16)
    tall_t[side : side + hidden] = nt(eye(hidden), s_inner[...]).astype(bf16)
    lines[...] = jnp.zeros(lines.shape, f32)
    for i, line in enumerate((gate, gain_in, gain_mid)):
        lines[i : i + 1, 0:side] = line[...]
    columns[...] = lines[...].T[0:side]


def project(tokens, gain, w_query, w_key, value_t, scale, queries):
    normed = norm_lanes(tokens.astype(f32), gain).astype(bf16)
    query = (nn(normed[0:queries], w_query[...]) * scale).astype(bf16)
    return query, nn(normed, w_key[...]).astype(bf16), nt(value_t[...], normed).astype(bf16)


def first_body(own, mate, gains, w_query, w_key, value_t, query, key, value):
    span, width = own.shape
    scale = LOG2E * (width // HEADS) ** -0.5
    tokens = jnp.concatenate([own[...], mate[...]], axis=0)
    query[...], key[...], value[...] = project(
        tokens, gains[0:1], w_query, w_key, value_t, scale, span
    )


def bounds(doc_lengths, row):
    starts, ends, at = [], [], jnp.int32(0)
    for d in range(doc_lengths.shape[1]):
        starts.append(at)
        at = at + doc_lengths[row, d]
        ends.append(at)
    return starts, ends


def in_doc(doc_lengths, row, blocks, span, shape, token_dim):
    starts, ends = bounds(doc_lengths, row)
    parts = []
    part_shape = list(shape)
    part_shape[token_dim] = span
    number = iota(tuple(part_shape), 1 - token_dim)
    first = jnp.zeros(tuple(part_shape), i32)
    last = first
    for d, (start, end) in enumerate(zip(starts, ends)):
        first = jnp.where(number == d, start, first)
        last = jnp.where(number == d, end, last)
    for block in blocks:
        position = iota(tuple(part_shape), token_dim) + block * span
        parts.append(jnp.where((position >= first) & (position < last), 1.0, 0.0))
    return jnp.concatenate(parts, axis=token_dim)


def out_of_range(totals):
    lowest, highest = jnp.min(totals), jnp.max(totals)
    return jnp.logical_not((lowest > LOW_TOTAL) & (highest < HIGH_TOTAL))


def backbone_body(
    doc_lengths,
    own,
    far,
    far_mate,
    query_own,
    key_near,
    value_near,
    gains,
    w_query,
    w_key,
    value_t,
    down_w,
    columns,
    state,
    side_far,
    w_out_hbm,
    w_inner_hbm,
    w_outer_hbm,
    out_own,
    out_far,
    sn_rows,
    sn_t,
    mixed_t,
    lead_t,
    query,
    key,
    value,
    key_doc,
    query_doc,
    totals,
    attended,
    after,
    w_out,
    w_inner,
    w_outer,
    sems,
):
    copies = [
        pltpu.make_async_copy(source, target, sems.at[i])
        for i, (source, target) in enumerate(
            ((w_out_hbm, w_out), (w_inner_hbm, w_inner), (w_outer_hbm, w_outer))
        )
    ]
    for copy in copies:
        copy.start()
    span, width = own.shape
    head = width // HEADS
    stride = value.shape[0] // HEADS
    place = lax.axis_index("blk")
    half = lax.axis_size("blk") // 2
    row = place // half
    near, opposite = place ^ 1, place ^ half
    opposite_near = opposite ^ 1

    tokens = jnp.concatenate([far[...], far_mate[...]], axis=0)
    query_far, key_far, value_far = project(
        tokens, gains[0:1], w_query, w_key, value_t, LOG2E * head**-0.5, span
    )
    query[0:span] = query_own[...]
    query[span : 2 * span] = query_far
    key[0 : 2 * span] = key_near[...]
    key[2 * span : 4 * span] = key_far
    for h in range(HEADS):
        base = h * stride
        value[base : base + head, 0 : 2 * span] = value_near[h * head : (h + 1) * head]
        value[base : base + head, 2 * span : 4 * span] = value_far[h * head : (h + 1) * head]
        value[base + head : base + stride] = jnp.ones((stride - head, 4 * span), bf16)
    keys_in = in_doc(doc_lengths, row, (place, near, opposite, opposite_near), span, (4 * span, 128), 0)
    key_doc[...] = (keys_in - 1.0).astype(bf16)
    query_doc[...] = (
        in_doc(doc_lengths, row, (place, opposite), span, (2 * span, 128), 0) * FAR
    ).astype(bf16)

    def attend(shifted):
        def pair(j, carry):
            lanes = pl.ds(pl.multiple_of(j * 128, 128), 128)
            keys = jnp.concatenate([key[:, lanes], key_doc[...]], axis=1)
            results = []
            for side in range(128 // head):
                mine = ones_where(iota((1, 128), 1) // head == side)
                queries = jnp.concatenate([query[:, lanes] * mine, query_doc[...]], axis=1)
                scores = nt(keys, queries)
                if shifted:
                    scores = scores - jnp.max(scores, axis=0, keepdims=True)
                weights = jnp.exp2(scores).astype(bf16)
                at = (j * (128 // head) + side) * stride
                summed = nn(value[pl.ds(pl.multiple_of(at, 16), stride), :], weights)
                total = summed[head : head + 1]
                slot = pl.multiple_of((j * (128 // head) + side) * 8, 8)
                totals[pl.ds(slot, 8), :] = summed[head : head + 8]
                results.append(summed[0:head] * (1.0 / total))
            joined = jnp.concatenate(results, axis=0)
            attended[:, lanes] = joined.T.astype(bf16)
            return carry

        lax.fori_loop(0, width // 128, pair, 0)

    attend(False)

    @pl.when(out_of_range(totals[...]))
    def _():
        attend(True)

    copies[0].wait()
    after[0:span] = own[...].astype(f32) + nn(attended[0:span], w_out[...])
    after[span : 2 * span] = far[...].astype(f32) + nn(attended[span : 2 * span], w_out[...])
    middle = norm_lanes(after[...], gains[1:2]).astype(bf16)
    copies[1].wait()
    copies[2].wait()
    hidden = w_inner.shape[1]
    step = width
    result = after[...]
    for at in range(0, hidden, step):
        act = gelu(nn(middle, w_inner[:, at : at + step])).astype(bf16)
        result = result + nn(act, w_outer[at : at + step, :])
    out = result.astype(bf16)
    out_own[...] = out[0:span]
    out_far[...] = out[span : 2 * span]

    side = state.shape[1]
    down_t = nt(down_w[...], out)
    state_t = jnp.concatenate([state[row], side_far[0:side]], axis=1).astype(f32)
    gate_open = jax.nn.sigmoid(columns[:, 0:1])
    mixed = gate_open * down_t + (1.0 - gate_open) * state_t
    normed = (
        mixed * lax.rsqrt(jnp.mean(mixed * mixed, axis=0, keepdims=True) + EPS) * columns[:, 1:2]
    )
    mixed_t[...] = mixed
    lead_t[...] = down_t - state_t
    sn_t[...] = normed.astype(bf16)
    sn_rows[...] = normed.T.astype(bf16)


def side_body(
    doc_lengths,
    sn_own,
    sn_mate,
    mixed_t,
    cot,
    side_far,
    dup,
    dup_t,
    tall_t,
    s_outer_t,
    s_out,
    s_inner,
    columns,
    out_own,
    out_far,
    dquery,
    dkv_own,
    dkv_mate,
    dmid_t,
    early,
    weights,
    keys,
    values,
    key_t,
    value_t,
    query_t,
    query_s,
    query_h,
    attn_t,
    inverse,
    totals,
    dattn_s,
    dterm_s,
    dattn_h,
    dkv_t,
):
    tokens, side = sn_own.shape
    span = tokens // 2
    feature = side // SHEADS
    hidden = s_inner.shape[1]
    wide = 2 * side
    place = lax.axis_index("blk")
    half = lax.axis_size("blk") // 2
    row = place // half
    near, opposite = place ^ 1, place ^ half
    opposite_near = opposite ^ 1
    scale = feature**-0.5

    sn = jnp.concatenate([sn_own[...], sn_mate[...]], axis=0)
    lane = iota((2 * tokens, keys.shape[1]), 1)
    docs = in_doc(
        doc_lengths, row, (place, opposite, near, opposite_near), span, (2 * tokens, 128), 0
    )
    shift = wide % 128
    docs = pltpu.roll(docs, shift, 1)
    projected = nn(sn, dup[0:side]).astype(bf16)
    low_lane = iota((2 * tokens, 128), 1) < shift
    keys[:, 0:128] = projected[:, 0:128]
    keys[:, 128:256] = jnp.where(low_lane, projected[:, 128:256].astype(f32), docs - 1.0).astype(bf16)
    projected = nn(sn, dup[side : 2 * side]).astype(bf16)
    values[:, 0:128] = projected[:, 0:128]
    values[:, 128:256] = jnp.where(low_lane, projected[:, 128:256].astype(f32), 1.0).astype(bf16)
    key_t[...] = nt(dup_t[wide : 2 * wide], sn).astype(bf16)
    second = iota((wide, 2 * tokens), 0) % (2 * feature) >= feature
    value_t[...] = jnp.where(second, 1.0, nt(dup_t[2 * wide : 3 * wide], sn)).astype(bf16)
    query = nt(dup_t[0:wide], sn_own[...]).astype(bf16)
    query_t[...] = query
    scaled = query.astype(f32) * (scale * LOG2E)
    high = scaled.astype(bf16).astype(f32)
    second = iota((wide, tokens), 0) % (2 * feature) >= feature
    query_s[...] = jnp.where(second, scaled - high, high).astype(bf16)
    query_docs = in_doc(doc_lengths, row, (place, opposite), span, (16, tokens), 1) * FAR
    for i in range(2):
        query_h[i] = jnp.zeros(query_h.shape[1:], bf16)
        query_h[i, wide : wide + 16] = query_docs.astype(bf16)

    def attend(shifted):
        def pair(j, carry):
            for i in range(2):
                h = 2 * j + i
                rows = pl.ds(pl.multiple_of(h * 16, 16), 16)
                eight = pl.ds(pl.multiple_of(h * 8, 8), 8)
                query_h[i, rows, :] = query_s[rows, :]
                scores = nn(keys[...], query_h[i])
                query_h[i, rows, :] = jnp.zeros((16, tokens), bf16)
                if shifted:
                    scores = scores - jnp.max(scores, axis=0, keepdims=True)
                weight = jnp.exp2(scores).astype(bf16)
                weights[h] = weight
                summed = nn(value_t[rows, :], weight)
                total = summed[feature : 2 * feature]
                totals[eight, :] = total
                invert = 1.0 / total
                inverse[eight, :] = invert
                attn_t[eight, :] = summed[0:feature] * invert
            return carry

        lax.fori_loop(0, SHEADS // 2, pair, 0)

    attend(False)

    @pl.when(out_of_range(totals[...]))
    def _():
        attend(True)

    attn = attn_t[...]
    attn_low = attn.astype(bf16)
    mid = mixed_t[...] + nn(tall_t[0:side], attn_low)
    mid_scale = lax.rsqrt(jnp.mean(mid * mid, axis=0, keepdims=True) + EPS)
    gain = columns[:, 2:3]
    unit = mid * mid_scale
    normed = (unit * gain).astype(bf16)
    inner = nn(tall_t[side : side + hidden], normed)
    act = gelu(inner).astype(bf16)
    out = (mid + nn(s_outer_t[...], act)).astype(bf16)
    out_own[...] = out[:, 0:span]
    out_far[...] = out[:, span : 2 * span]

    dy_low = jnp.concatenate([cot[row], side_far[side : 2 * side]], axis=1)
    dy = dy_low.astype(f32)
    early[:, hidden : 2 * hidden] = nt(dy_low, act)
    dinner = (gelu_slope(inner) * tn(s_outer_t[...], dy_low)).astype(bf16)
    early[:, 0:hidden] = nt(normed, dinner)
    dnormed = nn(s_inner[...], dinner)
    grad_gain = jnp.sum(dnormed * unit, axis=1, keepdims=True)
    scaled = dnormed * gain
    dmid = dy + mid_scale * (scaled - unit * jnp.mean(scaled * unit, axis=0, keepdims=True))
    dmid_t[...] = dmid
    dmid_low = dmid.astype(bf16)
    last = jnp.concatenate(
        [nt(attn_low, dmid_low), jnp.zeros((side, 128 - side), f32)], axis=1
    )
    early[:, 2 * hidden : 2 * hidden + 128] = jnp.where(
        iota((side, 128), 1) == side, grad_gain, last
    )
    dattn = nn(s_out[...], dmid_low).astype(bf16).astype(f32)

    number = iota((feature, tokens), 0)
    for h in range(SHEADS):
        eight = slice(h * feature, (h + 1) * feature)
        invert = inverse[eight, :]
        part = dattn[eight] * invert
        high = part.astype(bf16).astype(f32)
        dattn_s[h * 16 : (h + 1) * 16] = jnp.concatenate([high, part - high], axis=0).astype(bf16)
        term = -jnp.sum(dattn[eight] * attn[eight], axis=0, keepdims=True) * invert
        first = term.astype(bf16).astype(f32)
        rest = term - first
        middle = rest.astype(bf16).astype(f32)
        piece = jnp.where(
            number == 0, first, jnp.where(number == 1, middle, jnp.where(number == 2, rest - middle, 0.0))
        )
        dterm_s[h * 16 : (h + 1) * 16] = jnp.concatenate(
            [piece, jnp.zeros_like(piece)], axis=0
        ).astype(bf16)
    for i in range(2):
        dattn_h[i] = jnp.zeros(dattn_h.shape[1:], bf16)

    def back(j, carry):
        for i in range(2):
            h = 2 * j + i
            rows = pl.ds(pl.multiple_of(h * 16, 16), 16)
            eight = pl.ds(pl.multiple_of(h * 8, 8), 8)
            eight_v = pl.ds(pl.multiple_of(side + h * 8, 8), 8)
            dattn_h[i, rows, :] = dattn_s[rows, :]
            dattn_h[i, wide : wide + 16] = dterm_s[rows, :]
            slope = nn(values[...], dattn_h[i])
            dattn_h[i, rows, :] = jnp.zeros((16, tokens), bf16)
            weight = weights[h]
            dscores = (weight.astype(f32) * slope).astype(bf16)
            dquery[eight, :] = nn(key_t[rows, :], dscores)[0:feature] * scale
            dkv_t[eight, :] = nt(query_t[rows, :], dscores)[0:feature] * scale
            both = nt(dattn_s[rows, :], weight)
            dkv_t[eight_v, :] = both[0:feature] + both[feature : 2 * feature]
        return carry

    lax.fori_loop(0, SHEADS // 2, back, 0)
    dkv_own[...] = dkv_t[:, 0:tokens]
    dkv_mate[...] = dkv_t[:, tokens : 2 * tokens].astype(bf16)


def last_body(
    dquery,
    dkv_own,
    dkv_back,
    sn_t,
    dmid_t,
    mixed_t,
    lead_t,
    out_own,
    out_far,
    s_query,
    s_key,
    s_value,
    columns,
    early,
    side_out_far,
    state_own,
    far,
    keep,
    send,
    pack,
):
    side, tokens = sn_t.shape
    span = tokens // 2
    width = out_own.shape[1]
    dq = dquery[...].astype(bf16)
    dkv = (dkv_own[...].astype(bf16).astype(f32) + dkv_back[...].astype(f32)).astype(bf16)
    dk, dv = dkv[0:side], dkv[side : 2 * side]
    sn = sn_t[...]
    dnormed = nn(s_query[...], dq) + nn(s_key[...], dk) + nn(s_value[...], dv)
    mixed = mixed_t[...]
    mixed_scale = lax.rsqrt(jnp.mean(mixed * mixed, axis=0, keepdims=True) + EPS)
    unit = mixed * mixed_scale
    scaled = dnormed * columns[:, 1:2]
    dmixed = dmid_t[...] + mixed_scale * (
        scaled - unit * jnp.mean(scaled * unit, axis=0, keepdims=True)
    )
    gate_open = jax.nn.sigmoid(columns[:, 0:1])
    grad_gain = jnp.sum(dnormed * unit, axis=1, keepdims=True)
    grad_gate = jnp.sum(dmixed * lead_t[...], axis=1, keepdims=True) * gate_open * (1.0 - gate_open)
    state = (1.0 - gate_open) * dmixed
    state_own[...] = state[:, 0:span]
    far[0:side] = side_out_far[...]
    far[side : 2 * side] = state[:, span:tokens].astype(bf16)
    ddown = (gate_open * dmixed).astype(bf16)
    pack[:, 0:width] = nn(ddown[:, 0:span], out_own[...]) + nn(ddown[:, span:tokens], out_far[...])
    at = width
    blank = jnp.zeros((side, 128 - side), f32)
    for grad in (dq, dk, dv):
        pack[:, at : at + 128] = jnp.concatenate([nt(sn, grad), blank], axis=1)
        at += 128
    lane = iota((side, 128), 1)
    inner = early.shape[1] - 128
    vectors = early[:, inner : inner + 128]
    vectors = jnp.where(lane == side + 1, grad_gain, vectors)
    pack[:, at : at + 128] = jnp.where(lane == side + 2, grad_gate, vectors)
    pack[:, at + 128 : at + 128 + inner] = early[:, 0:inner]
    size = keep.shape[1]
    core = lax.axis_index("blk") % 2
    keep[...] = pack[:, pl.ds(pl.multiple_of(core * size, 128), size)].astype(bf16)
    send[...] = pack[:, pl.ds(pl.multiple_of((1 - core) * size, 128), size)].astype(bf16)


def spread_body(
    part,
    part_x,
    part_core,
    part_both,
    grad_down,
    grad_gate,
    gain_in,
    grad_query,
    grad_key,
    grad_value,
    grad_out,
    gain_mid,
    grad_inner,
    grad_outer,
):
    side, width = grad_down.shape
    hidden = grad_inner.shape[1]
    place = lax.axis_index("blk")
    core, chip = place % 2, place // 2
    mine, cross, beside, both = (ref[...].astype(f32) for ref in (part, part_x, part_core, part_both))
    near = [jnp.where(chip == 0, mine, cross), jnp.where(chip == 0, cross, mine)]
    far = [jnp.where(chip == 0, beside, both), jnp.where(chip == 0, both, beside)]
    pieces = [jnp.where(core == 0, a, b) for a, b in zip(near + far, far + near)]
    whole = jnp.concatenate(pieces, axis=1)
    grad_down[...] = whole[:, 0:width]
    at = width
    for target in (grad_query, grad_key, grad_value):
        target[...] = whole[:, at : at + side]
        at += 128
    block = whole[:, at : at + 128]
    grad_out[...] = block[:, 0:side]
    rows = block.T
    gain_mid[...] = rows[side : side + 1]
    gain_in[...] = rows[side + 1 : side + 2]
    grad_gate[...] = rows[side + 2 : side + 3]
    at += 128
    grad_inner[...] = whole[:, at : at + hidden]
    grad_outer[...] = whole[:, at + hidden : at + 2 * hidden]


def per_device(
    hidden,
    side_state,
    doc_lengths,
    norm_in,
    w_query,
    w_key,
    w_value,
    w_out,
    norm_mid,
    w_inner,
    w_outer,
    w_down,
    gate,
    side_norm_in,
    s_query,
    s_key,
    s_value,
    s_out,
    side_norm_mid,
    s_inner,
    s_outer,
    cotangent,
):
    span, rows, width = hidden.shape
    side = side_state.shape[2]
    ff = w_inner.shape[1]
    sff = s_inner.shape[1]
    tokens = 2 * span
    blk_size, dp_size = lax.axis_size("blk"), lax.axis_size("dp")
    half = blk_size // 2
    place = lax.axis_index("blk")
    row = place // half

    def swap(value, axis, size, hop):
        return lax.ppermute(value, axis, [(i, i ^ hop) for i in range(size)])

    def across(value):
        return swap(value, "blk", blk_size, half)

    def beside(value):
        return swap(value, "blk", blk_size, 1)

    def of_row(array, which):
        return lax.dynamic_index_in_dim(array, which, 1, keepdims=False)

    leaving = of_row(hidden, 1 - row)
    hidden_far = across(leaving)
    hidden_own = of_row(lax.optimization_barrier((hidden, leaving))[0], row)
    hidden_mate = beside(hidden_own)
    state, cot = (jnp.transpose(array, (1, 2, 0)) for array in (side_state, cotangent))
    side_far = across(
        lax.dynamic_index_in_dim(jnp.concatenate([state, cot], axis=1), 1 - row, 0, keepdims=False)
    )
    gains = jnp.stack([norm_in, norm_mid]).astype(f32)
    lines = [line.reshape(1, side) for line in (gate, side_norm_in, side_norm_mid)]
    down_w, s_outer_t = w_down.T, s_outer.T

    value_t, dup, dup_t, tall_t, columns = kernel_call(
        prepare_body,
        [
            ((width, width), bf16),
            ((2 * side, 256), bf16),
            ((6 * side, side), bf16),
            ((side + sff, side), bf16),
            ((side, 128), f32),
        ],
        [w_value, s_query, s_key, s_value, s_out, s_inner, *lines],
        vmem=12,
        scratch=[pltpu.VMEM((128, 128), f32)],
        cost=(2 * width**3, 4 * width * width, 0),
    )
    query_own, key_near, value_near = kernel_call(
        first_body,
        [((span, width), bf16), ((tokens, width), bf16), ((width, tokens), bf16)],
        [hidden_own, hidden_mate, gains, w_query, w_key, value_t],
        vmem=20,
        cost=(5 * tokens * width * width, 8 * width * width, 0),
    )
    hidden_far, side_far, query_own, key_near, value_near = lax.optimization_barrier(
        (hidden_far, side_far, query_own, key_near, value_near)
    )
    far_mate = beside(hidden_far)
    stride = width // HEADS + 16
    out_own, out_far, sn_rows, sn_t, mixed_t, lead_t = kernel_call(
        backbone_body,
        [
            ((span, width), bf16),
            ((span, width), bf16),
            ((tokens, side), bf16),
            ((side, tokens), bf16),
            ((side, tokens), f32),
            ((side, tokens), f32),
        ],
        [
            doc_lengths,
            hidden_own,
            hidden_far,
            far_mate,
            query_own,
            key_near,
            value_near,
            gains,
            w_query,
            w_key,
            value_t,
            down_w,
            columns,
            state,
            side_far,
            w_out,
            w_inner,
            w_outer,
        ],
        vmem=44,
        scalars=(0,),
        whole=(15, 16, 17),
        scratch=[
            pltpu.VMEM((tokens, width), bf16),
            pltpu.VMEM((2 * tokens, width), bf16),
            pltpu.VMEM((HEADS * stride, 2 * tokens), bf16),
            pltpu.VMEM((2 * tokens, 128), bf16),
            pltpu.VMEM((tokens, 128), bf16),
            pltpu.VMEM((HEADS * 8, tokens), f32),
            pltpu.VMEM((tokens, width), bf16),
            pltpu.VMEM((tokens, width), f32),
            pltpu.VMEM((width, width), bf16),
            pltpu.VMEM((width, ff), bf16),
            pltpu.VMEM((ff, width), bf16),
            pltpu.SemaphoreType.DMA((3,)),
        ],
        cost=(20 * 10**9, 16 * 10**6, 0),
    )
    sn_mate = beside(sn_rows)
    out_back = across(out_far)
    side_own, side_back, dquery, dkv_own, dkv_mate, dmid_t, early = kernel_call(
        side_body,
        [
            ((side, span), bf16),
            ((side, span), bf16),
            ((side, tokens), f32),
            ((2 * side, tokens), f32),
            ((2 * side, tokens), bf16),
            ((side, tokens), f32),
            ((side, 2 * sff + 128), f32),
        ],
        [
            doc_lengths,
            sn_rows,
            sn_mate,
            mixed_t,
            cot,
            side_far,
            dup,
            dup_t,
            tall_t,
            s_outer_t,
            s_out,
            s_inner,
            columns,
        ],
        vmem=36,
        scalars=(0,),
        scratch=[
            pltpu.VMEM((SHEADS, 2 * tokens, tokens), bf16),
            pltpu.VMEM((2 * tokens, 256), bf16),
            pltpu.VMEM((2 * tokens, 256), bf16),
            pltpu.VMEM((2 * side, 2 * tokens), bf16),
            pltpu.VMEM((2 * side, 2 * tokens), bf16),
            pltpu.VMEM((2 * side, tokens), bf16),
            pltpu.VMEM((2 * side, tokens), bf16),
            pltpu.VMEM((2, 256, tokens), bf16),
            pltpu.VMEM((side, tokens), f32),
            pltpu.VMEM((side, tokens), f32),
            pltpu.VMEM((side, tokens), f32),
            pltpu.VMEM((2 * side, tokens), bf16),
            pltpu.VMEM((2 * side, tokens), bf16),
            pltpu.VMEM((2, 256, tokens), bf16),
            pltpu.VMEM((2 * side, 2 * tokens), f32),
        ],
        cost=(30 * 10**9, 3 * 10**6, 0),
    )
    dkv_back = beside(dkv_mate)
    dkv_back, out_back = lax.optimization_barrier((dkv_back, out_back))
    packed = width + 4 * 128 + 2 * sff
    grad_own, far, keep, send = kernel_call(
        last_body,
        [
            ((side, span), f32),
            ((2 * side, span), bf16),
            ((side, packed // 2), bf16),
            ((side, packed // 2), bf16),
        ],
        [
            dquery,
            dkv_own,
            dkv_back,
            sn_t,
            dmid_t,
            mixed_t,
            lead_t,
            out_own,
            out_far,
            s_query,
            s_key,
            s_value,
            columns,
            early,
            side_back,
        ],
        vmem=16,
        scratch=[pltpu.VMEM((side, packed), f32)],
        cost=(10**9, 3 * 10**6, 0),
    )

    def add(left, right):
        return (left.astype(f32) + right.astype(f32)).astype(bf16)

    quarter = packed // 4
    chip = (place // 2) % 2
    total = add(keep, beside(send))
    leaving = lax.dynamic_slice_in_dim(total, (1 - chip) * quarter, quarter, 1)
    total = lax.dynamic_slice_in_dim(total, chip * quarter, quarter, 1)
    total = add(total, swap(leaving, "blk", blk_size, 2))
    hop = 1
    while hop < dp_size:
        total = add(total, swap(total, "dp", dp_size, hop))
        hop *= 2
    total_x = swap(total, "blk", blk_size, 2)
    total_core = beside(total)
    total_both = beside(total_x)
    vector = ((1, side), f32)
    square = ((side, side), f32)
    grads = kernel_call(
        spread_body,
        [
            ((side, width), f32),
            vector,
            vector,
            square,
            square,
            square,
            square,
            vector,
            ((side, sff), f32),
            ((side, sff), f32),
        ],
        [total, total_x, total_core, total_both],
        vmem=16,
        cost=(0, 2 * 10**6, 0),
    )
    grads = [grad.reshape(side) if grad.shape[0] == 1 else grad for grad in grads]
    grads[0], grads[-1] = grads[0].T, grads[-1].T

    def both_rows(own, back, axis):
        first = jnp.where(row == 0, own, back)
        second = jnp.where(row == 0, back, own)
        return jnp.stack([first, second], axis=axis)

    far = across(far)
    return (
        both_rows(out_own, out_back, 1),
        jnp.transpose(both_rows(side_own, far[0:side], 0), (2, 0, 1)),
        jnp.transpose(both_rows(grad_own, far[side : 2 * side].astype(f32), 0), (2, 0, 1)),
        *grads,
    )


def solution(mesh):
    split = P("blk", "dp", None)
    return jax.shard_map(
        per_device,
        mesh=mesh,
        in_specs=(split, split, P("dp", None)) + (P(),) * 18 + (split,),
        out_specs=(split,) * 3 + (P(),) * 10,
        check_vma=False,
    )
```

```python
import math

import jax
import jax.numpy as jnp
from jax import lax
from jax.experimental import pallas as pl
from jax.experimental.pallas import tpu as pltpu
from jax.sharding import PartitionSpec as P

HEADS = 12
SHEADS = 12
GROUP = 4
SPARE = 64
EPS = 1e-06
LOG2E = math.log2(math.e)
FAR = 2.0**100
LOW_TOTAL, HIGH_TOTAL = 2.0**-80, 2.0**100

f32, bf16, i32 = jnp.float32, jnp.bfloat16, jnp.int32


def nn(left, right):
    return jnp.dot(left, right, preferred_element_type=f32)


def nt(left, right):
    return lax.dot_general(left, right, (((1,), (1,)), ((), ())), preferred_element_type=f32)


def tn(left, right):
    return lax.dot_general(left, right, (((0,), (0,)), ((), ())), preferred_element_type=f32)


def ones_where(condition):
    return jnp.where(condition, 1.0, 0.0).astype(bf16)


def iota(shape, dim):
    return lax.broadcasted_iota(i32, shape, dim)


def eye(size):
    return ones_where(iota((size, size), 0) == iota((size, size), 1))


def norm_lanes(value, gain):
    return value * lax.rsqrt(jnp.mean(value * value, axis=1, keepdims=True) + EPS) * gain


def gelu(value):
    return 0.5 * value * (1.0 + lax.erf(value * math.sqrt(0.5)))


def gelu_slope(value):
    bell = jnp.exp2(value * value * (-0.5 * LOG2E)) * (1.0 / math.sqrt(2.0 * math.pi))
    return 0.5 * (1.0 + lax.erf(value * math.sqrt(0.5))) + value * bell


def kernel_call(body, outs, ins, *, vmem, scratch=(), whole=(), scalars=(), cost=(0, 0, 0)):
    specs = [
        pl.BlockSpec(
            memory_space=pl.ANY if i in whole else pltpu.SMEM if i in scalars else pltpu.VMEM
        )
        for i in range(len(ins))
    ]
    return pl.pallas_call(
        body,
        out_shape=[jax.ShapeDtypeStruct(shape, kind) for shape, kind in outs],
        in_specs=specs,
        out_specs=[pl.BlockSpec(memory_space=pltpu.VMEM)] * len(outs),
        scratch_shapes=list(scratch),
        compiler_params=pltpu.CompilerParams(vmem_limit_bytes=vmem * 2**20),
        cost_estimate=pl.CostEstimate(flops=cost[0], bytes_accessed=cost[1], transcendentals=cost[2]),
    )(*ins)


def doubled(rows, columns, feature, transposed):
    wide, thin = iota((rows, columns), 0), iota((rows, columns), 1)
    if not transposed:
        wide, thin = thin, wide
    source = (wide // (2 * feature)) * feature + wide % feature
    return ones_where(source == thin)


def bounds(doc_lengths, row):
    starts, ends, at = [], [], jnp.int32(0)
    for d in range(doc_lengths.shape[1]):
        starts.append(at)
        at = at + doc_lengths[row, d]
        ends.append(at)
    return starts, ends


def in_doc(doc_lengths, row, runs, length, shape, token_dim):
    starts, ends = bounds(doc_lengths, row)
    parts = []
    part_shape = list(shape)
    part_shape[token_dim] = length
    number = iota(tuple(part_shape), 1 - token_dim)
    first = jnp.zeros(tuple(part_shape), i32)
    last = first
    for d, (start, end) in enumerate(zip(starts, ends)):
        first = jnp.where(number == d, start, first)
        last = jnp.where(number == d, end, last)
    for run in runs:
        position = iota(tuple(part_shape), token_dim) + run
        parts.append(jnp.where((position >= first) & (position < last), 1.0, 0.0))
    return jnp.concatenate(parts, axis=token_dim)


def side_weights_body(
    s_query, s_key, s_value, s_out, s_inner, gate, gain_in, gain_mid, dup, dup_t, tall_t, columns, lines
):
    side, hidden = s_inner.shape
    feature = side // SHEADS
    spread = doubled(side, dup.shape[1], feature, False)
    dup[0:side] = nn(s_key[...], spread).astype(bf16)
    dup[side : 2 * side] = nn(s_value[...], spread).astype(bf16)
    spread_t = doubled(2 * side, side, feature, True)
    for i, weight in enumerate((s_query, s_key, s_value)):
        dup_t[2 * side * i : 2 * side * (i + 1)] = nt(spread_t, weight[...]).astype(bf16)
    tall_t[0:side] = nt(eye(side), s_out[...]).astype(bf16)
    tall_t[side : side + hidden] = nt(eye(hidden), s_inner[...]).astype(bf16)
    lines[...] = jnp.zeros(lines.shape, f32)
    for i, line in enumerate((gate, gain_in, gain_mid)):
        lines[i : i + 1, 0:side] = line[...].reshape(1, side)
    columns[...] = lines[...].T[0:side]


def prepare_body(
    doc_lengths, w_value, norm_in, norm_mid, value_t, gains, key_doc, query_doc, side_key_doc, side_query_doc
):
    value_t[...] = nt(eye(w_value.shape[0]), w_value[...]).astype(bf16)
    for i, line in enumerate((norm_in, norm_mid)):
        gains[i : i + 1] = line[...].astype(f32).reshape(1, line.shape[0])
    keys, tokens = key_doc.shape[0], query_doc.shape[0]
    span = tokens // 2
    place, half = lax.axis_index("blk"), lax.axis_size("blk") // 2
    row = place // half
    own, mate = place * span, (place ^ 1) * span
    far, far_mate = (place ^ half) * span, (place ^ half ^ 1) * span
    found = in_doc(doc_lengths, row, (own, mate, far, far_mate), span, (keys, 128), 0)
    key_doc[...] = (found - 1.0).astype(bf16)
    mine = jnp.concatenate([found[0:span], found[tokens : tokens + span]], axis=0)
    query_doc[...] = (mine * FAR).astype(bf16)
    mates = jnp.concatenate([found[span:tokens], found[tokens + span : keys]], axis=0)
    spare = SPARE
    low = iota((keys, 128), 1) < spare
    ordered = pltpu.roll(jnp.concatenate([mine, mates], axis=0), spare, 1)
    side_key_doc[...] = jnp.where(low, 0.0, ordered - 1.0).astype(bf16)
    side_query_doc[...] = (in_doc(doc_lengths, row, (own, far), span, (16, tokens), 1) * FAR).astype(bf16)


def project(tokens, gain, w_query, w_key, value_t, scale, queries):
    normed = norm_lanes(tokens.astype(f32), gain).astype(bf16)
    query = (nn(normed[0:queries], w_query[...]) * scale).astype(bf16)
    return query, nn(normed, w_key[...]).astype(bf16), nt(value_t[...], normed).astype(bf16)


def padded(value_t, head):
    ones = jnp.ones((16, value_t.shape[1]), bf16)
    pieces = []
    for at in range(0, value_t.shape[0], head):
        pieces += [value_t[at : at + head], ones]
    return jnp.concatenate(pieces, axis=0)


def pair_lanes(j):
    return pl.ds(pl.multiple_of(j * 128, 128), 128)


def pair_sums(j, queries, query_doc, keys, key_doc, values, shifted=False):
    width = queries[0].shape[1]
    head = width // HEADS
    stride = values[0].shape[0] // HEADS
    lanes = pair_lanes(j)
    key = jnp.concatenate([ref[:, lanes] for ref in keys], axis=0)
    key = jnp.concatenate([key, key_doc], axis=1)
    query = jnp.concatenate([ref[:, lanes] for ref in queries], axis=0)
    rows = pl.ds(pl.multiple_of(j * 2 * stride, 16), 2 * stride)
    value = jnp.concatenate([ref[rows, :] for ref in values], axis=1)
    lane = iota((1, 128), 1) // head
    masked = [jnp.concatenate([query * ones_where(lane == i), query_doc], axis=1) for i in range(2)]
    count = query.shape[0]

    scores = nt(key, jnp.concatenate(masked, axis=0))
    if shifted:
        scores = scores - jnp.max(scores, axis=0, keepdims=True)
    both = nn(value, jnp.exp2(scores).astype(bf16))
    return [both[i * stride : i * stride + head + 8, i * count : (i + 1) * count] for i in range(2)]


def first_body(own, mate, gains, w_query, w_key, value_t, key_doc, query_doc, query, key, value, part):
    _, span, width = own.shape
    head = width // HEADS
    row = lax.axis_index("blk") // (lax.axis_size("blk") // 2)
    tokens = jnp.concatenate([own[row], mate[row]], axis=0)
    query[...], key[...], value_new = project(
        tokens, gains[0:1], w_query, w_key, value_t, LOG2E * head**-0.5, span
    )
    value[...] = padded(value_new, head)

    def pair(j, carry):
        sums = pair_sums(j, [query], query_doc[0:span], [key], key_doc[0 : 2 * span], [value])
        part[j] = jnp.concatenate(sums, axis=0)
        return carry

    lax.fori_loop(0, HEADS // 2, pair, 0, unroll=3)


def out_of_range(totals):
    lowest, highest = jnp.min(totals), jnp.max(totals)
    return jnp.logical_not((lowest > LOW_TOTAL) & (highest < HIGH_TOTAL))


def second_body(
    far,
    far_mate,
    gains,
    w_query,
    w_key,
    value_t,
    key_doc,
    query_doc,
    query_a,
    key_a,
    value_a,
    part_a,
    attended,
    query,
    key,
    value,
    totals,
):
    span, width = far.shape
    head = width // HEADS
    tokens = jnp.concatenate([far[...], far_mate[...]], axis=0)
    query[...], key[...], value_new = project(
        tokens, gains[0:1], w_query, w_key, value_t, LOG2E * head**-0.5, span
    )
    value[...] = padded(value_new, head)
    keys, values, queries = [key_a, key], [value_a, value], [query_a, query]

    def finish(j, sums):
        results = []
        for i, summed in enumerate(sums):
            totals[pl.ds(pl.multiple_of((2 * j + i) * 8, 8), 8), :] = summed[head : head + 8]
            results.append(summed[0:head] * (1.0 / summed[head : head + 1]))
        attended[:, pair_lanes(j)] = jnp.concatenate(results, axis=0).T.astype(bf16)

    def pair(j, carry):
        old = pair_sums(j, [query_a], query_doc[0:span], [key], key_doc[2 * span : 4 * span], [value])
        new = pair_sums(j, [query], query_doc[span : 2 * span], keys, key_doc[...], values)
        sums = []
        for i in range(2):
            rows = slice(i * (head + 8), (i + 1) * (head + 8))
            sums.append(jnp.concatenate([old[i] + part_a[j, rows], new[i]], axis=1))
        finish(j, sums)
        return carry

    lax.fori_loop(0, HEADS // 2, pair, 0, unroll=3)

    @pl.when(out_of_range(totals[...]))
    def _():
        def again(j, carry):
            finish(j, pair_sums(j, queries, query_doc[...], keys, key_doc[...], values, shifted=True))
            return carry

        lax.fori_loop(0, HEADS // 2, again, 0)


def dense_body(
    own, far, attended, gains, w_out, w_inner, w_outer, down_w, columns, state, side_far, out_own, out_far, sn_rows, sn_t, mixed_t, lead_t
):
    _, span, width = own.shape
    row = lax.axis_index("blk") // (lax.axis_size("blk") // 2)
    tokens = jnp.concatenate([own[row], far[...]], axis=0)
    after = tokens.astype(f32) + nn(attended[...], w_out[...])
    middle = norm_lanes(after, gains[1:2]).astype(bf16)
    result = after
    for at in range(0, w_inner.shape[1], width):
        act = gelu(nn(middle, w_inner[:, at : at + width])).astype(bf16)
        result = result + nn(act, w_outer[at : at + width, :])
    out = result.astype(bf16)
    out_own[...] = out[0:span]
    out_far[...] = out[span : 2 * span]

    side = state.shape[1]
    down_t = nt(down_w[...], out)
    state_t = jnp.concatenate([state[row], side_far[0:side]], axis=1).astype(f32)
    gate_open = jax.nn.sigmoid(columns[:, 0:1])
    mixed = gate_open * down_t + (1.0 - gate_open) * state_t
    normed = (
        mixed * lax.rsqrt(jnp.mean(mixed * mixed, axis=0, keepdims=True) + EPS) * columns[:, 1:2]
    )
    mixed_t[...] = mixed
    lead_t[...] = down_t - state_t
    sn_t[...] = normed.astype(bf16)
    sn_rows[...] = normed.T.astype(bf16)


def side_body(
    sn_own,
    sn_mate,
    mixed_t,
    cot,
    side_far,
    dup,
    dup_t,
    tall_t,
    s_outer_t,
    s_out,
    s_inner,
    columns,
    key_doc,
    query_doc,
    out_own,
    out_far,
    dquery,
    dkv_own,
    dkv_mate,
    dmid_t,
    early,
    weights,
    keys,
    values,
    key_t,
    value_t,
    query_t,
    query_s,
    query_h,
    attn_t,
    inverse,
    totals,
    dattn_s,
    dterm_s,
    dattn_h,
    dkv_t,
):
    tokens, side = sn_own.shape
    span = tokens // 2
    feature = side // SHEADS
    hidden = s_inner.shape[1]
    wide = 2 * side
    place = lax.axis_index("blk")
    half = lax.axis_size("blk") // 2
    row = place // half
    scale = feature**-0.5

    sn = jnp.concatenate([sn_own[...], sn_mate[...]], axis=0)
    projected = nn(sn, dup[0:side]).astype(bf16)
    keys[:, 0:128] = projected[:, 0:128]
    keys[:, 128:256] = projected[:, 128:256] + key_doc[...]
    low_lane = iota((2 * tokens, 128), 1) < SPARE
    projected = nn(sn, dup[side : 2 * side]).astype(bf16)
    values[:, 0:128] = projected[:, 0:128]
    values[:, 128:256] = jnp.where(low_lane, projected[:, 128:256].astype(f32), 1.0).astype(bf16)
    key_t[...] = nt(dup_t[wide : 2 * wide], sn).astype(bf16)
    second = iota((wide, 2 * tokens), 0) % (2 * feature) >= feature
    value_t[...] = jnp.where(second, 1.0, nt(dup_t[2 * wide : 3 * wide], sn)).astype(bf16)
    query = nt(dup_t[0:wide], sn_own[...]).astype(bf16)
    query_t[...] = query
    scaled = query.astype(f32) * (scale * LOG2E)
    high = scaled.astype(bf16).astype(f32)
    second = iota((wide, tokens), 0) % (2 * feature) >= feature
    query_s[...] = jnp.where(second, scaled - high, high).astype(bf16)
    for i in range(GROUP):
        query_h[i] = jnp.zeros(query_h.shape[1:], bf16)
        query_h[i, wide : wide + 16] = query_doc[...]

    def attend(shifted):
        def pair(j, carry):
            for i in range(GROUP):
                h = GROUP * j + i
                rows = pl.ds(pl.multiple_of(h * 16, 16), 16)
                eight = pl.ds(pl.multiple_of(h * 8, 8), 8)
                query_h[i, rows, :] = query_s[rows, :]
                scores = nn(keys[...], query_h[i])
                query_h[i, rows, :] = jnp.zeros((16, tokens), bf16)
                if shifted:
                    scores = scores - jnp.max(scores, axis=0, keepdims=True)
                weight = jnp.exp2(scores).astype(bf16)
                weights[h] = weight
                summed = nn(value_t[rows, :], weight)
                total = summed[feature : 2 * feature]
                totals[eight, :] = total
                invert = 1.0 / total
                inverse[eight, :] = invert
                attn_t[eight, :] = summed[0:feature] * invert
            return carry

        lax.fori_loop(0, SHEADS // GROUP, pair, 0)

    attend(False)

    @pl.when(out_of_range(totals[...]))
    def _():
        attend(True)

    attn = attn_t[...]
    attn_low = attn.astype(bf16)
    mid = mixed_t[...] + nn(tall_t[0:side], attn_low)
    mid_scale = lax.rsqrt(jnp.mean(mid * mid, axis=0, keepdims=True) + EPS)
    gain = columns[:, 2:3]
    unit = mid * mid_scale
    normed = (unit * gain).astype(bf16)
    inner = nn(tall_t[side : side + hidden], normed)
    act = gelu(inner).astype(bf16)
    out = (mid + nn(s_outer_t[...], act)).astype(bf16)
    out_own[...] = out[:, 0:span]
    out_far[...] = out[:, span : 2 * span]

    dy_low = jnp.concatenate([cot[row], side_far[side : 2 * side]], axis=1)
    dy = dy_low.astype(f32)
    early[:, hidden : 2 * hidden] = nt(dy_low, act)
    dinner = (gelu_slope(inner) * tn(s_outer_t[...], dy_low)).astype(bf16)
    early[:, 0:hidden] = nt(normed, dinner)
    dnormed = nn(s_inner[...], dinner)
    grad_gain = jnp.sum(dnormed * unit, axis=1, keepdims=True)
    scaled = dnormed * gain
    dmid = dy + mid_scale * (scaled - unit * jnp.mean(scaled * unit, axis=0, keepdims=True))
    dmid_t[...] = dmid
    dmid_low = dmid.astype(bf16)
    last = jnp.concatenate(
        [nt(attn_low, dmid_low), jnp.zeros((side, 128 - side), f32)], axis=1
    )
    early[:, 2 * hidden : 2 * hidden + 128] = jnp.where(
        iota((side, 128), 1) == side, grad_gain, last
    )
    dattn = nn(s_out[...], dmid_low).astype(bf16).astype(f32)

    number = iota((feature, tokens), 0)
    for h in range(SHEADS):
        eight = slice(h * feature, (h + 1) * feature)
        invert = inverse[eight, :]
        part = dattn[eight] * invert
        high = part.astype(bf16).astype(f32)
        dattn_s[h * 16 : (h + 1) * 16] = jnp.concatenate([high, part - high], axis=0).astype(bf16)
        term = -jnp.sum(dattn[eight] * attn[eight], axis=0, keepdims=True) * invert
        first = term.astype(bf16).astype(f32)
        rest = term - first
        middle = rest.astype(bf16).astype(f32)
        piece = jnp.where(
            number == 0, first, jnp.where(number == 1, middle, jnp.where(number == 2, rest - middle, 0.0))
        )
        dterm_s[h * 16 : (h + 1) * 16] = jnp.concatenate(
            [piece, jnp.zeros_like(piece)], axis=0
        ).astype(bf16)
    for i in range(GROUP):
        dattn_h[i] = jnp.zeros(dattn_h.shape[1:], bf16)

    def back(j, carry):
        for i in range(GROUP):
            h = GROUP * j + i
            rows = pl.ds(pl.multiple_of(h * 16, 16), 16)
            eight = pl.ds(pl.multiple_of(h * 8, 8), 8)
            eight_v = pl.ds(pl.multiple_of(side + h * 8, 8), 8)
            dattn_h[i, rows, :] = dattn_s[rows, :]
            dattn_h[i, wide : wide + 16] = dterm_s[rows, :]
            slope = nn(values[...], dattn_h[i])
            dattn_h[i, rows, :] = jnp.zeros((16, tokens), bf16)
            weight = weights[h]
            dscores = (weight.astype(f32) * slope).astype(bf16)
            dquery[eight, :] = nn(key_t[rows, :], dscores)[0:feature] * scale
            dkv_t[eight, :] = nt(query_t[rows, :], dscores)[0:feature] * scale
            both = nt(dattn_s[rows, :], weight)
            dkv_t[eight_v, :] = both[0:feature] + both[feature : 2 * feature]
        return carry

    lax.fori_loop(0, SHEADS // GROUP, back, 0)
    dkv_own[...] = dkv_t[:, 0:tokens]
    dkv_mate[...] = dkv_t[:, tokens : 2 * tokens].astype(bf16)


def last_body(
    dquery,
    dkv_own,
    dkv_back,
    sn_t,
    dmid_t,
    mixed_t,
    lead_t,
    out_own,
    out_far,
    s_query,
    s_key,
    s_value,
    columns,
    early,
    side_out_far,
    state_own,
    far,
    keep,
    send,
    pack,
):
    side, tokens = sn_t.shape
    span = tokens // 2
    width = out_own.shape[1]
    dq = dquery[...].astype(bf16)
    dkv = (dkv_own[...].astype(bf16).astype(f32) + dkv_back[...].astype(f32)).astype(bf16)
    dk, dv = dkv[0:side], dkv[side : 2 * side]
    sn = sn_t[...]
    dnormed = nn(s_query[...], dq) + nn(s_key[...], dk) + nn(s_value[...], dv)
    mixed = mixed_t[...]
    mixed_scale = lax.rsqrt(jnp.mean(mixed * mixed, axis=0, keepdims=True) + EPS)
    unit = mixed * mixed_scale
    scaled = dnormed * columns[:, 1:2]
    dmixed = dmid_t[...] + mixed_scale * (
        scaled - unit * jnp.mean(scaled * unit, axis=0, keepdims=True)
    )
    gate_open = jax.nn.sigmoid(columns[:, 0:1])
    grad_gain = jnp.sum(dnormed * unit, axis=1, keepdims=True)
    grad_gate = jnp.sum(dmixed * lead_t[...], axis=1, keepdims=True) * gate_open * (1.0 - gate_open)
    state = (1.0 - gate_open) * dmixed
    state_own[...] = state[:, 0:span]
    far[0:side] = side_out_far[...]
    far[side : 2 * side] = state[:, span:tokens].astype(bf16)
    ddown = (gate_open * dmixed).astype(bf16)
    pack[:, 0:width] = nn(ddown[:, 0:span], out_own[...]) + nn(ddown[:, span:tokens], out_far[...])
    at = width
    blank = jnp.zeros((side, 128 - side), f32)
    for grad in (dq, dk, dv):
        pack[:, at : at + 128] = jnp.concatenate([nt(sn, grad), blank], axis=1)
        at += 128
    lane = iota((side, 128), 1)
    inner = early.shape[1] - 128
    vectors = early[:, inner : inner + 128]
    vectors = jnp.where(lane == side + 1, grad_gain, vectors)
    pack[:, at : at + 128] = jnp.where(lane == side + 2, grad_gate, vectors)
    pack[:, at + 128 : at + 128 + inner] = early[:, 0:inner]
    size = keep.shape[1]
    core = lax.axis_index("blk") % 2
    keep[...] = pack[:, pl.ds(pl.multiple_of(core * size, 128), size)].astype(bf16)
    send[...] = pack[:, pl.ds(pl.multiple_of((1 - core) * size, 128), size)].astype(bf16)


def spread_body(
    part,
    part_x,
    part_core,
    part_both,
    grad_down,
    grad_gate,
    gain_in,
    grad_query,
    grad_key,
    grad_value,
    grad_out,
    gain_mid,
    grad_inner,
    grad_outer,
):
    side, width = grad_down.shape
    hidden = grad_inner.shape[1]
    place = lax.axis_index("blk")
    core, chip = place % 2, place // 2
    mine, cross, beside, both = (ref[...].astype(f32) for ref in (part, part_x, part_core, part_both))
    near = [jnp.where(chip == 0, mine, cross), jnp.where(chip == 0, cross, mine)]
    far = [jnp.where(chip == 0, beside, both), jnp.where(chip == 0, both, beside)]
    pieces = [jnp.where(core == 0, a, b) for a, b in zip(near + far, far + near)]
    whole = jnp.concatenate(pieces, axis=1)
    grad_down[...] = whole[:, 0:width]
    at = width
    for target in (grad_query, grad_key, grad_value):
        target[...] = whole[:, at : at + side]
        at += 128
    block = whole[:, at : at + 128]
    grad_out[...] = block[:, 0:side]
    rows = block.T
    gain_mid[...] = rows[side : side + 1]
    gain_in[...] = rows[side + 1 : side + 2]
    grad_gate[...] = rows[side + 2 : side + 3]
    at += 128
    grad_inner[...] = whole[:, at : at + hidden]
    grad_outer[...] = whole[:, at + hidden : at + 2 * hidden]


def per_device(
    hidden,
    side_state,
    doc_lengths,
    norm_in,
    w_query,
    w_key,
    w_value,
    w_out,
    norm_mid,
    w_inner,
    w_outer,
    w_down,
    gate,
    side_norm_in,
    s_query,
    s_key,
    s_value,
    s_out,
    side_norm_mid,
    s_inner,
    s_outer,
    cotangent,
):
    span, rows, width = hidden.shape
    side = side_state.shape[2]
    ff = w_inner.shape[1]
    sff = s_inner.shape[1]
    tokens = 2 * span
    blk_size, dp_size = lax.axis_size("blk"), lax.axis_size("dp")
    half = blk_size // 2
    place = lax.axis_index("blk")
    row = place // half

    def swap(value, axis, size, hop):
        return lax.ppermute(value, axis, [(i, i ^ hop) for i in range(size)])

    def across(value):
        return swap(value, "blk", blk_size, half)

    def beside(value):
        return swap(value, "blk", blk_size, 1)

    hidden = jnp.transpose(hidden, (1, 0, 2))
    hidden_far = across(lax.dynamic_index_in_dim(hidden, 1 - row, 0, keepdims=False))
    hidden_mate = beside(hidden)
    state, cot = (jnp.transpose(array, (1, 2, 0)) for array in (side_state, cotangent))
    side_far = across(
        lax.dynamic_index_in_dim(jnp.concatenate([state, cot], axis=1), 1 - row, 0, keepdims=False)
    )
    down_w, s_outer_t = w_down.T, s_outer.T

    value_t, gains, key_doc, query_doc, side_key_doc, side_query_doc = kernel_call(
        prepare_body,
        [
            ((width, width), bf16),
            ((2, width), f32),
            ((2 * tokens, 128), bf16),
            ((tokens, 128), bf16),
            ((2 * tokens, 128), bf16),
            ((16, tokens), bf16),
        ],
        [doc_lengths, w_value, norm_in, norm_mid],
        vmem=16,
        scalars=(0,),
        cost=(1000, 1000, 0),
    )
    head = width // HEADS
    stride = head + 16
    projections = (gains, w_query, w_key, value_t, key_doc, query_doc)

    def state_of(queries, keys, columns):
        return [
            ((queries, width), bf16),
            ((keys, width), bf16),
            ((HEADS * stride, keys), bf16),
            ((HEADS // 2, 2 * (head + 8), columns), f32),
        ]

    state_a = kernel_call(
        first_body,
        state_of(span, tokens, span),
        [hidden, hidden_mate, *projections],
        vmem=24,
        cost=(1000, 1000, 0),
    )
    small = (s_query, s_key, s_value, s_out, s_inner, gate, side_norm_in, side_norm_mid)
    hidden_far, small, *state_a = lax.optimization_barrier((hidden_far, small, *state_a))
    dup, dup_t, tall_t, columns = kernel_call(
        side_weights_body,
        [
            ((2 * side, 256), bf16),
            ((6 * side, side), bf16),
            ((side + sff, side), bf16),
            ((side, 128), f32),
        ],
        small,
        vmem=8,
        scratch=[pltpu.VMEM((128, 128), f32)],
        cost=(1000, 1000, 0),
    )
    (attended,) = kernel_call(
        second_body,
        [((tokens, width), bf16)],
        [hidden_far, beside(hidden_far), *projections, *state_a],
        vmem=30,
        scratch=[
            pltpu.VMEM((span, width), bf16),
            pltpu.VMEM((tokens, width), bf16),
            pltpu.VMEM((HEADS * stride, tokens), bf16),
            pltpu.VMEM((HEADS * 8, tokens), f32),
        ],
        cost=(8 * 10**9, 8 * 10**6, 0),
    )
    side_far, attended = lax.optimization_barrier((side_far, attended))
    out_own, out_far, sn_rows, sn_t, mixed_t, lead_t = kernel_call(
        dense_body,
        [
            ((span, width), bf16),
            ((span, width), bf16),
            ((tokens, side), bf16),
            ((side, tokens), bf16),
            ((side, tokens), f32),
            ((side, tokens), f32),
        ],
        [
            hidden,
            hidden_far,
            attended,
            gains,
            w_out,
            w_inner,
            w_outer,
            down_w,
            columns,
            state,
            side_far,
        ],
        vmem=28,
        cost=(10 * 10**9, 14 * 10**6, 0),
    )
    sn_mate = beside(sn_rows)
    out_back = across(out_far)
    side_own, side_back, dquery, dkv_own, dkv_mate, dmid_t, early = kernel_call(
        side_body,
        [
            ((side, span), bf16),
            ((side, span), bf16),
            ((side, tokens), f32),
            ((2 * side, tokens), f32),
            ((2 * side, tokens), bf16),
            ((side, tokens), f32),
            ((side, 2 * sff + 128), f32),
        ],
        [
            sn_rows,
            sn_mate,
            mixed_t,
            cot,
            side_far,
            dup,
            dup_t,
            tall_t,
            s_outer_t,
            s_out,
            s_inner,
            columns,
            side_key_doc,
            side_query_doc,
        ],
        vmem=36,
        scratch=[
            pltpu.VMEM((SHEADS, 2 * tokens, tokens), bf16),
            pltpu.VMEM((2 * tokens, 256), bf16),
            pltpu.VMEM((2 * tokens, 256), bf16),
            pltpu.VMEM((2 * side, 2 * tokens), bf16),
            pltpu.VMEM((2 * side, 2 * tokens), bf16),
            pltpu.VMEM((2 * side, tokens), bf16),
            pltpu.VMEM((2 * side, tokens), bf16),
            pltpu.VMEM((GROUP, 256, tokens), bf16),
            pltpu.VMEM((side, tokens), f32),
            pltpu.VMEM((side, tokens), f32),
            pltpu.VMEM((side, tokens), f32),
            pltpu.VMEM((2 * side, tokens), bf16),
            pltpu.VMEM((2 * side, tokens), bf16),
            pltpu.VMEM((GROUP, 256, tokens), bf16),
            pltpu.VMEM((2 * side, 2 * tokens), f32),
        ],
        cost=(30 * 10**9, 3 * 10**6, 0),
    )
    dkv_back = beside(dkv_mate)
    dkv_back, out_back = lax.optimization_barrier((dkv_back, out_back))
    packed = width + 4 * 128 + 2 * sff
    grad_own, far, keep, send = kernel_call(
        last_body,
        [
            ((side, span), f32),
            ((2 * side, span), bf16),
            ((side, packed // 2), bf16),
            ((side, packed // 2), bf16),
        ],
        [
            dquery,
            dkv_own,
            dkv_back,
            sn_t,
            dmid_t,
            mixed_t,
            lead_t,
            out_own,
            out_far,
            s_query,
            s_key,
            s_value,
            columns,
            early,
            side_back,
        ],
        vmem=16,
        scratch=[pltpu.VMEM((side, packed), f32)],
        cost=(10**9, 3 * 10**6, 0),
    )

    def add(left, right):
        return (left.astype(f32) + right.astype(f32)).astype(bf16)

    quarter = packed // 4
    chip = (place // 2) % 2
    total = add(keep, beside(send))
    leaving = lax.dynamic_slice_in_dim(total, (1 - chip) * quarter, quarter, 1)
    total = lax.dynamic_slice_in_dim(total, chip * quarter, quarter, 1)
    total = add(total, swap(leaving, "blk", blk_size, 2))
    total, far = lax.optimization_barrier((total, far))
    hop = 1
    while hop < dp_size:
        total = add(total, swap(total, "dp", dp_size, hop))
        hop *= 2
    total_x = swap(total, "blk", blk_size, 2)
    total_core = beside(total)
    total_both = beside(total_x)
    vector = ((1, side), f32)
    square = ((side, side), f32)
    grads = kernel_call(
        spread_body,
        [
            ((side, width), f32),
            vector,
            vector,
            square,
            square,
            square,
            square,
            vector,
            ((side, sff), f32),
            ((side, sff), f32),
        ],
        [total, total_x, total_core, total_both],
        vmem=16,
        cost=(0, 2 * 10**6, 0),
    )
    grads = [grad.reshape(side) if grad.shape[0] == 1 else grad for grad in grads]
    grads[0], grads[-1] = grads[0].T, grads[-1].T

    def both_rows(own, back):
        first = jnp.where(row == 0, own, back)
        second = jnp.where(row == 0, back, own)
        return jnp.stack([first, second])

    far = across(far)
    return (
        jnp.transpose(both_rows(out_own, out_back), (1, 0, 2)),
        jnp.transpose(both_rows(side_own, far[0:side]), (2, 0, 1)),
        jnp.transpose(both_rows(grad_own, far[side : 2 * side].astype(f32)), (2, 0, 1)),
        *grads,
    )


def solution(mesh):
    split = P("blk", "dp", None)
    return jax.shard_map(
        per_device,
        mesh=mesh,
        in_specs=(split, split, P("dp", None)) + (P(),) * 18 + (split,),
        out_specs=(split,) * 3 + (P(),) * 10,
        check_vma=False,
    )
```

```python
import math

import jax
import jax.numpy as jnp
from jax import lax
from jax.experimental import pallas as pl
from jax.experimental.pallas import tpu as pltpu
from jax.sharding import PartitionSpec as P

HEADS = 12
SHEADS = 12
GROUP = 6
SPARE = 64
EPS = 1e-06
LOG2E = math.log2(math.e)
FAR = 2.0**100
LOW_TOTAL, HIGH_TOTAL = 2.0**-80, 2.0**100

f32, bf16, i32 = jnp.float32, jnp.bfloat16, jnp.int32


def nn(left, right):
    return jnp.dot(left, right, preferred_element_type=f32)


def nt(left, right):
    return lax.dot_general(left, right, (((1,), (1,)), ((), ())), preferred_element_type=f32)


def tn(left, right):
    return lax.dot_general(left, right, (((0,), (0,)), ((), ())), preferred_element_type=f32)


def ones_where(condition):
    return jnp.where(condition, 1.0, 0.0).astype(bf16)


def iota(shape, dim):
    return lax.broadcasted_iota(i32, shape, dim)


def eye(size):
    return ones_where(iota((size, size), 0) == iota((size, size), 1))


def norm_lanes(value, gain):
    return value * lax.rsqrt(jnp.mean(value * value, axis=1, keepdims=True) + EPS) * gain


def gelu(value):
    return 0.5 * value * (1.0 + lax.erf(value * math.sqrt(0.5)))


def gelu_slope(value):
    bell = jnp.exp2(value * value * (-0.5 * LOG2E)) * (1.0 / math.sqrt(2.0 * math.pi))
    return 0.5 * (1.0 + lax.erf(value * math.sqrt(0.5))) + value * bell


def kernel_call(body, outs, ins, *, vmem, scratch=(), whole=(), scalars=(), cost=(0, 0, 0)):
    specs = [
        pl.BlockSpec(
            memory_space=pl.ANY if i in whole else pltpu.SMEM if i in scalars else pltpu.VMEM
        )
        for i in range(len(ins))
    ]
    return pl.pallas_call(
        body,
        out_shape=[jax.ShapeDtypeStruct(shape, kind) for shape, kind in outs],
        in_specs=specs,
        out_specs=[pl.BlockSpec(memory_space=pltpu.VMEM)] * len(outs),
        scratch_shapes=list(scratch),
        compiler_params=pltpu.CompilerParams(vmem_limit_bytes=vmem * 2**20),
        cost_estimate=pl.CostEstimate(flops=cost[0], bytes_accessed=cost[1], transcendentals=cost[2]),
    )(*ins)


def doubled(rows, columns, feature, transposed):
    wide, thin = iota((rows, columns), 0), iota((rows, columns), 1)
    if not transposed:
        wide, thin = thin, wide
    source = (wide // (2 * feature)) * feature + wide % feature
    return ones_where(source == thin)


def bounds(doc_lengths, row):
    starts, ends, at = [], [], jnp.int32(0)
    for d in range(doc_lengths.shape[1]):
        starts.append(at)
        at = at + doc_lengths[row, d]
        ends.append(at)
    return starts, ends


def in_doc(doc_lengths, row, runs, length, shape, token_dim):
    starts, ends = bounds(doc_lengths, row)
    parts = []
    part_shape = list(shape)
    part_shape[token_dim] = length
    number = iota(tuple(part_shape), 1 - token_dim)
    first = jnp.zeros(tuple(part_shape), i32)
    last = first
    for d, (start, end) in enumerate(zip(starts, ends)):
        first = jnp.where(number == d, start, first)
        last = jnp.where(number == d, end, last)
    for run in runs:
        position = iota(tuple(part_shape), token_dim) + run
        parts.append(jnp.where((position >= first) & (position < last), 1.0, 0.0))
    return jnp.concatenate(parts, axis=token_dim)


def side_weights_body(
    s_query, s_key, s_value, s_out, s_inner, gate, gain_in, gain_mid, dup, dup_t, tall_t, columns, lines
):
    side, hidden = s_inner.shape
    feature = side // SHEADS
    spread = doubled(side, dup.shape[1], feature, False)
    dup[...] = nn(s_key[...], spread).astype(bf16)
    spread_t = doubled(2 * side, side, feature, True)
    for i, weight in enumerate((s_query, s_key, s_value)):
        dup_t[2 * side * i : 2 * side * (i + 1)] = nt(spread_t, weight[...]).astype(bf16)
    tall_t[0:side] = nt(eye(side), s_out[...]).astype(bf16)
    tall_t[side : side + hidden] = nt(eye(hidden), s_inner[...]).astype(bf16)
    lines[...] = jnp.zeros(lines.shape, f32)
    for i, line in enumerate((gate, gain_in, gain_mid)):
        lines[i : i + 1, 0:side] = line[...].reshape(1, side)
    columns[...] = lines[...].T[0:side]


def prepare_body(
    doc_lengths, w_value, norm_in, norm_mid, value_t, gains, key_doc, query_doc, side_key_doc, side_query_doc
):
    value_t[...] = nt(eye(w_value.shape[0]), w_value[...]).astype(bf16)
    for i, line in enumerate((norm_in, norm_mid)):
        gains[i : i + 1] = line[...].astype(f32).reshape(1, line.shape[0])
    keys, tokens = key_doc.shape[0], query_doc.shape[0]
    span = tokens // 2
    place, half = lax.axis_index("blk"), lax.axis_size("blk") // 2
    row = place // half
    own, mate = place * span, (place ^ 1) * span
    far, far_mate = (place ^ half) * span, (place ^ half ^ 1) * span
    found = in_doc(doc_lengths, row, (own, mate, far, far_mate), span, (keys, 128), 0)
    key_doc[...] = (found - 1.0).astype(bf16)
    mine = jnp.concatenate([found[0:span], found[tokens : tokens + span]], axis=0)
    query_doc[...] = (mine * FAR).astype(bf16)
    mates = jnp.concatenate([found[span:tokens], found[tokens + span : keys]], axis=0)
    spare = SPARE
    low = iota((keys, 128), 1) < spare
    ordered = pltpu.roll(jnp.concatenate([mine, mates], axis=0), spare, 1)
    side_key_doc[...] = jnp.where(low, 0.0, ordered - 1.0).astype(bf16)
    side_query_doc[...] = (in_doc(doc_lengths, row, (own, far), span, (16, tokens), 1) * FAR).astype(bf16)


def project(tokens, gain, w_query, w_key, value_t, scale, queries):
    normed = norm_lanes(tokens.astype(f32), gain).astype(bf16)
    query = (nn(normed[0:queries], w_query[...]) * scale).astype(bf16)
    return query, nn(normed, w_key[...]).astype(bf16), nt(value_t[...], normed).astype(bf16)


def padded(value_t, head):
    ones = jnp.ones((16, value_t.shape[1]), bf16)
    pieces = []
    for at in range(0, value_t.shape[0], head):
        pieces += [value_t[at : at + head], ones]
    return jnp.concatenate(pieces, axis=0)


def pair_lanes(j):
    return pl.ds(pl.multiple_of(j * 128, 128), 128)


def pair_sums(j, queries, query_doc, keys, key_doc, values, shifted=False):
    width = queries[0].shape[1]
    head = width // HEADS
    stride = values[0].shape[0] // HEADS
    lanes = pair_lanes(j)
    key = jnp.concatenate([ref[:, lanes] for ref in keys], axis=0)
    key = jnp.concatenate([key, key_doc], axis=1)
    query = jnp.concatenate([ref[:, lanes] for ref in queries], axis=0)
    rows = pl.ds(pl.multiple_of(j * 2 * stride, 16), 2 * stride)
    value = jnp.concatenate([ref[rows, :] for ref in values], axis=1)
    lane = iota((1, 128), 1) // head
    masked = [jnp.concatenate([query * ones_where(lane == i), query_doc], axis=1) for i in range(2)]
    count = query.shape[0]

    scores = nt(key, jnp.concatenate(masked, axis=0))
    if shifted:
        scores = scores - jnp.max(scores, axis=0, keepdims=True)
    both = nn(value, jnp.exp2(scores).astype(bf16))
    return [both[i * stride : i * stride + head + 8, i * count : (i + 1) * count] for i in range(2)]


def first_body(own, mate, gains, w_query, w_key, value_t, key_doc, query_doc, query, key, value, part):
    _, span, width = own.shape
    head = width // HEADS
    row = lax.axis_index("blk") // (lax.axis_size("blk") // 2)
    tokens = jnp.concatenate([own[row], mate[row]], axis=0)
    query[...], key[...], value_new = project(
        tokens, gains[0:1], w_query, w_key, value_t, LOG2E * head**-0.5, span
    )
    value[...] = padded(value_new, head)

    def pair(j, carry):
        sums = pair_sums(j, [query], query_doc[0:span], [key], key_doc[0 : 2 * span], [value])
        part[j] = jnp.concatenate(sums, axis=0)
        return carry

    lax.fori_loop(0, HEADS // 2, pair, 0, unroll=6)


def out_of_range(totals):
    lowest, highest = jnp.min(totals), jnp.max(totals)
    return jnp.logical_not((lowest > LOW_TOTAL) & (highest < HIGH_TOTAL))


def second_body(
    far,
    far_mate,
    gains,
    w_query,
    w_key,
    value_t,
    key_doc,
    query_doc,
    query_a,
    key_a,
    value_a,
    part_a,
    attended,
    query,
    key,
    value,
    totals,
):
    span, width = far.shape
    head = width // HEADS
    tokens = jnp.concatenate([far[...], far_mate[...]], axis=0)
    query[...], key[...], value_new = project(
        tokens, gains[0:1], w_query, w_key, value_t, LOG2E * head**-0.5, span
    )
    value[...] = padded(value_new, head)
    keys, values, queries = [key_a, key], [value_a, value], [query_a, query]

    def finish(j, sums):
        results = []
        for i, summed in enumerate(sums):
            totals[pl.ds(pl.multiple_of((2 * j + i) * 8, 8), 8), :] = summed[head : head + 8]
            results.append(summed[0:head] * (1.0 / summed[head : head + 1]))
        attended[:, pair_lanes(j)] = jnp.concatenate(results, axis=0).T.astype(bf16)

    def pair(j, carry):
        old = pair_sums(j, [query_a], query_doc[0:span], [key], key_doc[2 * span : 4 * span], [value])
        new = pair_sums(j, [query], query_doc[span : 2 * span], keys, key_doc[...], values)
        sums = []
        for i in range(2):
            rows = slice(i * (head + 8), (i + 1) * (head + 8))
            sums.append(jnp.concatenate([old[i] + part_a[j, rows], new[i]], axis=1))
        finish(j, sums)
        return carry

    lax.fori_loop(0, HEADS // 2, pair, 0, unroll=6)

    @pl.when(out_of_range(totals[...]))
    def _():
        def again(j, carry):
            finish(j, pair_sums(j, queries, query_doc[...], keys, key_doc[...], values, shifted=True))
            return carry

        lax.fori_loop(0, HEADS // 2, again, 0)


def dense_body(
    own, far, attended, gains, w_out, w_inner, w_outer, down_w, columns, state, side_far, out_own, out_far, sn_rows, sn_t, mixed_t, lead_t
):
    _, span, width = own.shape
    row = lax.axis_index("blk") // (lax.axis_size("blk") // 2)
    tokens = jnp.concatenate([own[row], far[...]], axis=0)
    after = tokens.astype(f32) + nn(attended[...], w_out[...])
    middle = norm_lanes(after, gains[1:2]).astype(bf16)
    result = after
    for at in range(0, w_inner.shape[1], width):
        act = gelu(nn(middle, w_inner[:, at : at + width])).astype(bf16)
        result = result + nn(act, w_outer[at : at + width, :])
    out = result.astype(bf16)
    out_own[...] = out[0:span]
    out_far[...] = out[span : 2 * span]

    side = state.shape[1]
    down_t = nt(down_w[...], out)
    state_t = jnp.concatenate([state[row], side_far[0:side]], axis=1).astype(f32)
    gate_open = jax.nn.sigmoid(columns[:, 0:1])
    mixed = gate_open * down_t + (1.0 - gate_open) * state_t
    normed = (
        mixed * lax.rsqrt(jnp.mean(mixed * mixed, axis=0, keepdims=True) + EPS) * columns[:, 1:2]
    )
    mixed_t[...] = mixed
    lead_t[...] = down_t - state_t
    sn_t[...] = normed.astype(bf16)
    sn_rows[...] = normed.T.astype(bf16)


def outer_rows(left, right):
    return jnp.concatenate([left[f : f + 1] * right for f in range(left.shape[0])], axis=0)


def inner_rows(left, products):
    count = left.shape[0]
    total = left[0:1] * products[0:count]
    for f in range(1, count):
        total = total + left[f : f + 1] * products[f * count : (f + 1) * count]
    return total


def two_parts(value):
    high = value.astype(bf16).astype(f32)
    return [high, value - high]


def side_body(
    sn_own,
    sn_mate,
    mixed_t,
    cot,
    side_far,
    dup,
    dup_t,
    tall_t,
    s_outer_t,
    s_out,
    s_inner,
    columns,
    key_doc,
    query_doc,
    out_own,
    out_far,
    dquery,
    dkv_own,
    dkv_mate,
    dmid_t,
    early,
    weights,
    keys,
    key_t,
    value_t,
    query_t,
    query_s,
    query_h,
    attn_t,
    inverse,
    totals,
    moments,
    back_rows,
    dkv_t,
):
    tokens, side = sn_own.shape
    span = tokens // 2
    feature = side // SHEADS
    hidden = s_inner.shape[1]
    wide = 2 * side
    row = lax.axis_index("blk") // (lax.axis_size("blk") // 2)
    scale = feature**-0.5

    sn = jnp.concatenate([sn_own[...], sn_mate[...]], axis=0)
    projected = nn(sn, dup[...]).astype(bf16)
    keys[:, 0:128] = projected[:, 0:128]
    keys[:, 128:256] = projected[:, 128:256] + key_doc[...]
    key_t[...] = nt(dup_t[wide : 2 * wide], sn).astype(bf16)
    second = iota((wide, 2 * tokens), 0) % (2 * feature) >= feature
    value_t[...] = jnp.where(second, 1.0, nt(dup_t[2 * wide : 3 * wide], sn)).astype(bf16)
    query = nt(dup_t[0:wide], sn_own[...]).astype(bf16)
    query_t[...] = query
    scaled = query.astype(f32) * (scale * LOG2E)
    high = scaled.astype(bf16).astype(f32)
    second = iota((wide, tokens), 0) % (2 * feature) >= feature
    query_s[...] = jnp.where(second, scaled - high, high).astype(bf16)
    for i in range(GROUP):
        query_h[i] = jnp.zeros(query_h.shape[1:], bf16)
        query_h[i, wide : wide + 16] = query_doc[...]

    def head_rows(h, count):
        return pl.ds(pl.multiple_of(h * count, count), count)

    def attend(shifted):
        def group(j, carry):
            for i in range(GROUP):
                h = GROUP * j + i
                rows, eight = head_rows(h, 16), head_rows(h, 8)
                query_h[i, rows, :] = query_s[rows, :]
                scores = nn(keys[...], query_h[i])
                query_h[i, rows, :] = jnp.zeros((16, tokens), bf16)
                if shifted:
                    scores = scores - jnp.max(scores, axis=0, keepdims=True)
                weight = jnp.exp2(scores).astype(bf16)
                weights[h] = weight
                value, key = value_t[rows, :], key_t[rows, :]
                products = outer_rows(value[0:feature].astype(f32), key[0:feature].astype(f32))
                products = jnp.concatenate(two_parts(products), axis=0).astype(bf16)
                summed = nn(jnp.concatenate([value, key, products], axis=0), weight)
                total = summed[feature : 2 * feature]
                totals[eight, :] = total
                invert = 1.0 / total
                inverse[eight, :] = invert
                attn_t[eight, :] = summed[0:feature] * invert
                at = 4 * feature + feature * feature
                moments[h] = jnp.concatenate(
                    [summed[2 * feature : 4 * feature], summed[4 * feature : at] + summed[at:]], axis=0
                )
            return carry

        lax.fori_loop(0, SHEADS // GROUP, group, 0)

    attend(False)

    @pl.when(out_of_range(totals[...]))
    def _():
        attend(True)

    attn = attn_t[...]
    attn_low = attn.astype(bf16)
    mid = mixed_t[...] + nn(tall_t[0:side], attn_low)
    mid_scale = lax.rsqrt(jnp.mean(mid * mid, axis=0, keepdims=True) + EPS)
    gain = columns[:, 2:3]
    unit = mid * mid_scale
    normed = (unit * gain).astype(bf16)
    inner = nn(tall_t[side : side + hidden], normed)
    act = gelu(inner).astype(bf16)
    out = (mid + nn(s_outer_t[...], act)).astype(bf16)
    out_own[...] = out[:, 0:span]
    out_far[...] = out[:, span : 2 * span]

    dy_low = jnp.concatenate([cot[row], side_far[side : 2 * side]], axis=1)
    dy = dy_low.astype(f32)
    early[:, hidden : 2 * hidden] = nt(dy_low, act)
    dinner = (gelu_slope(inner) * tn(s_outer_t[...], dy_low)).astype(bf16)
    early[:, 0:hidden] = nt(normed, dinner)
    dnormed = nn(s_inner[...], dinner)
    grad_gain = jnp.sum(dnormed * unit, axis=1, keepdims=True)
    scaled = dnormed * gain
    dmid = dy + mid_scale * (scaled - unit * jnp.mean(scaled * unit, axis=0, keepdims=True))
    dmid_t[...] = dmid
    dmid_low = dmid.astype(bf16)
    last = jnp.concatenate([nt(attn_low, dmid_low), jnp.zeros((side, 128 - side), f32)], axis=1)
    early[:, 2 * hidden : 2 * hidden + 128] = jnp.where(
        iota((side, 128), 1) == side, grad_gain, last
    )
    dattn = nn(s_out[...], dmid_low).astype(bf16).astype(f32)

    for h in range(SHEADS):
        eight = slice(h * feature, (h + 1) * feature)
        invert = inverse[eight, :]
        term = jnp.sum(dattn[eight] * attn[eight], axis=0, keepdims=True)
        moment = moments[h]
        raw = inner_rows(dattn[eight], moment[2 * feature :]) - term * moment[0:feature]
        dquery[eight, :] = raw * invert * scale
        query = query_t[2 * h * feature : (2 * h + 1) * feature].astype(f32)
        share = dattn[eight] * invert
        back_rows[h] = jnp.concatenate(
            two_parts(share) + two_parts(term * invert * query) + two_parts(outer_rows(share, query)), axis=0
        ).astype(bf16)

    def back(j, carry):
        for i in range(GROUP):
            h = GROUP * j + i
            summed = nt(back_rows[h], weights[h])
            dkv_t[pl.ds(pl.multiple_of(side + h * feature, feature), feature), :] = (
                summed[0:feature] + summed[feature : 2 * feature]
            )
            value = value_t[head_rows(h, 16), :][0:feature].astype(f32)
            at = 4 * feature + feature * feature
            raw = inner_rows(value, summed[4 * feature : at] + summed[at:])
            raw = raw - (summed[2 * feature : 3 * feature] + summed[3 * feature : 4 * feature])
            dkv_t[head_rows(h, feature), :] = raw * scale
        return carry

    lax.fori_loop(0, SHEADS // GROUP, back, 0)
    dkv_own[...] = dkv_t[:, 0:tokens]
    dkv_mate[...] = dkv_t[:, tokens : 2 * tokens].astype(bf16)


def last_body(
    dquery,
    dkv_own,
    dkv_back,
    sn_t,
    dmid_t,
    mixed_t,
    lead_t,
    out_own,
    out_far,
    s_query,
    s_key,
    s_value,
    columns,
    early,
    side_out_far,
    state_own,
    far,
    keep,
    send,
    pack,
):
    side, tokens = sn_t.shape
    span = tokens // 2
    width = out_own.shape[1]
    dq = dquery[...].astype(bf16)
    dkv = (dkv_own[...].astype(bf16).astype(f32) + dkv_back[...].astype(f32)).astype(bf16)
    dk, dv = dkv[0:side], dkv[side : 2 * side]
    sn = sn_t[...]
    dnormed = nn(s_query[...], dq) + nn(s_key[...], dk) + nn(s_value[...], dv)
    mixed = mixed_t[...]
    mixed_scale = lax.rsqrt(jnp.mean(mixed * mixed, axis=0, keepdims=True) + EPS)
    unit = mixed * mixed_scale
    scaled = dnormed * columns[:, 1:2]
    dmixed = dmid_t[...] + mixed_scale * (
        scaled - unit * jnp.mean(scaled * unit, axis=0, keepdims=True)
    )
    gate_open = jax.nn.sigmoid(columns[:, 0:1])
    grad_gain = jnp.sum(dnormed * unit, axis=1, keepdims=True)
    grad_gate = jnp.sum(dmixed * lead_t[...], axis=1, keepdims=True) * gate_open * (1.0 - gate_open)
    state = (1.0 - gate_open) * dmixed
    state_own[...] = state[:, 0:span]
    far[0:side] = side_out_far[...]
    far[side : 2 * side] = state[:, span:tokens].astype(bf16)
    ddown = (gate_open * dmixed).astype(bf16)
    pack[:, 0:width] = nn(ddown[:, 0:span], out_own[...]) + nn(ddown[:, span:tokens], out_far[...])
    at = width
    blank = jnp.zeros((side, 128 - side), f32)
    for grad in (dq, dk, dv):
        pack[:, at : at + 128] = jnp.concatenate([nt(sn, grad), blank], axis=1)
        at += 128
    lane = iota((side, 128), 1)
    inner = early.shape[1] - 128
    vectors = early[:, inner : inner + 128]
    vectors = jnp.where(lane == side + 1, grad_gain, vectors)
    pack[:, at : at + 128] = jnp.where(lane == side + 2, grad_gate, vectors)
    pack[:, at + 128 : at + 128 + inner] = early[:, 0:inner]
    size = keep.shape[1]
    core = lax.axis_index("blk") % 2
    keep[...] = pack[:, pl.ds(pl.multiple_of(core * size, 128), size)].astype(bf16)
    send[...] = pack[:, pl.ds(pl.multiple_of((1 - core) * size, 128), size)].astype(bf16)


def spread_body(
    part,
    part_x,
    part_core,
    part_both,
    grad_down,
    grad_gate,
    gain_in,
    grad_query,
    grad_key,
    grad_value,
    grad_out,
    gain_mid,
    grad_inner,
    grad_outer,
):
    side, width = grad_down.shape
    hidden = grad_inner.shape[1]
    place = lax.axis_index("blk")
    core, chip = place % 2, place // 2
    mine, cross, beside, both = (ref[...].astype(f32) for ref in (part, part_x, part_core, part_both))
    near = [jnp.where(chip == 0, mine, cross), jnp.where(chip == 0, cross, mine)]
    far = [jnp.where(chip == 0, beside, both), jnp.where(chip == 0, both, beside)]
    pieces = [jnp.where(core == 0, a, b) for a, b in zip(near + far, far + near)]
    whole = jnp.concatenate(pieces, axis=1)
    grad_down[...] = whole[:, 0:width]
    at = width
    for target in (grad_query, grad_key, grad_value):
        target[...] = whole[:, at : at + side]
        at += 128
    block = whole[:, at : at + 128]
    grad_out[...] = block[:, 0:side]
    rows = block.T
    gain_mid[...] = rows[side : side + 1]
    gain_in[...] = rows[side + 1 : side + 2]
    grad_gate[...] = rows[side + 2 : side + 3]
    at += 128
    grad_inner[...] = whole[:, at : at + hidden]
    grad_outer[...] = whole[:, at + hidden : at + 2 * hidden]


def per_device(
    hidden,
    side_state,
    doc_lengths,
    norm_in,
    w_query,
    w_key,
    w_value,
    w_out,
    norm_mid,
    w_inner,
    w_outer,
    w_down,
    gate,
    side_norm_in,
    s_query,
    s_key,
    s_value,
    s_out,
    side_norm_mid,
    s_inner,
    s_outer,
    cotangent,
):
    span, rows, width = hidden.shape
    side = side_state.shape[2]
    ff = w_inner.shape[1]
    sff = s_inner.shape[1]
    tokens = 2 * span
    feature = side // SHEADS
    blk_size, dp_size = lax.axis_size("blk"), lax.axis_size("dp")
    half = blk_size // 2
    place = lax.axis_index("blk")
    row = place // half

    def swap(value, axis, size, hop):
        return lax.ppermute(value, axis, [(i, i ^ hop) for i in range(size)])

    def across(value):
        return swap(value, "blk", blk_size, half)

    def beside(value):
        return swap(value, "blk", blk_size, 1)

    hidden = jnp.transpose(hidden, (1, 0, 2))
    hidden_far = across(lax.dynamic_index_in_dim(hidden, 1 - row, 0, keepdims=False))
    hidden_mate = beside(hidden)
    state, cot = (jnp.transpose(array, (1, 2, 0)) for array in (side_state, cotangent))
    side_far = across(
        lax.dynamic_index_in_dim(jnp.concatenate([state, cot], axis=1), 1 - row, 0, keepdims=False)
    )
    down_w, s_outer_t = w_down.T, s_outer.T

    value_t, gains, key_doc, query_doc, side_key_doc, side_query_doc = kernel_call(
        prepare_body,
        [
            ((width, width), bf16),
            ((2, width), f32),
            ((2 * tokens, 128), bf16),
            ((tokens, 128), bf16),
            ((2 * tokens, 128), bf16),
            ((16, tokens), bf16),
        ],
        [doc_lengths, w_value, norm_in, norm_mid],
        vmem=16,
        scalars=(0,),
        cost=(1000, 1000, 0),
    )
    head = width // HEADS
    stride = head + 16
    projections = (gains, w_query, w_key, value_t, key_doc, query_doc)

    def state_of(queries, keys, columns):
        return [
            ((queries, width), bf16),
            ((keys, width), bf16),
            ((HEADS * stride, keys), bf16),
            ((HEADS // 2, 2 * (head + 8), columns), f32),
        ]

    state_a = kernel_call(
        first_body,
        state_of(span, tokens, span),
        [hidden, hidden_mate, *projections],
        vmem=24,
        cost=(1000, 1000, 0),
    )
    small = (s_query, s_key, s_value, s_out, s_inner, gate, side_norm_in, side_norm_mid)
    hidden_far, small, *state_a = lax.optimization_barrier((hidden_far, small, *state_a))
    dup, dup_t, tall_t, columns = kernel_call(
        side_weights_body,
        [
            ((side, 256), bf16),
            ((6 * side, side), bf16),
            ((side + sff, side), bf16),
            ((side, 128), f32),
        ],
        small,
        vmem=8,
        scratch=[pltpu.VMEM((128, 128), f32)],
        cost=(1000, 1000, 0),
    )
    (attended,) = kernel_call(
        second_body,
        [((tokens, width), bf16)],
        [hidden_far, beside(hidden_far), *projections, *state_a],
        vmem=30,
        scratch=[
            pltpu.VMEM((span, width), bf16),
            pltpu.VMEM((tokens, width), bf16),
            pltpu.VMEM((HEADS * stride, tokens), bf16),
            pltpu.VMEM((HEADS * 8, tokens), f32),
        ],
        cost=(8 * 10**9, 8 * 10**6, 0),
    )
    side_far, attended = lax.optimization_barrier((side_far, attended))
    out_own, out_far, sn_rows, sn_t, mixed_t, lead_t = kernel_call(
        dense_body,
        [
            ((span, width), bf16),
            ((span, width), bf16),
            ((tokens, side), bf16),
            ((side, tokens), bf16),
            ((side, tokens), f32),
            ((side, tokens), f32),
        ],
        [
            hidden,
            hidden_far,
            attended,
            gains,
            w_out,
            w_inner,
            w_outer,
            down_w,
            columns,
            state,
            side_far,
        ],
        vmem=28,
        cost=(10 * 10**9, 14 * 10**6, 0),
    )
    sn_mate = beside(sn_rows)
    out_back = across(out_far)
    side_own, side_back, dquery, dkv_own, dkv_mate, dmid_t, early = kernel_call(
        side_body,
        [
            ((side, span), bf16),
            ((side, span), bf16),
            ((side, tokens), f32),
            ((2 * side, tokens), f32),
            ((2 * side, tokens), bf16),
            ((side, tokens), f32),
            ((side, 2 * sff + 128), f32),
        ],
        [
            sn_rows,
            sn_mate,
            mixed_t,
            cot,
            side_far,
            dup,
            dup_t,
            tall_t,
            s_outer_t,
            s_out,
            s_inner,
            columns,
            side_key_doc,
            side_query_doc,
        ],
        vmem=36,
        scratch=[
            pltpu.VMEM((SHEADS, 2 * tokens, tokens), bf16),
            pltpu.VMEM((2 * tokens, 256), bf16),
            pltpu.VMEM((2 * side, 2 * tokens), bf16),
            pltpu.VMEM((2 * side, 2 * tokens), bf16),
            pltpu.VMEM((2 * side, tokens), bf16),
            pltpu.VMEM((2 * side, tokens), bf16),
            pltpu.VMEM((GROUP, 256, tokens), bf16),
            pltpu.VMEM((side, tokens), f32),
            pltpu.VMEM((side, tokens), f32),
            pltpu.VMEM((side, tokens), f32),
            pltpu.VMEM((SHEADS, feature * (feature + 2), tokens), f32),
            pltpu.VMEM((SHEADS, feature * (2 * feature + 4), tokens), bf16),
            pltpu.VMEM((2 * side, 2 * tokens), f32),
        ],
        cost=(30 * 10**9, 3 * 10**6, 0),
    )
    dkv_back = beside(dkv_mate)
    dkv_back, out_back = lax.optimization_barrier((dkv_back, out_back))
    packed = width + 4 * 128 + 2 * sff
    grad_own, far, keep, send = kernel_call(
        last_body,
        [
            ((side, span), f32),
            ((2 * side, span), bf16),
            ((side, packed // 2), bf16),
            ((side, packed // 2), bf16),
        ],
        [
            dquery,
            dkv_own,
            dkv_back,
            sn_t,
            dmid_t,
            mixed_t,
            lead_t,
            out_own,
            out_far,
            s_query,
            s_key,
            s_value,
            columns,
            early,
            side_back,
        ],
        vmem=16,
        scratch=[pltpu.VMEM((side, packed), f32)],
        cost=(10**9, 3 * 10**6, 0),
    )

    def add(left, right):
        return (left.astype(f32) + right.astype(f32)).astype(bf16)

    quarter = packed // 4
    chip = (place // 2) % 2
    total = add(keep, beside(send))
    leaving = lax.dynamic_slice_in_dim(total, (1 - chip) * quarter, quarter, 1)
    total = lax.dynamic_slice_in_dim(total, chip * quarter, quarter, 1)
    total = add(total, swap(leaving, "blk", blk_size, 2))
    total, far = lax.optimization_barrier((total, far))
    hop = 1
    while hop < dp_size:
        total = add(total, swap(total, "dp", dp_size, hop))
        hop *= 2
    total_x = swap(total, "blk", blk_size, 2)
    total_core = beside(total)
    total_both = beside(total_x)
    vector = ((1, side), f32)
    square = ((side, side), f32)
    grads = kernel_call(
        spread_body,
        [
            ((side, width), f32),
            vector,
            vector,
            square,
            square,
            square,
            square,
            vector,
            ((side, sff), f32),
            ((side, sff), f32),
        ],
        [total, total_x, total_core, total_both],
        vmem=16,
        cost=(0, 2 * 10**6, 0),
    )
    grads = [grad.reshape(side) if grad.shape[0] == 1 else grad for grad in grads]
    grads[0], grads[-1] = grads[0].T, grads[-1].T

    def both_rows(own, back):
        first = jnp.where(row == 0, own, back)
        second = jnp.where(row == 0, back, own)
        return jnp.stack([first, second])

    far = across(far)
    return (
        jnp.transpose(both_rows(out_own, out_back), (1, 0, 2)),
        jnp.transpose(both_rows(side_own, far[0:side]), (2, 0, 1)),
        jnp.transpose(both_rows(grad_own, far[side : 2 * side].astype(f32)), (2, 0, 1)),
        *grads,
    )


def solution(mesh):
    split = P("blk", "dp", None)
    return jax.shard_map(
        per_device,
        mesh=mesh,
        in_specs=(split, split, P("dp", None)) + (P(),) * 18 + (split,),
        out_specs=(split,) * 3 + (P(),) * 10,
        check_vma=False,
    )
```

```python
import math

import jax
import jax.numpy as jnp
from jax import lax
from jax.experimental import pallas as pl
from jax.experimental.pallas import tpu as pltpu
from jax.sharding import PartitionSpec as P

HEADS = 12
SHEADS = 12
GROUP = 6
SPARE = 64
EPS = 1e-06
LOG2E = math.log2(math.e)
FAR = 2.0**100
LOW_TOTAL, HIGH_TOTAL = 2.0**-80, 2.0**100

f32, bf16, i32 = jnp.float32, jnp.bfloat16, jnp.int32


def nn(left, right):
    return jnp.dot(left, right, preferred_element_type=f32)


def nt(left, right):
    return lax.dot_general(left, right, (((1,), (1,)), ((), ())), preferred_element_type=f32)


def tn(left, right):
    return lax.dot_general(left, right, (((0,), (0,)), ((), ())), preferred_element_type=f32)


def ones_where(condition):
    return jnp.where(condition, 1.0, 0.0).astype(bf16)


def iota(shape, dim):
    return lax.broadcasted_iota(i32, shape, dim)


def eye(size):
    return ones_where(iota((size, size), 0) == iota((size, size), 1))


def norm_lanes(value, gain):
    return value * lax.rsqrt(jnp.mean(value * value, axis=1, keepdims=True) + EPS) * gain


def gelu(value):
    return 0.5 * value * (1.0 + lax.erf(value * math.sqrt(0.5)))


def gelu_slope(value):
    bell = jnp.exp2(value * value * (-0.5 * LOG2E)) * (1.0 / math.sqrt(2.0 * math.pi))
    return 0.5 * (1.0 + lax.erf(value * math.sqrt(0.5))) + value * bell


def kernel_call(body, outs, ins, *, vmem, scratch=(), whole=(), scalars=(), cost=(0, 0, 0)):
    specs = [
        pl.BlockSpec(
            memory_space=pl.ANY if i in whole else pltpu.SMEM if i in scalars else pltpu.VMEM
        )
        for i in range(len(ins))
    ]
    return pl.pallas_call(
        body,
        out_shape=[jax.ShapeDtypeStruct(shape, kind) for shape, kind in outs],
        in_specs=specs,
        out_specs=[pl.BlockSpec(memory_space=pltpu.VMEM)] * len(outs),
        scratch_shapes=list(scratch),
        compiler_params=pltpu.CompilerParams(vmem_limit_bytes=vmem * 2**20),
        cost_estimate=pl.CostEstimate(flops=cost[0], bytes_accessed=cost[1], transcendentals=cost[2]),
    )(*ins)


def doubled(rows, columns, feature, transposed):
    wide, thin = iota((rows, columns), 0), iota((rows, columns), 1)
    if not transposed:
        wide, thin = thin, wide
    source = (wide // (2 * feature)) * feature + wide % feature
    return ones_where(source == thin)


def bounds(doc_lengths, row):
    starts, ends, at = [], [], jnp.int32(0)
    for d in range(doc_lengths.shape[1]):
        starts.append(at)
        at = at + doc_lengths[row, d]
        ends.append(at)
    return starts, ends


def in_doc(doc_lengths, row, runs, length, shape, token_dim):
    starts, ends = bounds(doc_lengths, row)
    parts = []
    part_shape = list(shape)
    part_shape[token_dim] = length
    number = iota(tuple(part_shape), 1 - token_dim)
    first = jnp.zeros(tuple(part_shape), i32)
    last = first
    for d, (start, end) in enumerate(zip(starts, ends)):
        first = jnp.where(number == d, start, first)
        last = jnp.where(number == d, end, last)
    for run in runs:
        position = iota(tuple(part_shape), token_dim) + run
        parts.append(jnp.where((position >= first) & (position < last), 1.0, 0.0))
    return jnp.concatenate(parts, axis=token_dim)


def side_weights_body(
    s_query, s_key, s_value, s_out, s_inner, gate, gain_in, gain_mid, dup, dup_t, tall_t, columns, lines
):
    side, hidden = s_inner.shape
    feature = side // SHEADS
    spread = doubled(side, dup.shape[1], feature, False)
    dup[...] = nn(s_key[...], spread).astype(bf16)
    spread_t = doubled(2 * side, side, feature, True)
    for i, weight in enumerate((s_query, s_key, s_value)):
        dup_t[2 * side * i : 2 * side * (i + 1)] = nt(spread_t, weight[...]).astype(bf16)
    tall_t[0:side] = nt(eye(side), s_out[...]).astype(bf16)
    tall_t[side : side + hidden] = nt(eye(hidden), s_inner[...]).astype(bf16)
    lines[...] = jnp.zeros(lines.shape, f32)
    for i, line in enumerate((gate, gain_in, gain_mid)):
        lines[i : i + 1, 0:side] = line[...].reshape(1, side)
    columns[...] = lines[...].T[0:side]


def prepare_body(
    doc_lengths, w_value, norm_in, norm_mid, value_t, gains, key_doc, query_doc, side_key_doc, side_query_doc
):
    value_t[...] = nt(eye(w_value.shape[0]), w_value[...]).astype(bf16)
    for i, line in enumerate((norm_in, norm_mid)):
        gains[i : i + 1] = line[...].astype(f32).reshape(1, line.shape[0])
    keys, tokens = key_doc.shape[0], query_doc.shape[0]
    span = tokens // 2
    place, half = lax.axis_index("blk"), lax.axis_size("blk") // 2
    row = place // half
    own, mate = place * span, (place ^ 1) * span
    far, far_mate = (place ^ half) * span, (place ^ half ^ 1) * span
    found = in_doc(doc_lengths, row, (own, mate, far, far_mate), span, (keys, 128), 0)
    key_doc[...] = (found - 1.0).astype(bf16)
    mine = jnp.concatenate([found[0:span], found[tokens : tokens + span]], axis=0)
    query_doc[...] = (mine * FAR).astype(bf16)
    mates = jnp.concatenate([found[span:tokens], found[tokens + span : keys]], axis=0)
    spare = SPARE
    low = iota((keys, 128), 1) < spare
    ordered = pltpu.roll(jnp.concatenate([mine, mates], axis=0), spare, 1)
    side_key_doc[...] = jnp.where(low, 0.0, ordered - 1.0).astype(bf16)
    side_query_doc[...] = (in_doc(doc_lengths, row, (own, far), span, (16, tokens), 1) * FAR).astype(bf16)


def project(tokens, gain, w_query, w_key, value_t, scale, queries):
    normed = norm_lanes(tokens.astype(f32), gain).astype(bf16)
    query = (nn(normed[0:queries], w_query[...]) * scale).astype(bf16)
    return query, nn(normed, w_key[...]).astype(bf16), nt(value_t[...], normed).astype(bf16)


def padded(value_t, head):
    ones = jnp.ones((16, value_t.shape[1]), bf16)
    pieces = []
    for at in range(0, value_t.shape[0], head):
        pieces += [value_t[at : at + head], ones]
    return jnp.concatenate(pieces, axis=0)


def pair_lanes(j):
    return pl.ds(pl.multiple_of(j * 128, 128), 128)


def pair_sums(j, queries, query_doc, keys, key_doc, values, shifted=False):
    width = queries[0].shape[1]
    head = width // HEADS
    stride = values[0].shape[0] // HEADS
    lanes = pair_lanes(j)
    key = jnp.concatenate([ref[:, lanes] for ref in keys], axis=0)
    key = jnp.concatenate([key, key_doc], axis=1)
    query = jnp.concatenate([ref[:, lanes] for ref in queries], axis=0)
    rows = pl.ds(pl.multiple_of(j * 2 * stride, 16), 2 * stride)
    value = jnp.concatenate([ref[rows, :] for ref in values], axis=1)
    lane = iota((1, 128), 1) // head
    masked = [jnp.concatenate([query * ones_where(lane == i), query_doc], axis=1) for i in range(2)]
    count = query.shape[0]

    scores = nt(key, jnp.concatenate(masked, axis=0))
    if shifted:
        scores = scores - jnp.max(scores, axis=0, keepdims=True)
    both = nn(value, jnp.exp2(scores).astype(bf16))
    return [both[i * stride : i * stride + head + 8, i * count : (i + 1) * count] for i in range(2)]


def first_body(own, mate, gains, w_query, w_key, value_t, key_doc, query_doc, query, key, value, part):
    _, span, width = own.shape
    head = width // HEADS
    row = lax.axis_index("blk") // (lax.axis_size("blk") // 2)
    tokens = jnp.concatenate([own[row], mate[row]], axis=0)
    query[...], key[...], value_new = project(
        tokens, gains[0:1], w_query, w_key, value_t, LOG2E * head**-0.5, span
    )
    value[...] = padded(value_new, head)

    def pair(j, carry):
        sums = pair_sums(j, [query], query_doc[0:span], [key], key_doc[0 : 2 * span], [value])
        part[j] = jnp.concatenate(sums, axis=0)
        return carry

    lax.fori_loop(0, HEADS // 2, pair, 0, unroll=6)


def out_of_range(totals):
    lowest, highest = jnp.min(totals), jnp.max(totals)
    return jnp.logical_not((lowest > LOW_TOTAL) & (highest < HIGH_TOTAL))


def second_body(
    far,
    far_mate,
    gains,
    w_query,
    w_key,
    value_t,
    key_doc,
    query_doc,
    query_a,
    key_a,
    value_a,
    part_a,
    attended,
    query,
    key,
    value,
    totals,
):
    span, width = far.shape
    head = width // HEADS
    tokens = jnp.concatenate([far[...], far_mate[...]], axis=0)
    query[...], key[...], value_new = project(
        tokens, gains[0:1], w_query, w_key, value_t, LOG2E * head**-0.5, span
    )
    value[...] = padded(value_new, head)
    keys, values, queries = [key_a, key], [value_a, value], [query_a, query]

    def finish(j, sums):
        results = []
        for i, summed in enumerate(sums):
            totals[pl.ds(pl.multiple_of((2 * j + i) * 8, 8), 8), :] = summed[head : head + 8]
            results.append(summed[0:head] * (1.0 / summed[head : head + 1]))
        attended[:, pair_lanes(j)] = jnp.concatenate(results, axis=0).T.astype(bf16)

    def pair(j, carry):
        old = pair_sums(j, [query_a], query_doc[0:span], [key], key_doc[2 * span : 4 * span], [value])
        new = pair_sums(j, [query], query_doc[span : 2 * span], keys, key_doc[...], values)
        sums = []
        for i in range(2):
            rows = slice(i * (head + 8), (i + 1) * (head + 8))
            sums.append(jnp.concatenate([old[i] + part_a[j, rows], new[i]], axis=1))
        finish(j, sums)
        return carry

    lax.fori_loop(0, HEADS // 2, pair, 0, unroll=6)

    @pl.when(out_of_range(totals[...]))
    def _():
        def again(j, carry):
            finish(j, pair_sums(j, queries, query_doc[...], keys, key_doc[...], values, shifted=True))
            return carry

        lax.fori_loop(0, HEADS // 2, again, 0)


def dense_body(
    own, far, attended, gains, w_out, w_inner, w_outer, down_w, columns, state, side_far, out_own, out_far, sn_rows, sn_t, mixed_t, lead_t
):
    _, span, width = own.shape
    row = lax.axis_index("blk") // (lax.axis_size("blk") // 2)
    tokens = jnp.concatenate([own[row], far[...]], axis=0)
    after = tokens.astype(f32) + nn(attended[...], w_out[...])
    middle = norm_lanes(after, gains[1:2]).astype(bf16)
    result = after
    for at in range(0, w_inner.shape[1], width):
        act = gelu(nn(middle, w_inner[:, at : at + width])).astype(bf16)
        result = result + nn(act, w_outer[at : at + width, :])
    out = result.astype(bf16)
    out_own[...] = out[0:span]
    out_far[...] = out[span : 2 * span]

    side = state.shape[1]
    down_t = nt(down_w[...], out)
    state_t = jnp.concatenate([state[row], side_far[0:side]], axis=1).astype(f32)
    gate_open = jax.nn.sigmoid(columns[:, 0:1])
    mixed = gate_open * down_t + (1.0 - gate_open) * state_t
    normed = (
        mixed * lax.rsqrt(jnp.mean(mixed * mixed, axis=0, keepdims=True) + EPS) * columns[:, 1:2]
    )
    mixed_t[...] = mixed
    lead_t[...] = down_t - state_t
    sn_t[...] = normed.astype(bf16)
    sn_rows[...] = normed.T.astype(bf16)


def outer_rows(left, right):
    return jnp.concatenate([left[f : f + 1] * right for f in range(left.shape[0])], axis=0)


def inner_rows(left, products):
    count = left.shape[0]
    total = left[0:1] * products[0:count]
    for f in range(1, count):
        total = total + left[f : f + 1] * products[f * count : (f + 1) * count]
    return total


def two_parts(value):
    high = value.astype(bf16).astype(f32)
    return [high, value - high]


def side_body(
    sn_own,
    sn_mate,
    mixed_t,
    cot,
    side_far,
    dup,
    dup_t,
    tall_t,
    s_outer_t,
    s_out,
    s_inner,
    columns,
    key_doc,
    query_doc,
    dkv_own,
    dkv_mate,
    dmid_t,
    attn_t,
    inverse,
    moments,
    mid_t,
    inner_t,
    normed_t,
    dinner_t,
    dnormed_t,
    dattn_t,
    weights,
    keys,
    key_t,
    value_t,
    query_t,
    query_s,
    query_h,
    totals,
    back_rows,
    dkv_t,
):
    tokens, side = sn_own.shape
    feature = side // SHEADS
    hidden = s_inner.shape[1]
    wide = 2 * side
    row = lax.axis_index("blk") // (lax.axis_size("blk") // 2)
    scale = feature**-0.5

    sn = jnp.concatenate([sn_own[...], sn_mate[...]], axis=0)
    projected = nn(sn, dup[...]).astype(bf16)
    keys[:, 0:128] = projected[:, 0:128]
    keys[:, 128:256] = projected[:, 128:256] + key_doc[...]
    key_t[...] = nt(dup_t[wide : 2 * wide], sn).astype(bf16)
    second = iota((wide, 2 * tokens), 0) % (2 * feature) >= feature
    value_t[...] = jnp.where(second, 1.0, nt(dup_t[2 * wide : 3 * wide], sn)).astype(bf16)
    query = nt(dup_t[0:wide], sn_own[...]).astype(bf16)
    query_t[...] = query
    scaled = query.astype(f32) * (scale * LOG2E)
    high = scaled.astype(bf16).astype(f32)
    second = iota((wide, tokens), 0) % (2 * feature) >= feature
    query_s[...] = jnp.where(second, scaled - high, high).astype(bf16)
    for i in range(GROUP):
        query_h[i] = jnp.zeros(query_h.shape[1:], bf16)
        query_h[i, wide : wide + 16] = query_doc[...]

    def head_rows(h, count):
        return pl.ds(pl.multiple_of(h * count, count), count)

    def attend(shifted):
        def group(j, carry):
            for i in range(GROUP):
                h = GROUP * j + i
                rows, eight = head_rows(h, 16), head_rows(h, 8)
                query_h[i, rows, :] = query_s[rows, :]
                scores = nn(keys[...], query_h[i])
                query_h[i, rows, :] = jnp.zeros((16, tokens), bf16)
                if shifted:
                    scores = scores - jnp.max(scores, axis=0, keepdims=True)
                weight = jnp.exp2(scores).astype(bf16)
                weights[h] = weight
                value, key = value_t[rows, :], key_t[rows, :]
                products = outer_rows(value[0:feature].astype(f32), key[0:feature].astype(f32))
                products = jnp.concatenate(two_parts(products), axis=0).astype(bf16)
                summed = nn(jnp.concatenate([value, key, products], axis=0), weight)
                total = summed[feature : 2 * feature]
                totals[eight, :] = total
                invert = 1.0 / total
                inverse[eight, :] = invert
                attn_t[eight, :] = summed[0:feature] * invert
                at = 4 * feature + feature * feature
                moments[h] = jnp.concatenate(
                    [summed[2 * feature : 4 * feature], summed[4 * feature : at] + summed[at:]], axis=0
                )
            return carry

        lax.fori_loop(0, SHEADS // GROUP, group, 0)

    attend(False)

    @pl.when(out_of_range(totals[...]))
    def _():
        attend(True)

    attn = attn_t[...]
    attn_low = attn.astype(bf16)
    mid = mixed_t[...] + nn(tall_t[0:side], attn_low)
    mid_scale = lax.rsqrt(jnp.mean(mid * mid, axis=0, keepdims=True) + EPS)
    gain = columns[:, 2:3]
    unit = mid * mid_scale
    normed = (unit * gain).astype(bf16)
    inner = nn(tall_t[side : side + hidden], normed)
    dy_low = jnp.concatenate([cot[row], side_far[side : 2 * side]], axis=1)
    dinner = (gelu_slope(inner) * tn(s_outer_t[...], dy_low)).astype(bf16)
    dnormed = nn(s_inner[...], dinner)
    scaled = dnormed * gain
    dmid = dy_low.astype(f32) + mid_scale * (
        scaled - unit * jnp.mean(scaled * unit, axis=0, keepdims=True)
    )
    dmid_t[...] = dmid
    dattn = nn(s_out[...], dmid.astype(bf16)).astype(bf16).astype(f32)
    mid_t[...] = mid
    inner_t[...] = inner
    normed_t[...] = normed
    dinner_t[...] = dinner
    dnormed_t[...] = dnormed
    dattn_t[...] = dattn

    for h in range(SHEADS):
        eight = slice(h * feature, (h + 1) * feature)
        invert = inverse[eight, :]
        term = jnp.sum(dattn[eight] * attn[eight], axis=0, keepdims=True)
        query = query_t[2 * h * feature : (2 * h + 1) * feature].astype(f32)
        share = dattn[eight] * invert
        back_rows[h] = jnp.concatenate(
            two_parts(share) + two_parts(term * invert * query) + two_parts(outer_rows(share, query)), axis=0
        ).astype(bf16)

    def back(j, carry):
        for i in range(GROUP):
            h = GROUP * j + i
            summed = nt(back_rows[h], weights[h])
            dkv_t[pl.ds(pl.multiple_of(side + h * feature, feature), feature), :] = (
                summed[0:feature] + summed[feature : 2 * feature]
            )
            value = value_t[head_rows(h, 16), :][0:feature].astype(f32)
            at = 4 * feature + feature * feature
            raw = inner_rows(value, summed[4 * feature : at] + summed[at:])
            raw = raw - (summed[2 * feature : 3 * feature] + summed[3 * feature : 4 * feature])
            dkv_t[head_rows(h, feature), :] = raw * scale
        return carry

    lax.fori_loop(0, SHEADS // GROUP, back, 0)
    dkv_own[...] = dkv_t[:, 0:tokens]
    dkv_mate[...] = dkv_t[:, tokens : 2 * tokens].astype(bf16)


def aside_body(
    attn_t,
    inverse,
    moments,
    mid_t,
    inner_t,
    normed_t,
    dinner_t,
    dnormed_t,
    dattn_t,
    dmid_t,
    cot,
    side_far,
    s_outer_t,
    out_own,
    out_far,
    dquery,
    early,
):
    side, tokens = mid_t.shape
    span = tokens // 2
    feature = side // SHEADS
    hidden = inner_t.shape[0]
    row = lax.axis_index("blk") // (lax.axis_size("blk") // 2)
    mid = mid_t[...]
    act = gelu(inner_t[...]).astype(bf16)
    out = (mid + nn(s_outer_t[...], act)).astype(bf16)
    out_own[...] = out[:, 0:span]
    out_far[...] = out[:, span : 2 * span]
    dy_low = jnp.concatenate([cot[row], side_far[side : 2 * side]], axis=1)
    early[:, 0:hidden] = nt(normed_t[...], dinner_t[...])
    early[:, hidden : 2 * hidden] = nt(dy_low, act)
    unit = mid * lax.rsqrt(jnp.mean(mid * mid, axis=0, keepdims=True) + EPS)
    grad_gain = jnp.sum(dnormed_t[...] * unit, axis=1, keepdims=True)
    last = nt(attn_t[...].astype(bf16), dmid_t[...].astype(bf16))
    last = jnp.concatenate([last, jnp.zeros((side, 128 - side), f32)], axis=1)
    early[:, 2 * hidden : 2 * hidden + 128] = jnp.where(
        iota((side, 128), 1) == side, grad_gain, last
    )
    for h in range(SHEADS):
        eight = slice(h * feature, (h + 1) * feature)
        dattn = dattn_t[eight, :]
        term = jnp.sum(dattn * attn_t[eight, :], axis=0, keepdims=True)
        moment = moments[h]
        raw = inner_rows(dattn, moment[2 * feature :]) - term * moment[0:feature]
        dquery[eight, :] = raw * inverse[eight, :] * feature**-0.5


def last_body(
    dquery,
    dkv_own,
    dkv_back,
    sn_t,
    dmid_t,
    mixed_t,
    lead_t,
    out_own,
    out_far,
    s_query,
    s_key,
    s_value,
    columns,
    early,
    side_out_far,
    state_own,
    far,
    keep,
    send,
    pack,
):
    side, tokens = sn_t.shape
    span = tokens // 2
    width = out_own.shape[1]
    dq = dquery[...].astype(bf16)
    dkv = (dkv_own[...].astype(bf16).astype(f32) + dkv_back[...].astype(f32)).astype(bf16)
    dk, dv = dkv[0:side], dkv[side : 2 * side]
    sn = sn_t[...]
    dnormed = nn(s_query[...], dq) + nn(s_key[...], dk) + nn(s_value[...], dv)
    mixed = mixed_t[...]
    mixed_scale = lax.rsqrt(jnp.mean(mixed * mixed, axis=0, keepdims=True) + EPS)
    unit = mixed * mixed_scale
    scaled = dnormed * columns[:, 1:2]
    dmixed = dmid_t[...] + mixed_scale * (
        scaled - unit * jnp.mean(scaled * unit, axis=0, keepdims=True)
    )
    gate_open = jax.nn.sigmoid(columns[:, 0:1])
    grad_gain = jnp.sum(dnormed * unit, axis=1, keepdims=True)
    grad_gate = jnp.sum(dmixed * lead_t[...], axis=1, keepdims=True) * gate_open * (1.0 - gate_open)
    state = (1.0 - gate_open) * dmixed
    state_own[...] = state[:, 0:span]
    far[0:side] = side_out_far[...]
    far[side : 2 * side] = state[:, span:tokens].astype(bf16)
    ddown = (gate_open * dmixed).astype(bf16)
    pack[:, 0:width] = nn(ddown[:, 0:span], out_own[...]) + nn(ddown[:, span:tokens], out_far[...])
    at = width
    blank = jnp.zeros((side, 128 - side), f32)
    for grad in (dq, dk, dv):
        pack[:, at : at + 128] = jnp.concatenate([nt(sn, grad), blank], axis=1)
        at += 128
    lane = iota((side, 128), 1)
    inner = early.shape[1] - 128
    vectors = early[:, inner : inner + 128]
    vectors = jnp.where(lane == side + 1, grad_gain, vectors)
    pack[:, at : at + 128] = jnp.where(lane == side + 2, grad_gate, vectors)
    pack[:, at + 128 : at + 128 + inner] = early[:, 0:inner]
    size = keep.shape[1]
    core = lax.axis_index("blk") % 2
    keep[...] = pack[:, pl.ds(pl.multiple_of(core * size, 128), size)].astype(bf16)
    send[...] = pack[:, pl.ds(pl.multiple_of((1 - core) * size, 128), size)].astype(bf16)


def quarter_index():
    return (lax.axis_index("blk") // 2) % 2 + 2 * (lax.axis_index("dp") % 2)


def spread_body(*refs):
    pieces, refs = refs[0:8], refs[8:]
    (
        grad_down,
        grad_gate,
        gain_in,
        grad_query,
        grad_key,
        grad_value,
        grad_out,
        gain_mid,
        grad_inner,
        grad_outer,
        pack,
    ) = refs
    side, width = grad_down.shape
    hidden = grad_inner.shape[1]
    size = pieces[0].shape[1]
    core, quarter = lax.axis_index("blk") % 2, quarter_index()
    for i, piece in enumerate(pieces):
        at = ((core ^ (i // 4)) * 4 + (quarter ^ (i % 4))) * size
        pack[:, pl.ds(pl.multiple_of(at, 128), size)] = piece[...].astype(f32)
    whole = pack[...]
    grad_down[...] = whole[:, 0:width]
    at = width
    for target in (grad_query, grad_key, grad_value):
        target[...] = whole[:, at : at + side]
        at += 128
    block = whole[:, at : at + 128]
    grad_out[...] = block[:, 0:side]
    rows = block.T
    gain_mid[...] = rows[side : side + 1]
    gain_in[...] = rows[side + 1 : side + 2]
    grad_gate[...] = rows[side + 2 : side + 3]
    at += 128
    grad_inner[...] = whole[:, at : at + hidden]
    grad_outer[...] = whole[:, at + hidden : at + 2 * hidden]


def per_device(
    hidden,
    side_state,
    doc_lengths,
    norm_in,
    w_query,
    w_key,
    w_value,
    w_out,
    norm_mid,
    w_inner,
    w_outer,
    w_down,
    gate,
    side_norm_in,
    s_query,
    s_key,
    s_value,
    s_out,
    side_norm_mid,
    s_inner,
    s_outer,
    cotangent,
):
    span, rows, width = hidden.shape
    side = side_state.shape[2]
    ff = w_inner.shape[1]
    sff = s_inner.shape[1]
    tokens = 2 * span
    feature = side // SHEADS
    blk_size, dp_size = lax.axis_size("blk"), lax.axis_size("dp")
    half = blk_size // 2
    place = lax.axis_index("blk")
    row = place // half

    def swap(value, axis, size, hop):
        return lax.ppermute(value, axis, [(i, i ^ hop) for i in range(size)])

    def across(value):
        return swap(value, "blk", blk_size, half)

    def beside(value):
        return swap(value, "blk", blk_size, 1)

    hidden = jnp.transpose(hidden, (1, 0, 2))
    hidden_far = across(lax.dynamic_index_in_dim(hidden, 1 - row, 0, keepdims=False))
    hidden_mate = beside(hidden)
    state, cot = (jnp.transpose(array, (1, 2, 0)) for array in (side_state, cotangent))
    side_far = across(
        lax.dynamic_index_in_dim(jnp.concatenate([state, cot], axis=1), 1 - row, 0, keepdims=False)
    )
    down_w, s_outer_t = w_down.T, s_outer.T

    value_t, gains, key_doc, query_doc, side_key_doc, side_query_doc = kernel_call(
        prepare_body,
        [
            ((width, width), bf16),
            ((2, width), f32),
            ((2 * tokens, 128), bf16),
            ((tokens, 128), bf16),
            ((2 * tokens, 128), bf16),
            ((16, tokens), bf16),
        ],
        [doc_lengths, w_value, norm_in, norm_mid],
        vmem=16,
        scalars=(0,),
        cost=(1000, 1000, 0),
    )
    head = width // HEADS
    stride = head + 16
    projections = (gains, w_query, w_key, value_t, key_doc, query_doc)

    def state_of(queries, keys, columns):
        return [
            ((queries, width), bf16),
            ((keys, width), bf16),
            ((HEADS * stride, keys), bf16),
            ((HEADS // 2, 2 * (head + 8), columns), f32),
        ]

    state_a = kernel_call(
        first_body,
        state_of(span, tokens, span),
        [hidden, hidden_mate, *projections],
        vmem=24,
        cost=(1000, 1000, 0),
    )
    small = (s_query, s_key, s_value, s_out, s_inner, gate, side_norm_in, side_norm_mid)
    hidden_far, small, *state_a = lax.optimization_barrier((hidden_far, small, *state_a))
    dup, dup_t, tall_t, columns = kernel_call(
        side_weights_body,
        [
            ((side, 256), bf16),
            ((6 * side, side), bf16),
            ((side + sff, side), bf16),
            ((side, 128), f32),
        ],
        small,
        vmem=8,
        scratch=[pltpu.VMEM((128, 128), f32)],
        cost=(1000, 1000, 0),
    )
    (attended,) = kernel_call(
        second_body,
        [((tokens, width), bf16)],
        [hidden_far, beside(hidden_far), *projections, *state_a],
        vmem=30,
        scratch=[
            pltpu.VMEM((span, width), bf16),
            pltpu.VMEM((tokens, width), bf16),
            pltpu.VMEM((HEADS * stride, tokens), bf16),
            pltpu.VMEM((HEADS * 8, tokens), f32),
        ],
        cost=(8 * 10**9, 8 * 10**6, 0),
    )
    side_far, attended = lax.optimization_barrier((side_far, attended))
    out_own, out_far, sn_rows, sn_t, mixed_t, lead_t = kernel_call(
        dense_body,
        [
            ((span, width), bf16),
            ((span, width), bf16),
            ((tokens, side), bf16),
            ((side, tokens), bf16),
            ((side, tokens), f32),
            ((side, tokens), f32),
        ],
        [
            hidden,
            hidden_far,
            attended,
            gains,
            w_out,
            w_inner,
            w_outer,
            down_w,
            columns,
            state,
            side_far,
        ],
        vmem=28,
        cost=(10 * 10**9, 14 * 10**6, 0),
    )
    sn_mate = beside(sn_rows)
    out_back = across(out_far)
    dkv_own, dkv_mate, dmid_t, *carried = kernel_call(
        side_body,
        [
            ((2 * side, tokens), f32),
            ((2 * side, tokens), bf16),
            ((side, tokens), f32),
            ((side, tokens), f32),
            ((side, tokens), f32),
            ((SHEADS, feature * (feature + 2), tokens), f32),
            ((side, tokens), f32),
            ((sff, tokens), f32),
            ((side, tokens), bf16),
            ((sff, tokens), bf16),
            ((side, tokens), f32),
            ((side, tokens), f32),
        ],
        [
            sn_rows,
            sn_mate,
            mixed_t,
            cot,
            side_far,
            dup,
            dup_t,
            tall_t,
            s_outer_t,
            s_out,
            s_inner,
            columns,
            side_key_doc,
            side_query_doc,
        ],
        vmem=36,
        scratch=[
            pltpu.VMEM((SHEADS, 2 * tokens, tokens), bf16),
            pltpu.VMEM((2 * tokens, 256), bf16),
            pltpu.VMEM((2 * side, 2 * tokens), bf16),
            pltpu.VMEM((2 * side, 2 * tokens), bf16),
            pltpu.VMEM((2 * side, tokens), bf16),
            pltpu.VMEM((2 * side, tokens), bf16),
            pltpu.VMEM((GROUP, 256, tokens), bf16),
            pltpu.VMEM((side, tokens), f32),
            pltpu.VMEM((SHEADS, feature * (2 * feature + 4), tokens), bf16),
            pltpu.VMEM((2 * side, 2 * tokens), f32),
        ],
        cost=(30 * 10**9, 3 * 10**6, 0),
    )
    dkv_back = beside(dkv_mate)
    side_own, side_back, dquery, early = kernel_call(
        aside_body,
        [
            ((side, span), bf16),
            ((side, span), bf16),
            ((side, tokens), f32),
            ((side, 2 * sff + 128), f32),
        ],
        [*carried, dmid_t, cot, side_far, s_outer_t],
        vmem=12,
        cost=(10**9, 6 * 10**6, 0),
    )
    dkv_back, out_back = lax.optimization_barrier((dkv_back, out_back))
    packed = width + 4 * 128 + 2 * sff
    grad_own, far, keep, send = kernel_call(
        last_body,
        [
            ((side, span), f32),
            ((2 * side, span), bf16),
            ((side, packed // 2), bf16),
            ((side, packed // 2), bf16),
        ],
        [
            dquery,
            dkv_own,
            dkv_back,
            sn_t,
            dmid_t,
            mixed_t,
            lead_t,
            out_own,
            out_far,
            s_query,
            s_key,
            s_value,
            columns,
            early,
            side_back,
        ],
        vmem=16,
        scratch=[pltpu.VMEM((side, packed), f32)],
        cost=(10**9, 3 * 10**6, 0),
    )

    def add(*terms):
        total = terms[0].astype(f32)
        for term in terms[1:]:
            total = total + term.astype(f32)
        return total.astype(bf16)

    quarter = packed // 8
    mine = quarter_index()
    devices = dp_size * blk_size

    def between(value, chip):
        mask = 2 * (chip % 2) + blk_size * (chip // 2)
        return lax.ppermute(value, ("dp", "blk"), [(i, i ^ mask) for i in range(devices)])

    def part(value, index):
        return lax.dynamic_slice_in_dim(value, index * quarter, quarter, 1)

    total = add(keep, beside(send))
    total = add(part(total, mine), *[between(part(total, mine ^ chip), chip) for chip in (1, 2, 3)])
    total, far = lax.optimization_barrier((total, far))
    hop = 2
    while hop < dp_size:
        total = add(total, swap(total, "dp", dp_size, hop))
        hop *= 2
    pieces = [total] + [between(total, chip) for chip in (1, 2, 3)]
    pieces += [beside(piece) for piece in pieces]
    vector = ((1, side), f32)
    square = ((side, side), f32)
    grads = kernel_call(
        spread_body,
        [
            ((side, width), f32),
            vector,
            vector,
            square,
            square,
            square,
            square,
            vector,
            ((side, sff), f32),
            ((side, sff), f32),
        ],
        pieces,
        vmem=16,
        scratch=[pltpu.VMEM((side, packed), f32)],
        cost=(0, 2 * 10**6, 0),
    )
    grads = [grad.reshape(side) if grad.shape[0] == 1 else grad for grad in grads]
    grads[0], grads[-1] = grads[0].T, grads[-1].T

    def both_rows(own, back):
        first = jnp.where(row == 0, own, back)
        second = jnp.where(row == 0, back, own)
        return jnp.stack([first, second])

    far = across(far)
    return (
        jnp.transpose(both_rows(out_own, out_back), (1, 0, 2)),
        jnp.transpose(both_rows(side_own, far[0:side]), (2, 0, 1)),
        jnp.transpose(both_rows(grad_own, far[side : 2 * side].astype(f32)), (2, 0, 1)),
        *grads,
    )


def solution(mesh):
    split = P("blk", "dp", None)
    return jax.shard_map(
        per_device,
        mesh=mesh,
        in_specs=(split, split, P("dp", None)) + (P(),) * 18 + (split,),
        out_specs=(split,) * 3 + (P(),) * 10,
        check_vma=False,
    )
```

```python
import math

import jax
import jax.numpy as jnp
from jax import lax
from jax.experimental import pallas as pl
from jax.experimental.pallas import tpu as pltpu
from jax.sharding import PartitionSpec as P

HEADS = 12
SHEADS = 12
SPARE = 64
EPS = 1e-06
LOG2E = math.log2(math.e)
FAR = 2.0**100
LOW_TOTAL, HIGH_TOTAL = 2.0**-60, 2.0**60

f32, bf16, i32 = jnp.float32, jnp.bfloat16, jnp.int32


def nn(left, right):
    return jnp.dot(left, right, preferred_element_type=f32)


def nt(left, right):
    return lax.dot_general(left, right, (((1,), (1,)), ((), ())), preferred_element_type=f32)


def tn(left, right):
    return lax.dot_general(left, right, (((0,), (0,)), ((), ())), preferred_element_type=f32)


def ones_where(condition):
    return jnp.where(condition, 1.0, 0.0).astype(bf16)


def iota(shape, dim):
    return lax.broadcasted_iota(i32, shape, dim)


def eye(size):
    return ones_where(iota((size, size), 0) == iota((size, size), 1))


def norm_lanes(value, gain):
    return value * lax.rsqrt(jnp.mean(value * value, axis=1, keepdims=True) + EPS) * gain


def gelu(value):
    return 0.5 * value * (1.0 + lax.erf(value * math.sqrt(0.5)))


def gelu_slope(value):
    bell = jnp.exp2(value * value * (-0.5 * LOG2E)) * (1.0 / math.sqrt(2.0 * math.pi))
    return 0.5 * (1.0 + lax.erf(value * math.sqrt(0.5))) + value * bell


def kernel_call(body, outs, ins, *, vmem, scratch=(), whole=(), scalars=(), cost=(0, 0, 0)):
    specs = [
        pl.BlockSpec(
            memory_space=pl.ANY if i in whole else pltpu.SMEM if i in scalars else pltpu.VMEM
        )
        for i in range(len(ins))
    ]
    return pl.pallas_call(
        body,
        out_shape=[jax.ShapeDtypeStruct(shape, kind) for shape, kind in outs],
        in_specs=specs,
        out_specs=[pl.BlockSpec(memory_space=pltpu.VMEM)] * len(outs),
        scratch_shapes=list(scratch),
        compiler_params=pltpu.CompilerParams(vmem_limit_bytes=vmem * 2**20),
        cost_estimate=pl.CostEstimate(flops=cost[0], bytes_accessed=cost[1], transcendentals=cost[2]),
    )(*ins)


def doubled(rows, columns, feature, transposed):
    wide, thin = iota((rows, columns), 0), iota((rows, columns), 1)
    if not transposed:
        wide, thin = thin, wide
    source = (wide // (2 * feature)) * feature + wide % feature
    return ones_where(source == thin)


def bounds(doc_lengths, row):
    starts, ends, at = [], [], jnp.int32(0)
    for d in range(doc_lengths.shape[1]):
        starts.append(at)
        at = at + doc_lengths[row, d]
        ends.append(at)
    return starts, ends


def in_doc(doc_lengths, row, runs, length, shape, token_dim):
    starts, ends = bounds(doc_lengths, row)
    parts = []
    part_shape = list(shape)
    part_shape[token_dim] = length
    number = iota(tuple(part_shape), 1 - token_dim)
    first = jnp.zeros(tuple(part_shape), i32)
    last = first
    for d, (start, end) in enumerate(zip(starts, ends)):
        first = jnp.where(number == d, start, first)
        last = jnp.where(number == d, end, last)
    for run in runs:
        position = iota(tuple(part_shape), token_dim) + run
        parts.append(jnp.where((position >= first) & (position < last), 1.0, 0.0))
    return jnp.concatenate(parts, axis=token_dim)


def side_weights_body(
    s_query, s_key, s_value, s_out, s_inner, gate, gain_in, gain_mid, dup, dup_t, tall_t, columns, lines
):
    side, hidden = s_inner.shape
    feature = side // SHEADS
    spread = doubled(side, dup.shape[1], feature, False)
    dup[...] = nn(s_key[...], spread).astype(bf16)
    spread_t = doubled(2 * side, side, feature, True)
    for i, weight in enumerate((s_query, s_key, s_value)):
        dup_t[2 * side * i : 2 * side * (i + 1)] = nt(spread_t, weight[...]).astype(bf16)
    tall_t[0:side] = nt(eye(side), s_out[...]).astype(bf16)
    tall_t[side : side + hidden] = nt(eye(hidden), s_inner[...]).astype(bf16)
    lines[...] = jnp.zeros(lines.shape, f32)
    for i, line in enumerate((gate, gain_in, gain_mid)):
        lines[i : i + 1, 0:side] = line[...].reshape(1, side)
    columns[...] = lines[...].T[0:side]


def prepare_body(
    doc_lengths, w_value, norm_in, norm_mid, value_t, gains, key_doc, query_doc, side_key_doc, side_query_doc
):
    value_t[...] = nt(eye(w_value.shape[0]), w_value[...]).astype(bf16)
    for i, line in enumerate((norm_in, norm_mid)):
        gains[i : i + 1] = line[...].astype(f32).reshape(1, line.shape[0])
    keys, tokens = key_doc.shape[0], query_doc.shape[0]
    span = tokens // 2
    place, half = lax.axis_index("blk"), lax.axis_size("blk") // 2
    row = place // half
    own, mate = place * span, (place ^ 1) * span
    far, far_mate = (place ^ half) * span, (place ^ half ^ 1) * span
    found = in_doc(doc_lengths, row, (own, mate, far, far_mate), span, (keys, 128), 0)
    key_doc[...] = (found - 1.0).astype(bf16)
    mine = jnp.concatenate([found[0:span], found[tokens : tokens + span]], axis=0)
    query_doc[...] = (mine * FAR).astype(bf16)
    mates = jnp.concatenate([found[span:tokens], found[tokens + span : keys]], axis=0)
    spare = SPARE
    low = iota((keys, 128), 1) < spare
    ordered = pltpu.roll(jnp.concatenate([mine, mates], axis=0), spare, 1)
    side_key_doc[...] = jnp.where(low, 0.0, ordered - 1.0).astype(bf16)
    side_query_doc[...] = (in_doc(doc_lengths, row, (own, far), span, (16, tokens), 1) * FAR).astype(bf16)


def project(tokens, gain, w_query, w_key, value_t, scale, queries):
    normed = norm_lanes(tokens.astype(f32), gain).astype(bf16)
    query = (nn(normed[0:queries], w_query[...]) * scale).astype(bf16)
    return query, nn(normed, w_key[...]).astype(bf16), nt(value_t[...], normed).astype(bf16)


def padded(value_t, head):
    ones = jnp.ones((16, value_t.shape[1]), bf16)
    pieces = []
    for at in range(0, value_t.shape[0], head):
        pieces += [value_t[at : at + head], ones]
    return jnp.concatenate(pieces, axis=0)


def pair_lanes(j):
    return pl.ds(pl.multiple_of(j * 128, 128), 128)


def pair_sums(j, queries, query_doc, keys, key_doc, values, shifted=False):
    width = queries[0].shape[1]
    head = width // HEADS
    stride = values[0].shape[0] // HEADS
    lanes = pair_lanes(j)
    key = jnp.concatenate([ref[:, lanes] for ref in keys], axis=0)
    key = jnp.concatenate([key, key_doc], axis=1)
    query = jnp.concatenate([ref[:, lanes] for ref in queries], axis=0)
    rows = pl.ds(pl.multiple_of(j * 2 * stride, 16), 2 * stride)
    value = jnp.concatenate([ref[rows, :] for ref in values], axis=1)
    lane = iota((1, 128), 1) // head
    masked = [jnp.concatenate([query * ones_where(lane == i), query_doc], axis=1) for i in range(2)]
    count = query.shape[0]

    scores = nt(key, jnp.concatenate(masked, axis=0))
    if shifted:
        scores = scores - jnp.max(scores, axis=0, keepdims=True)
    both = nn(value, jnp.exp2(scores).astype(bf16))
    return [both[i * stride : i * stride + head + 8, i * count : (i + 1) * count] for i in range(2)]


def first_body(own, mate, gains, w_query, w_key, value_t, key_doc, query_doc, query, key, value, part):
    _, span, width = own.shape
    head = width // HEADS
    row = lax.axis_index("blk") // (lax.axis_size("blk") // 2)
    tokens = jnp.concatenate([own[row], mate[row]], axis=0)
    query[...], key[...], value_new = project(
        tokens, gains[0:1], w_query, w_key, value_t, LOG2E * head**-0.5, span
    )
    value[...] = padded(value_new, head)

    def pair(j, carry):
        sums = pair_sums(j, [query], query_doc[0:span], [key], key_doc[0 : 2 * span], [value])
        part[j] = jnp.concatenate(sums, axis=0)
        return carry

    lax.fori_loop(0, HEADS // 2, pair, 0, unroll=6)


def out_of_range(totals):
    lowest, highest = jnp.min(totals), jnp.max(totals)
    return jnp.logical_not((lowest > LOW_TOTAL) & (highest < HIGH_TOTAL))


def second_body(
    far,
    far_mate,
    gains,
    w_query,
    w_key,
    value_t,
    key_doc,
    query_doc,
    query_a,
    key_a,
    value_a,
    part_a,
    attended,
    query,
    key,
    value,
    totals,
):
    span, width = far.shape
    head = width // HEADS
    tokens = jnp.concatenate([far[...], far_mate[...]], axis=0)
    query[...], key[...], value_new = project(
        tokens, gains[0:1], w_query, w_key, value_t, LOG2E * head**-0.5, span
    )
    value[...] = padded(value_new, head)
    keys, values, queries = [key_a, key], [value_a, value], [query_a, query]

    def finish(j, sums):
        results = []
        for i, summed in enumerate(sums):
            totals[pl.ds(pl.multiple_of((2 * j + i) * 8, 8), 8), :] = summed[head : head + 8]
            results.append(summed[0:head] * (1.0 / summed[head : head + 1]))
        attended[:, pair_lanes(j)] = jnp.concatenate(results, axis=0).T.astype(bf16)

    def pair(j, carry):
        old = pair_sums(j, [query_a], query_doc[0:span], [key], key_doc[2 * span : 4 * span], [value])
        new = pair_sums(j, [query], query_doc[span : 2 * span], keys, key_doc[...], values)
        sums = []
        for i in range(2):
            rows = slice(i * (head + 8), (i + 1) * (head + 8))
            sums.append(jnp.concatenate([old[i] + part_a[j, rows], new[i]], axis=1))
        finish(j, sums)
        return carry

    lax.fori_loop(0, HEADS // 2, pair, 0, unroll=6)

    @pl.when(out_of_range(totals[...]))
    def _():
        def again(j, carry):
            finish(j, pair_sums(j, queries, query_doc[...], keys, key_doc[...], values, shifted=True))
            return carry

        lax.fori_loop(0, HEADS // 2, again, 0)


def dense_body(
    own, far, attended, gains, w_out, w_inner, w_outer, down_w, columns, state, side_far, out_own, out_far, sn_rows, sn_t, mixed_t, lead_t
):
    _, span, width = own.shape
    row = lax.axis_index("blk") // (lax.axis_size("blk") // 2)
    tokens = jnp.concatenate([own[row], far[...]], axis=0)
    after = tokens.astype(f32) + nn(attended[...], w_out[...])
    middle = norm_lanes(after, gains[1:2]).astype(bf16)
    result = after
    for at in range(0, w_inner.shape[1], width):
        act = gelu(nn(middle, w_inner[:, at : at + width])).astype(bf16)
        result = result + nn(act, w_outer[at : at + width, :])
    out = result.astype(bf16)
    out_own[...] = out[0:span]
    out_far[...] = out[span : 2 * span]

    side = state.shape[1]
    down_t = nt(down_w[...], out)
    state_t = jnp.concatenate([state[row], side_far[0:side]], axis=1).astype(f32)
    gate_open = jax.nn.sigmoid(columns[:, 0:1])
    mixed = gate_open * down_t + (1.0 - gate_open) * state_t
    normed = (
        mixed * lax.rsqrt(jnp.mean(mixed * mixed, axis=0, keepdims=True) + EPS) * columns[:, 1:2]
    )
    mixed_t[...] = mixed
    lead_t[...] = down_t - state_t
    sn_t[...] = normed.astype(bf16)
    sn_rows[...] = normed.T.astype(bf16)


def outer_rows(left, right):
    return jnp.concatenate([left[f : f + 1] * right for f in range(left.shape[0])], axis=0)


def inner_rows(left, products):
    count = left.shape[0]
    total = left[0:1] * products[0:count]
    for f in range(1, count):
        total = total + left[f : f + 1] * products[f * count : (f + 1) * count]
    return total


def two_parts(value):
    high = value.astype(bf16).astype(f32)
    return [high, value - high]


def side_body(
    sn_own,
    sn_mate,
    mixed_t,
    cot,
    side_far,
    dup,
    dup_t,
    tall_t,
    s_outer_t,
    s_out,
    s_inner,
    columns,
    key_doc,
    query_doc,
    dkv_own,
    dkv_mate,
    dmid_t,
    attn_t,
    inverse,
    moments,
    mid_t,
    inner_t,
    normed_t,
    dinner_t,
    dnormed_t,
    dattn_t,
    weights,
    keys,
    key_t,
    value_t,
    query_t,
    query_s,
    query_h,
    totals,
    back_rows,
    dkv_t,
):
    tokens, side = sn_own.shape
    feature = side // SHEADS
    hidden = s_inner.shape[1]
    wide = 2 * side
    row = lax.axis_index("blk") // (lax.axis_size("blk") // 2)
    scale = feature**-0.5

    sn = jnp.concatenate([sn_own[...], sn_mate[...]], axis=0)
    projected = nn(sn, dup[...]).astype(bf16)
    keys[:, 0:128] = projected[:, 0:128]
    keys[:, 128:256] = projected[:, 128:256] + key_doc[...]
    key_t[...] = nt(dup_t[wide : 2 * wide], sn).astype(bf16)
    second = iota((wide, 2 * tokens), 0) % (2 * feature) >= feature
    value_t[...] = jnp.where(second, 1.0, nt(dup_t[2 * wide : 3 * wide], sn)).astype(bf16)
    query = nt(dup_t[0:wide], sn_own[...]).astype(bf16)
    query_t[...] = query
    scaled = query.astype(f32) * (scale * LOG2E)
    high = scaled.astype(bf16).astype(f32)
    second = iota((wide, tokens), 0) % (2 * feature) >= feature
    query_s[...] = jnp.where(second, scaled - high, high).astype(bf16)
    for i in range(SHEADS):
        query_h[i] = jnp.zeros(query_h.shape[1:], bf16)
        query_h[i, wide : wide + 16] = query_doc[...]

    def head_rows(h, count):
        return pl.ds(pl.multiple_of(h * count, count), count)

    def attend(shifted, size):
        def group(j, carry):
            for i in range(size):
                h = size * j + i
                rows, eight = head_rows(h, 16), head_rows(h, 8)
                query_h[i, rows, :] = query_s[rows, :]
                scores = nn(keys[...], query_h[i])
                query_h[i, rows, :] = jnp.zeros((16, tokens), bf16)
                if shifted:
                    scores = scores - jnp.max(scores, axis=0, keepdims=True)
                weight = jnp.exp2(scores).astype(bf16)
                weights[h] = weight.T
                value, key = value_t[rows, :], key_t[rows, :]
                products = outer_rows(value[0:feature].astype(f32), key[0:feature].astype(f32))
                products = jnp.concatenate(two_parts(products), axis=0).astype(bf16)
                summed = nn(jnp.concatenate([value, key, products], axis=0), weight)
                total = summed[feature : 2 * feature]
                totals[eight, :] = total
                invert = 1.0 / total
                inverse[eight, :] = invert
                attn_t[eight, :] = summed[0:feature] * invert
                at = 4 * feature + feature * feature
                moments[h] = jnp.concatenate(
                    [summed[2 * feature : 4 * feature], summed[4 * feature : at] + summed[at:]], axis=0
                )
            return carry

        lax.fori_loop(0, SHEADS // size, group, 0)

    attend(False, SHEADS)

    @pl.when(out_of_range(totals[...]))
    def _():
        attend(True, 2)

    attn = attn_t[...]
    attn_low = attn.astype(bf16)
    mid = mixed_t[...] + nn(tall_t[0:side], attn_low)
    mid_scale = lax.rsqrt(jnp.mean(mid * mid, axis=0, keepdims=True) + EPS)
    gain = columns[:, 2:3]
    unit = mid * mid_scale
    normed = (unit * gain).astype(bf16)
    inner = nn(tall_t[side : side + hidden], normed)
    dy_low = jnp.concatenate([cot[row], side_far[side : 2 * side]], axis=1)
    dinner = (gelu_slope(inner) * tn(s_outer_t[...], dy_low)).astype(bf16)
    dnormed = nn(s_inner[...], dinner)
    scaled = dnormed * gain
    dmid = dy_low.astype(f32) + mid_scale * (
        scaled - unit * jnp.mean(scaled * unit, axis=0, keepdims=True)
    )
    dmid_t[...] = dmid
    dattn = nn(s_out[...], dmid.astype(bf16)).astype(bf16).astype(f32)
    mid_t[...] = mid
    inner_t[...] = inner
    normed_t[...] = normed
    dinner_t[...] = dinner
    dnormed_t[...] = dnormed
    dattn_t[...] = dattn

    for h in range(SHEADS):
        eight = slice(h * feature, (h + 1) * feature)
        invert = inverse[eight, :]
        term = jnp.sum(dattn[eight] * attn[eight], axis=0, keepdims=True)
        query = query_t[2 * h * feature : (2 * h + 1) * feature].astype(f32)
        share = dattn[eight] * invert
        back_rows[h] = jnp.concatenate(
            two_parts(share) + two_parts(term * invert * query) + two_parts(outer_rows(share, query)), axis=0
        ).astype(bf16)

    for h in range(SHEADS):
        eight = slice(h * feature, (h + 1) * feature)
        summed = nn(back_rows[h], weights[h])
        dkv_t[side + h * feature : side + (h + 1) * feature] = (
            summed[0:feature] + summed[feature : 2 * feature]
        )
        value = value_t[2 * h * feature : (2 * h + 1) * feature].astype(f32)
        at = 4 * feature + feature * feature
        raw = inner_rows(value, summed[4 * feature : at] + summed[at:])
        raw = raw - (summed[2 * feature : 3 * feature] + summed[3 * feature : 4 * feature])
        dkv_t[eight] = raw * scale
    dkv_own[...] = dkv_t[:, 0:tokens]
    dkv_mate[...] = dkv_t[:, tokens : 2 * tokens].astype(bf16)


def aside_body(
    attn_t,
    inverse,
    moments,
    mid_t,
    inner_t,
    normed_t,
    dinner_t,
    dnormed_t,
    dattn_t,
    dmid_t,
    cot,
    side_far,
    s_outer_t,
    out_own,
    out_far,
    dquery,
    early,
):
    side, tokens = mid_t.shape
    span = tokens // 2
    feature = side // SHEADS
    hidden = inner_t.shape[0]
    row = lax.axis_index("blk") // (lax.axis_size("blk") // 2)
    mid = mid_t[...]
    act = gelu(inner_t[...]).astype(bf16)
    out = (mid + nn(s_outer_t[...], act)).astype(bf16)
    out_own[...] = out[:, 0:span]
    out_far[...] = out[:, span : 2 * span]
    dy_low = jnp.concatenate([cot[row], side_far[side : 2 * side]], axis=1)
    early[:, 0:hidden] = nt(normed_t[...], dinner_t[...])
    early[:, hidden : 2 * hidden] = nt(dy_low, act)
    unit = mid * lax.rsqrt(jnp.mean(mid * mid, axis=0, keepdims=True) + EPS)
    grad_gain = jnp.sum(dnormed_t[...] * unit, axis=1, keepdims=True)
    last = nt(attn_t[...].astype(bf16), dmid_t[...].astype(bf16))
    last = jnp.concatenate([last, jnp.zeros((side, 128 - side), f32)], axis=1)
    early[:, 2 * hidden : 2 * hidden + 128] = jnp.where(
        iota((side, 128), 1) == side, grad_gain, last
    )
    for h in range(SHEADS):
        eight = slice(h * feature, (h + 1) * feature)
        dattn = dattn_t[eight, :]
        term = jnp.sum(dattn * attn_t[eight, :], axis=0, keepdims=True)
        moment = moments[h]
        raw = inner_rows(dattn, moment[2 * feature :]) - term * moment[0:feature]
        dquery[eight, :] = raw * inverse[eight, :] * feature**-0.5


def last_body(
    dquery,
    dkv_own,
    dkv_back,
    sn_t,
    dmid_t,
    mixed_t,
    lead_t,
    out_own,
    out_far,
    s_query,
    s_key,
    s_value,
    columns,
    early,
    side_out_far,
    state_own,
    far,
    keep,
    send,
    pack,
):
    side, tokens = sn_t.shape
    span = tokens // 2
    width = out_own.shape[1]
    dq = dquery[...].astype(bf16)
    dkv = (dkv_own[...].astype(bf16).astype(f32) + dkv_back[...].astype(f32)).astype(bf16)
    dk, dv = dkv[0:side], dkv[side : 2 * side]
    sn = sn_t[...]
    dnormed = nn(s_query[...], dq) + nn(s_key[...], dk) + nn(s_value[...], dv)
    mixed = mixed_t[...]
    mixed_scale = lax.rsqrt(jnp.mean(mixed * mixed, axis=0, keepdims=True) + EPS)
    unit = mixed * mixed_scale
    scaled = dnormed * columns[:, 1:2]
    dmixed = dmid_t[...] + mixed_scale * (
        scaled - unit * jnp.mean(scaled * unit, axis=0, keepdims=True)
    )
    gate_open = jax.nn.sigmoid(columns[:, 0:1])
    grad_gain = jnp.sum(dnormed * unit, axis=1, keepdims=True)
    grad_gate = jnp.sum(dmixed * lead_t[...], axis=1, keepdims=True) * gate_open * (1.0 - gate_open)
    state = (1.0 - gate_open) * dmixed
    state_own[...] = state[:, 0:span]
    far[0:side] = side_out_far[...]
    far[side : 2 * side] = state[:, span:tokens].astype(bf16)
    ddown = (gate_open * dmixed).astype(bf16)
    pack[:, 0:width] = nn(ddown[:, 0:span], out_own[...]) + nn(ddown[:, span:tokens], out_far[...])
    at = width
    blank = jnp.zeros((side, 128 - side), f32)
    for grad in (dq, dk, dv):
        pack[:, at : at + 128] = jnp.concatenate([nt(sn, grad), blank], axis=1)
        at += 128
    lane = iota((side, 128), 1)
    inner = early.shape[1] - 128
    vectors = early[:, inner : inner + 128]
    vectors = jnp.where(lane == side + 1, grad_gain, vectors)
    pack[:, at : at + 128] = jnp.where(lane == side + 2, grad_gate, vectors)
    pack[:, at + 128 : at + 128 + inner] = early[:, 0:inner]
    size = keep.shape[1]
    core = lax.axis_index("blk") % 2
    keep[...] = pack[:, pl.ds(pl.multiple_of(core * size, 128), size)].astype(bf16)
    send[...] = pack[:, pl.ds(pl.multiple_of((1 - core) * size, 128), size)].astype(bf16)


def quarter_index():
    return (lax.axis_index("blk") // 2) % 2 + 2 * (lax.axis_index("dp") % 2)


def spread_body(*refs):
    pieces, refs = refs[0:8], refs[8:]
    (
        grad_down,
        grad_gate,
        gain_in,
        grad_query,
        grad_key,
        grad_value,
        grad_out,
        gain_mid,
        grad_inner,
        grad_outer,
        pack,
    ) = refs
    side, width = grad_down.shape
    hidden = grad_inner.shape[1]
    size = pieces[0].shape[1]
    core, quarter = lax.axis_index("blk") % 2, quarter_index()
    for i, piece in enumerate(pieces):
        at = ((core ^ (i // 4)) * 4 + (quarter ^ (i % 4))) * size
        pack[:, pl.ds(pl.multiple_of(at, 128), size)] = piece[...].astype(f32)
    whole = pack[...]
    grad_down[...] = whole[:, 0:width]
    at = width
    for target in (grad_query, grad_key, grad_value):
        target[...] = whole[:, at : at + side]
        at += 128
    block = whole[:, at : at + 128]
    grad_out[...] = block[:, 0:side]
    rows = block.T
    gain_mid[...] = rows[side : side + 1]
    gain_in[...] = rows[side + 1 : side + 2]
    grad_gate[...] = rows[side + 2 : side + 3]
    at += 128
    grad_inner[...] = whole[:, at : at + hidden]
    grad_outer[...] = whole[:, at + hidden : at + 2 * hidden]


def per_device(
    hidden,
    side_state,
    doc_lengths,
    norm_in,
    w_query,
    w_key,
    w_value,
    w_out,
    norm_mid,
    w_inner,
    w_outer,
    w_down,
    gate,
    side_norm_in,
    s_query,
    s_key,
    s_value,
    s_out,
    side_norm_mid,
    s_inner,
    s_outer,
    cotangent,
):
    span, rows, width = hidden.shape
    side = side_state.shape[2]
    ff = w_inner.shape[1]
    sff = s_inner.shape[1]
    tokens = 2 * span
    feature = side // SHEADS
    blk_size, dp_size = lax.axis_size("blk"), lax.axis_size("dp")
    half = blk_size // 2
    place = lax.axis_index("blk")
    row = place // half

    def swap(value, axis, size, hop):
        return lax.ppermute(value, axis, [(i, i ^ hop) for i in range(size)])

    def across(value):
        return swap(value, "blk", blk_size, half)

    def beside(value):
        return swap(value, "blk", blk_size, 1)

    hidden = jnp.transpose(hidden, (1, 0, 2))
    hidden_far = across(lax.dynamic_index_in_dim(hidden, 1 - row, 0, keepdims=False))
    hidden_mate = beside(hidden)
    state, cot = (jnp.transpose(array, (1, 2, 0)) for array in (side_state, cotangent))
    side_far = across(
        lax.dynamic_index_in_dim(jnp.concatenate([state, cot], axis=1), 1 - row, 0, keepdims=False)
    )
    down_w, s_outer_t = w_down.T, s_outer.T

    value_t, gains, key_doc, query_doc, side_key_doc, side_query_doc = kernel_call(
        prepare_body,
        [
            ((width, width), bf16),
            ((2, width), f32),
            ((2 * tokens, 128), bf16),
            ((tokens, 128), bf16),
            ((2 * tokens, 128), bf16),
            ((16, tokens), bf16),
        ],
        [doc_lengths, w_value, norm_in, norm_mid],
        vmem=16,
        scalars=(0,),
        cost=(1000, 1000, 0),
    )
    head = width // HEADS
    stride = head + 16
    projections = (gains, w_query, w_key, value_t, key_doc, query_doc)

    def state_of(queries, keys, columns):
        return [
            ((queries, width), bf16),
            ((keys, width), bf16),
            ((HEADS * stride, keys), bf16),
            ((HEADS // 2, 2 * (head + 8), columns), f32),
        ]

    state_a = kernel_call(
        first_body,
        state_of(span, tokens, span),
        [hidden, hidden_mate, *projections],
        vmem=24,
        cost=(1000, 1000, 0),
    )
    small = (s_query, s_key, s_value, s_out, s_inner, gate, side_norm_in, side_norm_mid)
    hidden_far, small, *state_a = lax.optimization_barrier((hidden_far, small, *state_a))
    dup, dup_t, tall_t, columns = kernel_call(
        side_weights_body,
        [
            ((side, 256), bf16),
            ((6 * side, side), bf16),
            ((side + sff, side), bf16),
            ((side, 128), f32),
        ],
        small,
        vmem=8,
        scratch=[pltpu.VMEM((128, 128), f32)],
        cost=(1000, 1000, 0),
    )
    (attended,) = kernel_call(
        second_body,
        [((tokens, width), bf16)],
        [hidden_far, beside(hidden_far), *projections, *state_a],
        vmem=30,
        scratch=[
            pltpu.VMEM((span, width), bf16),
            pltpu.VMEM((tokens, width), bf16),
            pltpu.VMEM((HEADS * stride, tokens), bf16),
            pltpu.VMEM((HEADS * 8, tokens), f32),
        ],
        cost=(8 * 10**9, 8 * 10**6, 0),
    )
    side_far, attended = lax.optimization_barrier((side_far, attended))
    out_own, out_far, sn_rows, sn_t, mixed_t, lead_t = kernel_call(
        dense_body,
        [
            ((span, width), bf16),
            ((span, width), bf16),
            ((tokens, side), bf16),
            ((side, tokens), bf16),
            ((side, tokens), f32),
            ((side, tokens), f32),
        ],
        [
            hidden,
            hidden_far,
            attended,
            gains,
            w_out,
            w_inner,
            w_outer,
            down_w,
            columns,
            state,
            side_far,
        ],
        vmem=28,
        cost=(10 * 10**9, 14 * 10**6, 0),
    )
    sn_mate = beside(sn_rows)
    out_back = across(out_far)
    dkv_own, dkv_mate, dmid_t, *carried = kernel_call(
        side_body,
        [
            ((2 * side, tokens), f32),
            ((2 * side, tokens), bf16),
            ((side, tokens), f32),
            ((side, tokens), f32),
            ((side, tokens), f32),
            ((SHEADS, feature * (feature + 2), tokens), f32),
            ((side, tokens), f32),
            ((sff, tokens), f32),
            ((side, tokens), bf16),
            ((sff, tokens), bf16),
            ((side, tokens), f32),
            ((side, tokens), f32),
        ],
        [
            sn_rows,
            sn_mate,
            mixed_t,
            cot,
            side_far,
            dup,
            dup_t,
            tall_t,
            s_outer_t,
            s_out,
            s_inner,
            columns,
            side_key_doc,
            side_query_doc,
        ],
        vmem=36,
        scratch=[
            pltpu.VMEM((SHEADS, tokens, 2 * tokens), bf16),
            pltpu.VMEM((2 * tokens, 256), bf16),
            pltpu.VMEM((2 * side, 2 * tokens), bf16),
            pltpu.VMEM((2 * side, 2 * tokens), bf16),
            pltpu.VMEM((2 * side, tokens), bf16),
            pltpu.VMEM((2 * side, tokens), bf16),
            pltpu.VMEM((SHEADS, 256, tokens), bf16),
            pltpu.VMEM((side, tokens), f32),
            pltpu.VMEM((SHEADS, feature * (2 * feature + 4), tokens), bf16),
            pltpu.VMEM((2 * side, 2 * tokens), f32),
        ],
        cost=(30 * 10**9, 3 * 10**6, 0),
    )
    dkv_back = beside(dkv_mate)
    side_own, side_back, dquery, early = kernel_call(
        aside_body,
        [
            ((side, span), bf16),
            ((side, span), bf16),
            ((side, tokens), f32),
            ((side, 2 * sff + 128), f32),
        ],
        [*carried, dmid_t, cot, side_far, s_outer_t],
        vmem=12,
        cost=(10**9, 6 * 10**6, 0),
    )
    dkv_back, out_back = lax.optimization_barrier((dkv_back, out_back))
    packed = width + 4 * 128 + 2 * sff
    grad_own, far, keep, send = kernel_call(
        last_body,
        [
            ((side, span), f32),
            ((2 * side, span), bf16),
            ((side, packed // 2), bf16),
            ((side, packed // 2), bf16),
        ],
        [
            dquery,
            dkv_own,
            dkv_back,
            sn_t,
            dmid_t,
            mixed_t,
            lead_t,
            out_own,
            out_far,
            s_query,
            s_key,
            s_value,
            columns,
            early,
            side_back,
        ],
        vmem=16,
        scratch=[pltpu.VMEM((side, packed), f32)],
        cost=(10**9, 3 * 10**6, 0),
    )

    def add(*terms):
        total = terms[0].astype(f32)
        for term in terms[1:]:
            total = total + term.astype(f32)
        return total.astype(bf16)

    quarter = packed // 8
    mine = quarter_index()
    devices = dp_size * blk_size

    def between(value, chip):
        mask = 2 * (chip % 2) + blk_size * (chip // 2)
        return lax.ppermute(value, ("dp", "blk"), [(i, i ^ mask) for i in range(devices)])

    def part(value, index):
        return lax.dynamic_slice_in_dim(value, index * quarter, quarter, 1)

    total = add(keep, beside(send))
    total = add(part(total, mine), *[between(part(total, mine ^ chip), chip) for chip in (1, 2, 3)])
    total, far = lax.optimization_barrier((total, far))
    hop = 2
    while hop < dp_size:
        total = add(total, swap(total, "dp", dp_size, hop))
        hop *= 2
    pieces = [total] + [between(total, chip) for chip in (1, 2, 3)]
    pieces += [beside(piece) for piece in pieces]
    vector = ((1, side), f32)
    square = ((side, side), f32)
    grads = kernel_call(
        spread_body,
        [
            ((side, width), f32),
            vector,
            vector,
            square,
            square,
            square,
            square,
            vector,
            ((side, sff), f32),
            ((side, sff), f32),
        ],
        pieces,
        vmem=16,
        scratch=[pltpu.VMEM((side, packed), f32)],
        cost=(0, 2 * 10**6, 0),
    )
    grads = [grad.reshape(side) if grad.shape[0] == 1 else grad for grad in grads]
    grads[0], grads[-1] = grads[0].T, grads[-1].T

    def both_rows(own, back):
        first = jnp.where(row == 0, own, back)
        second = jnp.where(row == 0, back, own)
        return jnp.stack([first, second])

    far = across(far)
    return (
        jnp.transpose(both_rows(out_own, out_back), (1, 0, 2)),
        jnp.transpose(both_rows(side_own, far[0:side]), (2, 0, 1)),
        jnp.transpose(both_rows(grad_own, far[side : 2 * side].astype(f32)), (2, 0, 1)),
        *grads,
    )


def solution(mesh):
    split = P("blk", "dp", None)
    return jax.shard_map(
        per_device,
        mesh=mesh,
        in_specs=(split, split, P("dp", None)) + (P(),) * 18 + (split,),
        out_specs=(split,) * 3 + (P(),) * 10,
        check_vma=False,
    )
```

```python
import math

import jax
import jax.numpy as jnp
from jax import lax
from jax.experimental import pallas as pl
from jax.experimental.pallas import tpu as pltpu
from jax.sharding import PartitionSpec as P

HEADS = 12
SHEADS = 12
SPARE = 96
EPS = 1e-06
LOG2E = math.log2(math.e)
FAR = 2.0**100
LOW_TOTAL, HIGH_TOTAL = 2.0**-60, 2.0**60

f32, bf16, i32 = jnp.float32, jnp.bfloat16, jnp.int32


def nn(left, right):
    return jnp.dot(left, right, preferred_element_type=f32)


def nt(left, right):
    return lax.dot_general(left, right, (((1,), (1,)), ((), ())), preferred_element_type=f32)


def tn(left, right):
    return lax.dot_general(left, right, (((0,), (0,)), ((), ())), preferred_element_type=f32)


def ones_where(condition):
    return jnp.where(condition, 1.0, 0.0).astype(bf16)


def iota(shape, dim):
    return lax.broadcasted_iota(i32, shape, dim)


def eye(size):
    return ones_where(iota((size, size), 0) == iota((size, size), 1))


def norm_lanes(value, gain):
    return value * lax.rsqrt(jnp.mean(value * value, axis=1, keepdims=True) + EPS) * gain


def gelu(value):
    return 0.5 * value * (1.0 + lax.erf(value * math.sqrt(0.5)))


def gelu_slope(value):
    bell = jnp.exp2(value * value * (-0.5 * LOG2E)) * (1.0 / math.sqrt(2.0 * math.pi))
    return 0.5 * (1.0 + lax.erf(value * math.sqrt(0.5))) + value * bell


def kernel_call(body, outs, ins, *, vmem, scratch=(), whole=(), scalars=(), cost=(0, 0, 0)):
    specs = [
        pl.BlockSpec(
            memory_space=pl.ANY if i in whole else pltpu.SMEM if i in scalars else pltpu.VMEM
        )
        for i in range(len(ins))
    ]
    return pl.pallas_call(
        body,
        out_shape=[jax.ShapeDtypeStruct(shape, kind) for shape, kind in outs],
        in_specs=specs,
        out_specs=[pl.BlockSpec(memory_space=pltpu.VMEM)] * len(outs),
        scratch_shapes=list(scratch),
        compiler_params=pltpu.CompilerParams(vmem_limit_bytes=vmem * 2**20),
        cost_estimate=pl.CostEstimate(flops=cost[0], bytes_accessed=cost[1], transcendentals=cost[2]),
    )(*ins)


def doubled(rows, columns, feature):
    wide, thin = iota((rows, columns), 0), iota((rows, columns), 1)
    source = (wide // (2 * feature)) * feature + wide % feature
    return ones_where(source == thin)


def bounds(doc_lengths, row):
    starts, ends, at = [], [], jnp.int32(0)
    for d in range(doc_lengths.shape[1]):
        starts.append(at)
        at = at + doc_lengths[row, d]
        ends.append(at)
    return starts, ends


def in_doc(doc_lengths, row, runs, length, shape, token_dim):
    starts, ends = bounds(doc_lengths, row)
    parts = []
    part_shape = list(shape)
    part_shape[token_dim] = length
    number = iota(tuple(part_shape), 1 - token_dim)
    first = jnp.zeros(tuple(part_shape), i32)
    last = first
    for d, (start, end) in enumerate(zip(starts, ends)):
        first = jnp.where(number == d, start, first)
        last = jnp.where(number == d, end, last)
    for run in runs:
        position = iota(tuple(part_shape), token_dim) + run
        parts.append(jnp.where((position >= first) & (position < last), 1.0, 0.0))
    return jnp.concatenate(parts, axis=token_dim)


def side_weights_body(
    s_query, s_key, s_value, s_out, s_inner, gate, gain_in, gain_mid, dup, dup_t, tall_t, columns, query_t, lines
):
    side, hidden = s_inner.shape
    feature = side // SHEADS
    dup[...] = nn(s_key[...], ones_where(iota(dup.shape, 0) == iota(dup.shape, 1))).astype(bf16)
    query_t[...] = nt(eye(side), s_query[...]).astype(bf16)
    spread_t = doubled(2 * side, side, feature)
    for i, weight in enumerate((s_query, s_key, s_value)):
        dup_t[2 * side * i : 2 * side * (i + 1)] = nt(spread_t, weight[...]).astype(bf16)
    tall_t[0:side] = nt(eye(side), s_out[...]).astype(bf16)
    tall_t[side : side + hidden] = nt(eye(hidden), s_inner[...]).astype(bf16)
    lines[...] = jnp.zeros(lines.shape, f32)
    for i, line in enumerate((gate, gain_in, gain_mid)):
        lines[i : i + 1, 0:side] = line[...].reshape(1, side)
    columns[...] = lines[...].T[0:side]


def prepare_body(
    doc_lengths, w_value, norm_in, norm_mid, value_t, gains, key_doc, query_doc, side_key_doc, side_query_doc
):
    value_t[...] = nt(eye(w_value.shape[0]), w_value[...]).astype(bf16)
    for i, line in enumerate((norm_in, norm_mid)):
        gains[i : i + 1] = line[...].astype(f32).reshape(1, line.shape[0])
    keys, tokens = key_doc.shape[0], query_doc.shape[0]
    span = tokens // 2
    place, half = lax.axis_index("blk"), lax.axis_size("blk") // 2
    row = place // half
    own, mate = place * span, (place ^ 1) * span
    far, far_mate = (place ^ half) * span, (place ^ half ^ 1) * span
    found = in_doc(doc_lengths, row, (own, mate, far, far_mate), span, (keys, 128), 0)
    key_doc[...] = (found - 1.0).astype(bf16)
    mine = jnp.concatenate([found[0:span], found[tokens : tokens + span]], axis=0)
    query_doc[...] = (mine * FAR).astype(bf16)
    mates = jnp.concatenate([found[span:tokens], found[tokens + span : keys]], axis=0)
    spare = SPARE
    low = iota((keys, 128), 1) < spare
    ordered = pltpu.roll(jnp.concatenate([mine, mates], axis=0), spare, 1)
    side_key_doc[...] = jnp.where(low, 0.0, ordered - 1.0).astype(bf16)
    side_query_doc[...] = (in_doc(doc_lengths, row, (own, far), span, (16, tokens), 1) * FAR).astype(bf16)


def project(tokens, gain, w_query, w_key, value_t, scale, queries):
    normed = norm_lanes(tokens.astype(f32), gain).astype(bf16)
    query = (nn(normed[0:queries], w_query[...]) * scale).astype(bf16)
    return query, nn(normed, w_key[...]).astype(bf16), nt(value_t[...], normed).astype(bf16)


def padded(value_t, head):
    ones = jnp.ones((16, value_t.shape[1]), bf16)
    pieces = []
    for at in range(0, value_t.shape[0], head):
        pieces += [value_t[at : at + head], ones]
    return jnp.concatenate(pieces, axis=0)


def pair_lanes(j):
    return pl.ds(pl.multiple_of(j * 128, 128), 128)


def pair_sums(j, queries, query_doc, keys, key_doc, values, shifted=False):
    width = queries[0].shape[1]
    head = width // HEADS
    stride = values[0].shape[0] // HEADS
    lanes = pair_lanes(j)
    key = jnp.concatenate([ref[:, lanes] for ref in keys], axis=0)
    key = jnp.concatenate([key, key_doc], axis=1)
    query = jnp.concatenate([ref[:, lanes] for ref in queries], axis=0)
    rows = pl.ds(pl.multiple_of(j * 2 * stride, 16), 2 * stride)
    value = jnp.concatenate([ref[rows, :] for ref in values], axis=1)
    lane = iota((1, 128), 1) // head
    masked = [jnp.concatenate([query * ones_where(lane == i), query_doc], axis=1) for i in range(2)]
    count = query.shape[0]

    scores = nt(key, jnp.concatenate(masked, axis=0))
    if shifted:
        scores = scores - jnp.max(scores, axis=0, keepdims=True)
    both = nn(value, jnp.exp2(scores).astype(bf16))
    return [both[i * stride : i * stride + head + 8, i * count : (i + 1) * count] for i in range(2)]


def first_body(own, mate, gains, w_query, w_key, value_t, key_doc, query_doc, query, key, value, part):
    _, span, width = own.shape
    head = width // HEADS
    row = lax.axis_index("blk") // (lax.axis_size("blk") // 2)
    tokens = jnp.concatenate([own[row], mate[row]], axis=0)
    query[...], key[...], value_new = project(
        tokens, gains[0:1], w_query, w_key, value_t, LOG2E * head**-0.5, span
    )
    value[...] = padded(value_new, head)

    def pair(j, carry):
        sums = pair_sums(j, [query], query_doc[0:span], [key], key_doc[0 : 2 * span], [value])
        part[j] = jnp.concatenate(sums, axis=0)
        return carry

    lax.fori_loop(0, HEADS // 2, pair, 0, unroll=6)


def out_of_range(totals):
    lowest, highest = jnp.min(totals), jnp.max(totals)
    return jnp.logical_not((lowest > LOW_TOTAL) & (highest < HIGH_TOTAL))


def second_body(
    far,
    far_mate,
    gains,
    w_query,
    w_key,
    value_t,
    key_doc,
    query_doc,
    query_a,
    key_a,
    value_a,
    part_a,
    attended,
    query,
    key,
    value,
    totals,
):
    span, width = far.shape
    head = width // HEADS
    tokens = jnp.concatenate([far[...], far_mate[...]], axis=0)
    query[...], key[...], value_new = project(
        tokens, gains[0:1], w_query, w_key, value_t, LOG2E * head**-0.5, span
    )
    value[...] = padded(value_new, head)
    keys, values, queries = [key_a, key], [value_a, value], [query_a, query]

    def finish(j, sums):
        results = []
        for i, summed in enumerate(sums):
            totals[pl.ds(pl.multiple_of((2 * j + i) * 8, 8), 8), :] = summed[head : head + 8]
            results.append(summed[0:head] * (1.0 / summed[head : head + 1]))
        attended[:, pair_lanes(j)] = jnp.concatenate(results, axis=0).T.astype(bf16)

    def pair(j, carry):
        old = pair_sums(j, [query_a], query_doc[0:span], [key], key_doc[2 * span : 4 * span], [value])
        new = pair_sums(j, [query], query_doc[span : 2 * span], keys, key_doc[...], values)
        sums = []
        for i in range(2):
            rows = slice(i * (head + 8), (i + 1) * (head + 8))
            sums.append(jnp.concatenate([old[i] + part_a[j, rows], new[i]], axis=1))
        finish(j, sums)
        return carry

    lax.fori_loop(0, HEADS // 2, pair, 0, unroll=6)

    @pl.when(out_of_range(totals[...]))
    def _():
        def again(j, carry):
            finish(j, pair_sums(j, queries, query_doc[...], keys, key_doc[...], values, shifted=True))
            return carry

        lax.fori_loop(0, HEADS // 2, again, 0)


def dense_body(
    own, far, attended, gains, w_out, w_inner, w_outer, down_w, columns, state, side_far, out_own, out_far, sn_rows, sn_t, mixed_t, lead_t
):
    _, span, width = own.shape
    row = lax.axis_index("blk") // (lax.axis_size("blk") // 2)
    tokens = jnp.concatenate([own[row], far[...]], axis=0)
    after = tokens.astype(f32) + nn(attended[...], w_out[...])
    middle = norm_lanes(after, gains[1:2]).astype(bf16)
    result = after
    for at in range(0, w_inner.shape[1], width):
        act = gelu(nn(middle, w_inner[:, at : at + width])).astype(bf16)
        result = result + nn(act, w_outer[at : at + width, :])
    out = result.astype(bf16)
    out_own[...] = out[0:span]
    out_far[...] = out[span : 2 * span]

    side = state.shape[1]
    down_t = nt(down_w[...], out)
    state_t = jnp.concatenate([state[row], side_far[0:side]], axis=1).astype(f32)
    gate_open = jax.nn.sigmoid(columns[:, 0:1])
    mixed = gate_open * down_t + (1.0 - gate_open) * state_t
    normed = (
        mixed * lax.rsqrt(jnp.mean(mixed * mixed, axis=0, keepdims=True) + EPS) * columns[:, 1:2]
    )
    mixed_t[...] = mixed
    lead_t[...] = down_t - state_t
    sn_t[...] = normed.astype(bf16)
    sn_rows[...] = normed.T.astype(bf16)


def outer_rows(left, right):
    return jnp.concatenate([left[f : f + 1] * right for f in range(left.shape[0])], axis=0)


def inner_rows(left, products):
    count = left.shape[0]
    total = left[0:1] * products[0:count]
    for f in range(1, count):
        total = total + left[f : f + 1] * products[f * count : (f + 1) * count]
    return total


def two_parts(value):
    high = value.astype(bf16).astype(f32)
    return [high, value - high]


def side_body(
    sn_own,
    sn_mate,
    mixed_t,
    cot,
    side_far,
    dup,
    dup_t,
    tall_t,
    s_outer_t,
    s_out,
    s_inner,
    columns,
    key_doc,
    query_doc,
    thin_query,
    dkv_own,
    dkv_mate,
    dmid_t,
    attn_t,
    inverse,
    moments,
    mid_t,
    inner_t,
    normed_t,
    dinner_t,
    dnormed_t,
    dattn_t,
    weights,
    keys,
    key_t,
    value_t,
    query_t,
    query_s,
    totals,
    back_rows,
    dkv_t,
):
    tokens, side = sn_own.shape
    feature = side // SHEADS
    hidden = s_inner.shape[1]
    wide = 2 * side
    row = lax.axis_index("blk") // (lax.axis_size("blk") // 2)
    scale = feature**-0.5

    sn = jnp.concatenate([sn_own[...], sn_mate[...]], axis=0)
    keys[...] = nn(sn, dup[...]).astype(bf16) + key_doc[...]
    key_t[...] = nt(dup_t[wide : 2 * wide], sn).astype(bf16)
    second = iota((wide, 2 * tokens), 0) % (2 * feature) >= feature
    value_t[...] = jnp.where(second, 1.0, nt(dup_t[2 * wide : 3 * wide], sn)).astype(bf16)
    query = nt(dup_t[0:wide], sn_own[...]).astype(bf16)
    query_t[...] = query
    query_s[0:side] = nt(thin_query[...], sn_own[...]).astype(bf16)
    query_s[side : side + 16] = query_doc[...]
    query_s[side + 16 :] = jnp.zeros((128 - side - 16, tokens), bf16)
    owner = iota((128, 1), 0) // feature

    def head_rows(h, count):
        return pl.ds(pl.multiple_of(h * count, count), count)

    def attend(shifted, size):
        def group(j, carry):
            for i in range(size):
                h = size * j + i
                rows, eight = head_rows(h, 16), head_rows(h, 8)
                mine = ones_where((owner == h) | (owner >= SHEADS))
                scores = nn(keys[...], query_s[...] * mine) * (scale * LOG2E)
                if shifted:
                    scores = scores - jnp.max(scores, axis=0, keepdims=True)
                weight = jnp.exp2(scores).astype(bf16)
                weights[h] = weight.T
                value, key = value_t[rows, :], key_t[rows, :]
                products = outer_rows(value[0:feature].astype(f32), key[0:feature].astype(f32))
                products = jnp.concatenate(two_parts(products), axis=0).astype(bf16)
                summed = nn(jnp.concatenate([value, key, products], axis=0), weight)
                total = summed[feature : 2 * feature]
                totals[eight, :] = total
                invert = 1.0 / total
                inverse[eight, :] = invert
                attn_t[eight, :] = summed[0:feature] * invert
                at = 4 * feature + feature * feature
                moments[h] = jnp.concatenate(
                    [summed[2 * feature : 4 * feature], summed[4 * feature : at] + summed[at:]], axis=0
                )
            return carry

        lax.fori_loop(0, SHEADS // size, group, 0)

    attend(False, SHEADS)

    @pl.when(out_of_range(totals[...]))
    def _():
        attend(True, 2)

    attn = attn_t[...]
    attn_low = attn.astype(bf16)
    mid = mixed_t[...] + nn(tall_t[0:side], attn_low)
    mid_scale = lax.rsqrt(jnp.mean(mid * mid, axis=0, keepdims=True) + EPS)
    gain = columns[:, 2:3]
    unit = mid * mid_scale
    normed = (unit * gain).astype(bf16)
    inner = nn(tall_t[side : side + hidden], normed)
    dy_low = jnp.concatenate([cot[row], side_far[side : 2 * side]], axis=1)
    dinner = (gelu_slope(inner) * tn(s_outer_t[...], dy_low)).astype(bf16)
    dnormed = nn(s_inner[...], dinner)
    scaled = dnormed * gain
    dmid = dy_low.astype(f32) + mid_scale * (
        scaled - unit * jnp.mean(scaled * unit, axis=0, keepdims=True)
    )
    dmid_t[...] = dmid
    dattn = nn(s_out[...], dmid.astype(bf16)).astype(bf16).astype(f32)
    mid_t[...] = mid
    inner_t[...] = inner
    normed_t[...] = normed
    dinner_t[...] = dinner
    dnormed_t[...] = dnormed
    dattn_t[...] = dattn

    for h in range(SHEADS):
        eight = slice(h * feature, (h + 1) * feature)
        invert = inverse[eight, :]
        term = jnp.sum(dattn[eight] * attn[eight], axis=0, keepdims=True)
        query = query_t[2 * h * feature : 2 * (h + 1) * feature].astype(f32)[0:feature]
        share = dattn[eight] * invert
        back_rows[h] = jnp.concatenate(
            two_parts(share) + two_parts(term * invert * query) + two_parts(outer_rows(share, query)), axis=0
        ).astype(bf16)

    for h in range(SHEADS):
        eight = slice(h * feature, (h + 1) * feature)
        summed = nn(back_rows[h], weights[h])
        dkv_t[side + h * feature : side + (h + 1) * feature] = (
            summed[0:feature] + summed[feature : 2 * feature]
        )
        value = value_t[2 * h * feature : 2 * (h + 1) * feature].astype(f32)[0:feature]
        at = 4 * feature + feature * feature
        raw = inner_rows(value, summed[4 * feature : at] + summed[at:])
        raw = raw - (summed[2 * feature : 3 * feature] + summed[3 * feature : 4 * feature])
        dkv_t[eight] = raw * scale
    dkv_own[...] = dkv_t[:, 0:tokens]
    dkv_mate[...] = dkv_t[:, tokens : 2 * tokens].astype(bf16)


def aside_body(
    attn_t,
    inverse,
    moments,
    mid_t,
    inner_t,
    normed_t,
    dinner_t,
    dnormed_t,
    dattn_t,
    dmid_t,
    cot,
    side_far,
    s_outer_t,
    out_own,
    out_far,
    dquery,
    early,
):
    side, tokens = mid_t.shape
    span = tokens // 2
    feature = side // SHEADS
    hidden = inner_t.shape[0]
    row = lax.axis_index("blk") // (lax.axis_size("blk") // 2)
    mid = mid_t[...]
    act = gelu(inner_t[...]).astype(bf16)
    out = (mid + nn(s_outer_t[...], act)).astype(bf16)
    out_own[...] = out[:, 0:span]
    out_far[...] = out[:, span : 2 * span]
    dy_low = jnp.concatenate([cot[row], side_far[side : 2 * side]], axis=1)
    early[:, 0:hidden] = nt(normed_t[...], dinner_t[...])
    early[:, hidden : 2 * hidden] = nt(dy_low, act)
    unit = mid * lax.rsqrt(jnp.mean(mid * mid, axis=0, keepdims=True) + EPS)
    grad_gain = jnp.sum(dnormed_t[...] * unit, axis=1, keepdims=True)
    last = nt(attn_t[...].astype(bf16), dmid_t[...].astype(bf16))
    last = jnp.concatenate([last, jnp.zeros((side, 128 - side), f32)], axis=1)
    early[:, 2 * hidden : 2 * hidden + 128] = jnp.where(
        iota((side, 128), 1) == side, grad_gain, last
    )
    for h in range(SHEADS):
        eight = slice(h * feature, (h + 1) * feature)
        dattn = dattn_t[eight, :]
        term = jnp.sum(dattn * attn_t[eight, :], axis=0, keepdims=True)
        moment = moments[h]
        raw = inner_rows(dattn, moment[2 * feature :]) - term * moment[0:feature]
        dquery[eight, :] = raw * inverse[eight, :] * feature**-0.5


def last_body(
    dquery,
    dkv_own,
    dkv_back,
    sn_t,
    dmid_t,
    mixed_t,
    lead_t,
    out_own,
    out_far,
    s_query,
    s_key,
    s_value,
    columns,
    early,
    side_out_far,
    state_own,
    far,
    keep,
    send,
    pack,
):
    side, tokens = sn_t.shape
    span = tokens // 2
    width = out_own.shape[1]
    dq = dquery[...].astype(bf16)
    dkv = (dkv_own[...].astype(bf16).astype(f32) + dkv_back[...].astype(f32)).astype(bf16)
    dk, dv = dkv[0:side], dkv[side : 2 * side]
    sn = sn_t[...]
    dnormed = nn(s_query[...], dq) + nn(s_key[...], dk) + nn(s_value[...], dv)
    mixed = mixed_t[...]
    mixed_scale = lax.rsqrt(jnp.mean(mixed * mixed, axis=0, keepdims=True) + EPS)
    unit = mixed * mixed_scale
    scaled = dnormed * columns[:, 1:2]
    dmixed = dmid_t[...] + mixed_scale * (
        scaled - unit * jnp.mean(scaled * unit, axis=0, keepdims=True)
    )
    gate_open = jax.nn.sigmoid(columns[:, 0:1])
    grad_gain = jnp.sum(dnormed * unit, axis=1, keepdims=True)
    grad_gate = jnp.sum(dmixed * lead_t[...], axis=1, keepdims=True) * gate_open * (1.0 - gate_open)
    state = (1.0 - gate_open) * dmixed
    state_own[...] = state[:, 0:span]
    far[0:side] = side_out_far[...]
    far[side : 2 * side] = state[:, span:tokens].astype(bf16)
    ddown = (gate_open * dmixed).astype(bf16)
    pack[:, 0:width] = nn(ddown[:, 0:span], out_own[...]) + nn(ddown[:, span:tokens], out_far[...])
    at = width
    blank = jnp.zeros((side, 128 - side), f32)
    for grad in (dq, dk, dv):
        pack[:, at : at + 128] = jnp.concatenate([nt(sn, grad), blank], axis=1)
        at += 128
    lane = iota((side, 128), 1)
    inner = early.shape[1] - 128
    vectors = early[:, inner : inner + 128]
    vectors = jnp.where(lane == side + 1, grad_gain, vectors)
    pack[:, at : at + 128] = jnp.where(lane == side + 2, grad_gate, vectors)
    pack[:, at + 128 : at + 128 + inner] = early[:, 0:inner]
    size = keep.shape[1]
    core = lax.axis_index("blk") % 2
    keep[...] = pack[:, pl.ds(pl.multiple_of(core * size, 128), size)].astype(bf16)
    send[...] = pack[:, pl.ds(pl.multiple_of((1 - core) * size, 128), size)].astype(bf16)


def quarter_index():
    return (lax.axis_index("blk") // 2) % 2 + 2 * (lax.axis_index("dp") % 2)


def spread_body(*refs):
    pieces, refs = refs[0:8], refs[8:]
    (
        grad_down,
        grad_gate,
        gain_in,
        grad_query,
        grad_key,
        grad_value,
        grad_out,
        gain_mid,
        grad_inner,
        grad_outer,
        pack,
    ) = refs
    side, width = grad_down.shape
    hidden = grad_inner.shape[1]
    size = pieces[0].shape[1]
    core, quarter = lax.axis_index("blk") % 2, quarter_index()
    for i, piece in enumerate(pieces):
        at = ((core ^ (i // 4)) * 4 + (quarter ^ (i % 4))) * size
        pack[:, pl.ds(pl.multiple_of(at, 128), size)] = piece[...].astype(f32)
    whole = pack[...]
    grad_down[...] = whole[:, 0:width]
    at = width
    for target in (grad_query, grad_key, grad_value):
        target[...] = whole[:, at : at + side]
        at += 128
    block = whole[:, at : at + 128]
    grad_out[...] = block[:, 0:side]
    rows = block.T
    gain_mid[...] = rows[side : side + 1]
    gain_in[...] = rows[side + 1 : side + 2]
    grad_gate[...] = rows[side + 2 : side + 3]
    at += 128
    grad_inner[...] = whole[:, at : at + hidden]
    grad_outer[...] = whole[:, at + hidden : at + 2 * hidden]


def per_device(
    hidden,
    side_state,
    doc_lengths,
    norm_in,
    w_query,
    w_key,
    w_value,
    w_out,
    norm_mid,
    w_inner,
    w_outer,
    w_down,
    gate,
    side_norm_in,
    s_query,
    s_key,
    s_value,
    s_out,
    side_norm_mid,
    s_inner,
    s_outer,
    cotangent,
):
    span, rows, width = hidden.shape
    side = side_state.shape[2]
    ff = w_inner.shape[1]
    sff = s_inner.shape[1]
    tokens = 2 * span
    feature = side // SHEADS
    blk_size, dp_size = lax.axis_size("blk"), lax.axis_size("dp")
    half = blk_size // 2
    place = lax.axis_index("blk")
    row = place // half

    def swap(value, axis, size, hop):
        return lax.ppermute(value, axis, [(i, i ^ hop) for i in range(size)])

    def across(value):
        return swap(value, "blk", blk_size, half)

    def beside(value):
        return swap(value, "blk", blk_size, 1)

    hidden = jnp.transpose(hidden, (1, 0, 2))
    hidden_far = across(lax.dynamic_index_in_dim(hidden, 1 - row, 0, keepdims=False))
    hidden_mate = beside(hidden)
    state, cot = (jnp.transpose(array, (1, 2, 0)) for array in (side_state, cotangent))
    side_far = across(
        lax.dynamic_index_in_dim(jnp.concatenate([state, cot], axis=1), 1 - row, 0, keepdims=False)
    )
    down_w, s_outer_t = w_down.T, s_outer.T

    value_t, gains, key_doc, query_doc, side_key_doc, side_query_doc = kernel_call(
        prepare_body,
        [
            ((width, width), bf16),
            ((2, width), f32),
            ((2 * tokens, 128), bf16),
            ((tokens, 128), bf16),
            ((2 * tokens, 128), bf16),
            ((16, tokens), bf16),
        ],
        [doc_lengths, w_value, norm_in, norm_mid],
        vmem=16,
        scalars=(0,),
        cost=(1000, 1000, 0),
    )
    head = width // HEADS
    stride = head + 16
    projections = (gains, w_query, w_key, value_t, key_doc, query_doc)

    def state_of(queries, keys, columns):
        return [
            ((queries, width), bf16),
            ((keys, width), bf16),
            ((HEADS * stride, keys), bf16),
            ((HEADS // 2, 2 * (head + 8), columns), f32),
        ]

    state_a = kernel_call(
        first_body,
        state_of(span, tokens, span),
        [hidden, hidden_mate, *projections],
        vmem=24,
        cost=(1000, 1000, 0),
    )
    small = (s_query, s_key, s_value, s_out, s_inner, gate, side_norm_in, side_norm_mid)
    hidden_far, small, *state_a = lax.optimization_barrier((hidden_far, small, *state_a))
    dup, dup_t, tall_t, columns, s_query_t = kernel_call(
        side_weights_body,
        [
            ((side, 128), bf16),
            ((6 * side, side), bf16),
            ((side + sff, side), bf16),
            ((side, 128), f32),
            ((side, side), bf16),
        ],
        small,
        vmem=8,
        scratch=[pltpu.VMEM((128, 128), f32)],
        cost=(1000, 1000, 0),
    )
    (attended,) = kernel_call(
        second_body,
        [((tokens, width), bf16)],
        [hidden_far, beside(hidden_far), *projections, *state_a],
        vmem=30,
        scratch=[
            pltpu.VMEM((span, width), bf16),
            pltpu.VMEM((tokens, width), bf16),
            pltpu.VMEM((HEADS * stride, tokens), bf16),
            pltpu.VMEM((HEADS * 8, tokens), f32),
        ],
        cost=(8 * 10**9, 8 * 10**6, 0),
    )
    side_far, attended = lax.optimization_barrier((side_far, attended))
    out_own, out_far, sn_rows, sn_t, mixed_t, lead_t = kernel_call(
        dense_body,
        [
            ((span, width), bf16),
            ((span, width), bf16),
            ((tokens, side), bf16),
            ((side, tokens), bf16),
            ((side, tokens), f32),
            ((side, tokens), f32),
        ],
        [
            hidden,
            hidden_far,
            attended,
            gains,
            w_out,
            w_inner,
            w_outer,
            down_w,
            columns,
            state,
            side_far,
        ],
        vmem=28,
        cost=(10 * 10**9, 14 * 10**6, 0),
    )
    sn_mate = beside(sn_rows)
    out_back = across(out_far)
    dkv_own, dkv_mate, dmid_t, *carried = kernel_call(
        side_body,
        [
            ((2 * side, tokens), f32),
            ((2 * side, tokens), bf16),
            ((side, tokens), f32),
            ((side, tokens), f32),
            ((side, tokens), f32),
            ((SHEADS, feature * (feature + 2), tokens), f32),
            ((side, tokens), f32),
            ((sff, tokens), f32),
            ((side, tokens), bf16),
            ((sff, tokens), bf16),
            ((side, tokens), f32),
            ((side, tokens), f32),
        ],
        [
            sn_rows,
            sn_mate,
            mixed_t,
            cot,
            side_far,
            dup,
            dup_t,
            tall_t,
            s_outer_t,
            s_out,
            s_inner,
            columns,
            side_key_doc,
            side_query_doc,
            s_query_t,
        ],
        vmem=36,
        scratch=[
            pltpu.VMEM((SHEADS, tokens, 2 * tokens), bf16),
            pltpu.VMEM((2 * tokens, 128), bf16),
            pltpu.VMEM((2 * side, 2 * tokens), bf16),
            pltpu.VMEM((2 * side, 2 * tokens), bf16),
            pltpu.VMEM((2 * side, tokens), bf16),
            pltpu.VMEM((128, tokens), bf16),
            pltpu.VMEM((side, tokens), f32),
            pltpu.VMEM((SHEADS, feature * (2 * feature + 4), tokens), bf16),
            pltpu.VMEM((2 * side, 2 * tokens), f32),
        ],
        cost=(30 * 10**9, 3 * 10**6, 0),
    )
    dkv_back = beside(dkv_mate)
    side_own, side_back, dquery, early = kernel_call(
        aside_body,
        [
            ((side, span), bf16),
            ((side, span), bf16),
            ((side, tokens), f32),
            ((side, 2 * sff + 128), f32),
        ],
        [*carried, dmid_t, cot, side_far, s_outer_t],
        vmem=12,
        cost=(10**9, 6 * 10**6, 0),
    )
    dkv_back, out_back = lax.optimization_barrier((dkv_back, out_back))
    packed = width + 4 * 128 + 2 * sff
    grad_own, far, keep, send = kernel_call(
        last_body,
        [
            ((side, span), f32),
            ((2 * side, span), bf16),
            ((side, packed // 2), bf16),
            ((side, packed // 2), bf16),
        ],
        [
            dquery,
            dkv_own,
            dkv_back,
            sn_t,
            dmid_t,
            mixed_t,
            lead_t,
            out_own,
            out_far,
            s_query,
            s_key,
            s_value,
            columns,
            early,
            side_back,
        ],
        vmem=16,
        scratch=[pltpu.VMEM((side, packed), f32)],
        cost=(10**9, 3 * 10**6, 0),
    )

    def add(*terms):
        total = terms[0].astype(f32)
        for term in terms[1:]:
            total = total + term.astype(f32)
        return total.astype(bf16)

    quarter = packed // 8
    mine = quarter_index()
    devices = dp_size * blk_size

    def between(value, chip):
        mask = 2 * (chip % 2) + blk_size * (chip // 2)
        return lax.ppermute(value, ("dp", "blk"), [(i, i ^ mask) for i in range(devices)])

    def part(value, index):
        return lax.dynamic_slice_in_dim(value, index * quarter, quarter, 1)

    total = add(keep, beside(send))
    total = add(part(total, mine), *[between(part(total, mine ^ chip), chip) for chip in (1, 2, 3)])
    total, far = lax.optimization_barrier((total, far))
    hop = 2
    while hop < dp_size:
        total = add(total, swap(total, "dp", dp_size, hop))
        hop *= 2
    pieces = [total] + [between(total, chip) for chip in (1, 2, 3)]
    pieces += [beside(piece) for piece in pieces]
    vector = ((1, side), f32)
    square = ((side, side), f32)
    grads = kernel_call(
        spread_body,
        [
            ((side, width), f32),
            vector,
            vector,
            square,
            square,
            square,
            square,
            vector,
            ((side, sff), f32),
            ((side, sff), f32),
        ],
        pieces,
        vmem=16,
        scratch=[pltpu.VMEM((side, packed), f32)],
        cost=(0, 2 * 10**6, 0),
    )
    grads = [grad.reshape(side) if grad.shape[0] == 1 else grad for grad in grads]
    grads[0], grads[-1] = grads[0].T, grads[-1].T

    def both_rows(own, back):
        first = jnp.where(row == 0, own, back)
        second = jnp.where(row == 0, back, own)
        return jnp.stack([first, second])

    far = across(far)
    return (
        jnp.transpose(both_rows(out_own, out_back), (1, 0, 2)),
        jnp.transpose(both_rows(side_own, far[0:side]), (2, 0, 1)),
        jnp.transpose(both_rows(grad_own, far[side : 2 * side].astype(f32)), (2, 0, 1)),
        *grads,
    )


def solution(mesh):
    split = P("blk", "dp", None)
    return jax.shard_map(
        per_device,
        mesh=mesh,
        in_specs=(split, split, P("dp", None)) + (P(),) * 18 + (split,),
        out_specs=(split,) * 3 + (P(),) * 10,
        check_vma=False,
    )
```

```python
import math

import jax
import jax.numpy as jnp
from jax import lax
from jax.experimental import pallas as pl
from jax.experimental.pallas import tpu as pltpu
from jax.sharding import PartitionSpec as P

HEADS = 12
SHEADS = 12
SPARE = 96
EPS = 1e-06
LOG2E = math.log2(math.e)
FAR = 2.0**100
LOW_TOTAL, HIGH_TOTAL = 2.0**-60, 2.0**60

f32, bf16, i32 = jnp.float32, jnp.bfloat16, jnp.int32


def nn(left, right):
    return jnp.dot(left, right, preferred_element_type=f32)


def nt(left, right):
    return lax.dot_general(left, right, (((1,), (1,)), ((), ())), preferred_element_type=f32)


def tn(left, right):
    return lax.dot_general(left, right, (((0,), (0,)), ((), ())), preferred_element_type=f32)


def ones_where(condition):
    return jnp.where(condition, 1.0, 0.0).astype(bf16)


def iota(shape, dim):
    return lax.broadcasted_iota(i32, shape, dim)


def eye(size):
    return ones_where(iota((size, size), 0) == iota((size, size), 1))


def norm_lanes(value, gain):
    return value * lax.rsqrt(jnp.mean(value * value, axis=1, keepdims=True) + EPS) * gain


def gelu(value):
    return 0.5 * value * (1.0 + lax.erf(value * math.sqrt(0.5)))


def gelu_slope(value):
    bell = jnp.exp2(value * value * (-0.5 * LOG2E)) * (1.0 / math.sqrt(2.0 * math.pi))
    return 0.5 * (1.0 + lax.erf(value * math.sqrt(0.5))) + value * bell


def kernel_call(body, outs, ins, *, vmem, scratch=(), whole=(), scalars=(), cost=(0, 0, 0)):
    specs = [
        pl.BlockSpec(
            memory_space=pl.ANY if i in whole else pltpu.SMEM if i in scalars else pltpu.VMEM
        )
        for i in range(len(ins))
    ]
    return pl.pallas_call(
        body,
        out_shape=[jax.ShapeDtypeStruct(shape, kind) for shape, kind in outs],
        in_specs=specs,
        out_specs=[pl.BlockSpec(memory_space=pltpu.VMEM)] * len(outs),
        scratch_shapes=list(scratch),
        compiler_params=pltpu.CompilerParams(vmem_limit_bytes=vmem * 2**20),
        cost_estimate=pl.CostEstimate(flops=cost[0], bytes_accessed=cost[1], transcendentals=cost[2]),
    )(*ins)


def doubled(rows, columns, feature):
    wide, thin = iota((rows, columns), 0), iota((rows, columns), 1)
    source = (wide // (2 * feature)) * feature + wide % feature
    return ones_where(source == thin)


def bounds(doc_lengths, row):
    starts, ends, at = [], [], jnp.int32(0)
    for d in range(doc_lengths.shape[1]):
        starts.append(at)
        at = at + doc_lengths[row, d]
        ends.append(at)
    return starts, ends


def in_doc(doc_lengths, row, runs, length, shape, token_dim):
    starts, ends = bounds(doc_lengths, row)
    parts = []
    part_shape = list(shape)
    part_shape[token_dim] = length
    number = iota(tuple(part_shape), 1 - token_dim)
    first = jnp.zeros(tuple(part_shape), i32)
    last = first
    for d, (start, end) in enumerate(zip(starts, ends)):
        first = jnp.where(number == d, start, first)
        last = jnp.where(number == d, end, last)
    for run in runs:
        position = iota(tuple(part_shape), token_dim) + run
        parts.append(jnp.where((position >= first) & (position < last), 1.0, 0.0))
    return jnp.concatenate(parts, axis=token_dim)


def side_weights_body(
    s_query, s_key, s_value, s_out, s_inner, gate, gain_in, gain_mid, dup, dup_t, tall_t, columns, query_t, lines
):
    side, hidden = s_inner.shape
    feature = side // SHEADS
    dup[...] = nn(s_key[...], ones_where(iota(dup.shape, 0) == iota(dup.shape, 1))).astype(bf16)
    query_t[...] = nt(eye(side), s_query[...]).astype(bf16)
    spread_t = doubled(2 * side, side, feature)
    for i, weight in enumerate((s_query, s_key, s_value)):
        dup_t[2 * side * i : 2 * side * (i + 1)] = nt(spread_t, weight[...]).astype(bf16)
    tall_t[0:side] = nt(eye(side), s_out[...]).astype(bf16)
    tall_t[side : side + hidden] = nt(eye(hidden), s_inner[...]).astype(bf16)
    lines[...] = jnp.zeros(lines.shape, f32)
    for i, line in enumerate((gate, gain_in, gain_mid)):
        lines[i : i + 1, 0:side] = line[...].reshape(1, side)
    columns[...] = lines[...].T[0:side]


def prepare_body(
    doc_lengths, w_value, norm_in, norm_mid, value_t, gains, key_doc, query_doc, side_key_doc, side_query_doc
):
    value_t[...] = nt(eye(w_value.shape[0]), w_value[...]).astype(bf16)
    for i, line in enumerate((norm_in, norm_mid)):
        gains[i : i + 1] = line[...].astype(f32).reshape(1, line.shape[0])
    keys, tokens = key_doc.shape[0], query_doc.shape[0]
    span = tokens // 2
    place, half = lax.axis_index("blk"), lax.axis_size("blk") // 2
    row = place // half
    own, mate = place * span, (place ^ 1) * span
    far, far_mate = (place ^ half) * span, (place ^ half ^ 1) * span
    found = in_doc(doc_lengths, row, (own, mate, far, far_mate), span, (keys, 128), 0)
    key_doc[...] = (found - 1.0).astype(bf16)
    mine = jnp.concatenate([found[0:span], found[tokens : tokens + span]], axis=0)
    query_doc[...] = (mine * FAR).astype(bf16)
    mates = jnp.concatenate([found[span:tokens], found[tokens + span : keys]], axis=0)
    spare = SPARE
    low = iota((keys, 128), 1) < spare
    ordered = pltpu.roll(jnp.concatenate([mine, mates], axis=0), spare, 1)
    side_key_doc[...] = jnp.where(low, 0.0, ordered - 1.0).astype(bf16)
    side_query_doc[...] = (in_doc(doc_lengths, row, (own, far), span, (16, tokens), 1) * FAR).astype(bf16)


def project(tokens, gain, w_query, w_key, value_t, queries):
    normed = norm_lanes(tokens.astype(f32), gain).astype(bf16)
    query = nn(normed[0:queries], w_query[...]).astype(bf16)
    return query, nn(normed, w_key[...]).astype(bf16), nt(value_t[...], normed).astype(bf16)


def padded(value_t, head):
    ones = jnp.ones((16, value_t.shape[1]), bf16)
    pieces = []
    for at in range(0, value_t.shape[0], head):
        pieces += [value_t[at : at + head], ones]
    return jnp.concatenate(pieces, axis=0)


def pair_lanes(j):
    return pl.ds(pl.multiple_of(j * 128, 128), 128)


def pair_sums(j, queries, query_doc, keys, key_doc, values, shifted=False):
    width = queries[0].shape[1]
    head = width // HEADS
    stride = values[0].shape[0] // HEADS
    lanes = pair_lanes(j)
    key = jnp.concatenate([ref[:, lanes] for ref in keys], axis=0)
    key = jnp.concatenate([key, key_doc], axis=1)
    query = jnp.concatenate([ref[:, lanes] for ref in queries], axis=0)
    rows = pl.ds(pl.multiple_of(j * 2 * stride, 16), 2 * stride)
    value = jnp.concatenate([ref[rows, :] for ref in values], axis=1)
    lane = iota((1, 128), 1) // head
    masked = [jnp.concatenate([query * ones_where(lane == i), query_doc], axis=1) for i in range(2)]
    count = query.shape[0]

    scores = nt(key, jnp.concatenate(masked, axis=0)) * (LOG2E * head**-0.5)
    if shifted:
        scores = scores - jnp.max(scores, axis=0, keepdims=True)
    both = nn(value, jnp.exp2(scores).astype(bf16))
    return [both[i * stride : i * stride + head + 8, i * count : (i + 1) * count] for i in range(2)]


def first_body(own, mate, gains, w_query, w_key, value_t, key_doc, query_doc, query, key, value, part):
    _, span, width = own.shape
    head = width // HEADS
    row = lax.axis_index("blk") // (lax.axis_size("blk") // 2)
    tokens = jnp.concatenate([own[row], mate[row]], axis=0)
    query[...], key[...], value_new = project(
        tokens, gains[0:1], w_query, w_key, value_t, span
    )
    value[...] = padded(value_new, head)

    def pair(j, carry):
        sums = pair_sums(j, [query], query_doc[0:span], [key], key_doc[0 : 2 * span], [value])
        part[j] = jnp.concatenate(sums, axis=0)
        return carry

    lax.fori_loop(0, HEADS // 2, pair, 0, unroll=6)


def out_of_range(totals):
    lowest, highest = jnp.min(totals), jnp.max(totals)
    return jnp.logical_not((lowest > LOW_TOTAL) & (highest < HIGH_TOTAL))


def second_body(
    far,
    far_mate,
    gains,
    w_query,
    w_key,
    value_t,
    key_doc,
    query_doc,
    query_a,
    key_a,
    value_a,
    part_a,
    attended,
    query,
    key,
    value,
    totals,
):
    span, width = far.shape
    head = width // HEADS
    tokens = jnp.concatenate([far[...], far_mate[...]], axis=0)
    query[...], key[...], value_new = project(
        tokens, gains[0:1], w_query, w_key, value_t, span
    )
    value[...] = padded(value_new, head)
    keys, values, queries = [key_a, key], [value_a, value], [query_a, query]

    def finish(j, sums):
        results = []
        for i, summed in enumerate(sums):
            totals[pl.ds(pl.multiple_of((2 * j + i) * 8, 8), 8), :] = summed[head : head + 8]
            results.append(summed[0:head] * (1.0 / summed[head : head + 1]))
        attended[:, pair_lanes(j)] = jnp.concatenate(results, axis=0).T.astype(bf16)

    def pair(j, carry):
        old = pair_sums(j, [query_a], query_doc[0:span], [key], key_doc[2 * span : 4 * span], [value])
        new = pair_sums(j, [query], query_doc[span : 2 * span], keys, key_doc[...], values)
        sums = []
        for i in range(2):
            rows = slice(i * (head + 8), (i + 1) * (head + 8))
            sums.append(jnp.concatenate([old[i] + part_a[j, rows], new[i]], axis=1))
        finish(j, sums)
        return carry

    lax.fori_loop(0, HEADS // 2, pair, 0, unroll=6)

    @pl.when(out_of_range(totals[...]))
    def _():
        def again(j, carry):
            finish(j, pair_sums(j, queries, query_doc[...], keys, key_doc[...], values, shifted=True))
            return carry

        lax.fori_loop(0, HEADS // 2, again, 0)


def dense_body(
    own, far, attended, gains, w_out, w_inner, w_outer, down_w, columns, state, side_far, out_own, out_far, sn_rows, sn_t, mixed_t, lead_t
):
    _, span, width = own.shape
    row = lax.axis_index("blk") // (lax.axis_size("blk") // 2)
    tokens = jnp.concatenate([own[row], far[...]], axis=0)
    after = tokens.astype(f32) + nn(attended[...], w_out[...])
    middle = norm_lanes(after, gains[1:2]).astype(bf16)
    result = after
    for at in range(0, w_inner.shape[1], width):
        act = gelu(nn(middle, w_inner[:, at : at + width])).astype(bf16)
        result = result + nn(act, w_outer[at : at + width, :])
    out = result.astype(bf16)
    out_own[...] = out[0:span]
    out_far[...] = out[span : 2 * span]

    side = state.shape[1]
    down_t = nt(down_w[...], out)
    state_t = jnp.concatenate([state[row], side_far[0:side]], axis=1).astype(f32)
    gate_open = jax.nn.sigmoid(columns[:, 0:1])
    mixed = gate_open * down_t + (1.0 - gate_open) * state_t
    normed = (
        mixed * lax.rsqrt(jnp.mean(mixed * mixed, axis=0, keepdims=True) + EPS) * columns[:, 1:2]
    )
    mixed_t[...] = mixed
    lead_t[...] = down_t - state_t
    sn_t[...] = normed.astype(bf16)
    sn_rows[...] = normed.T.astype(bf16)


def outer_rows(left, right):
    return jnp.concatenate([left[f : f + 1] * right for f in range(left.shape[0])], axis=0)


def inner_rows(left, products):
    count = left.shape[0]
    total = left[0:1] * products[0:count]
    for f in range(1, count):
        total = total + left[f : f + 1] * products[f * count : (f + 1) * count]
    return total


def two_parts(value):
    high = value.astype(bf16).astype(f32)
    return [high, value - high]


def side_body(
    sn_own,
    sn_mate,
    mixed_t,
    cot,
    side_far,
    dup,
    dup_t,
    tall_t,
    s_outer_t,
    s_out,
    s_inner,
    columns,
    key_doc,
    query_doc,
    thin_query,
    dkv_own,
    dkv_mate,
    dmid_t,
    attn_t,
    inverse,
    moments,
    mid_t,
    inner_t,
    normed_t,
    dinner_t,
    dnormed_t,
    dattn_t,
    weights,
    keys,
    key_t,
    value_t,
    query_t,
    query_s,
    totals,
    back_rows,
    dkv_t,
):
    tokens, side = sn_own.shape
    feature = side // SHEADS
    hidden = s_inner.shape[1]
    wide = 2 * side
    row = lax.axis_index("blk") // (lax.axis_size("blk") // 2)
    scale = feature**-0.5

    sn = jnp.concatenate([sn_own[...], sn_mate[...]], axis=0)
    keys[...] = nn(sn, dup[...]).astype(bf16) + key_doc[...]
    key_t[...] = nt(dup_t[wide : 2 * wide], sn).astype(bf16)
    second = iota((wide, 2 * tokens), 0) % (2 * feature) >= feature
    value_t[...] = jnp.where(second, 1.0, nt(dup_t[2 * wide : 3 * wide], sn)).astype(bf16)
    query = nt(dup_t[0:wide], sn_own[...]).astype(bf16)
    query_t[...] = query
    query_s[0:side] = nt(thin_query[...], sn_own[...]).astype(bf16)
    query_s[side : side + 16] = query_doc[...]
    query_s[side + 16 :] = jnp.zeros((128 - side - 16, tokens), bf16)
    owner = iota((128, 1), 0) // feature

    def head_rows(h, count):
        return pl.ds(pl.multiple_of(h * count, count), count)

    def attend(shifted, size):
        def group(j, carry):
            for i in range(size):
                h = size * j + i
                rows, eight = head_rows(h, 16), head_rows(h, 8)
                mine = ones_where((owner == h) | (owner >= SHEADS))
                scores = nn(keys[...], query_s[...] * mine) * (scale * LOG2E)
                if shifted:
                    scores = scores - jnp.max(scores, axis=0, keepdims=True)
                weight = jnp.exp2(scores).astype(bf16)
                weights[h] = weight.T
                value, key = value_t[rows, :], key_t[rows, :]
                products = outer_rows(value[0:feature].astype(f32), key[0:feature].astype(f32))
                products = jnp.concatenate(two_parts(products), axis=0).astype(bf16)
                summed = nn(jnp.concatenate([value, key, products], axis=0), weight)
                total = summed[feature : 2 * feature]
                totals[eight, :] = total
                invert = 1.0 / total
                inverse[eight, :] = invert
                attn_t[eight, :] = summed[0:feature] * invert
                at = 4 * feature + feature * feature
                moments[h] = jnp.concatenate(
                    [summed[2 * feature : 4 * feature], summed[4 * feature : at] + summed[at:]], axis=0
                )
            return carry

        lax.fori_loop(0, SHEADS // size, group, 0)

    attend(False, SHEADS)

    @pl.when(out_of_range(totals[...]))
    def _():
        attend(True, 2)

    attn = attn_t[...]
    attn_low = attn.astype(bf16)
    mid = mixed_t[...] + nn(tall_t[0:side], attn_low)
    mid_scale = lax.rsqrt(jnp.mean(mid * mid, axis=0, keepdims=True) + EPS)
    gain = columns[:, 2:3]
    unit = mid * mid_scale
    normed = (unit * gain).astype(bf16)
    inner = nn(tall_t[side : side + hidden], normed)
    dy_low = jnp.concatenate([cot[row], side_far[side : 2 * side]], axis=1)
    dinner = (gelu_slope(inner) * tn(s_outer_t[...], dy_low)).astype(bf16)
    dnormed = nn(s_inner[...], dinner)
    scaled = dnormed * gain
    dmid = dy_low.astype(f32) + mid_scale * (
        scaled - unit * jnp.mean(scaled * unit, axis=0, keepdims=True)
    )
    dmid_t[...] = dmid
    dattn = nn(s_out[...], dmid.astype(bf16)).astype(bf16).astype(f32)
    mid_t[...] = mid
    inner_t[...] = inner
    normed_t[...] = normed
    dinner_t[...] = dinner
    dnormed_t[...] = dnormed
    dattn_t[...] = dattn

    for h in range(SHEADS):
        eight = slice(h * feature, (h + 1) * feature)
        invert = inverse[eight, :]
        term = jnp.sum(dattn[eight] * attn[eight], axis=0, keepdims=True)
        query = query_t[2 * h * feature : 2 * (h + 1) * feature].astype(f32)[0:feature]
        share = dattn[eight] * invert
        back_rows[h] = jnp.concatenate(
            two_parts(share) + two_parts(term * invert * query) + two_parts(outer_rows(share, query)), axis=0
        ).astype(bf16)

    for h in range(SHEADS):
        eight = slice(h * feature, (h + 1) * feature)
        summed = nn(back_rows[h], weights[h])
        dkv_t[side + h * feature : side + (h + 1) * feature] = (
            summed[0:feature] + summed[feature : 2 * feature]
        )
        value = value_t[2 * h * feature : 2 * (h + 1) * feature].astype(f32)[0:feature]
        at = 4 * feature + feature * feature
        raw = inner_rows(value, summed[4 * feature : at] + summed[at:])
        raw = raw - (summed[2 * feature : 3 * feature] + summed[3 * feature : 4 * feature])
        dkv_t[eight] = raw * scale
    dkv_own[...] = dkv_t[:, 0:tokens]
    dkv_mate[...] = dkv_t[:, tokens : 2 * tokens].astype(bf16)


def aside_body(
    attn_t,
    inverse,
    moments,
    mid_t,
    inner_t,
    normed_t,
    dinner_t,
    dnormed_t,
    dattn_t,
    dmid_t,
    cot,
    side_far,
    s_outer_t,
    out_own,
    out_far,
    dquery,
    early,
):
    side, tokens = mid_t.shape
    span = tokens // 2
    feature = side // SHEADS
    hidden = inner_t.shape[0]
    row = lax.axis_index("blk") // (lax.axis_size("blk") // 2)
    mid = mid_t[...]
    act = gelu(inner_t[...]).astype(bf16)
    out = (mid + nn(s_outer_t[...], act)).astype(bf16)
    out_own[...] = out[:, 0:span]
    out_far[...] = out[:, span : 2 * span]
    dy_low = jnp.concatenate([cot[row], side_far[side : 2 * side]], axis=1)
    early[:, 0:hidden] = nt(normed_t[...], dinner_t[...])
    early[:, hidden : 2 * hidden] = nt(dy_low, act)
    unit = mid * lax.rsqrt(jnp.mean(mid * mid, axis=0, keepdims=True) + EPS)
    grad_gain = jnp.sum(dnormed_t[...] * unit, axis=1, keepdims=True)
    last = nt(attn_t[...].astype(bf16), dmid_t[...].astype(bf16))
    last = jnp.concatenate([last, jnp.zeros((side, 128 - side), f32)], axis=1)
    early[:, 2 * hidden : 2 * hidden + 128] = jnp.where(
        iota((side, 128), 1) == side, grad_gain, last
    )
    for h in range(SHEADS):
        eight = slice(h * feature, (h + 1) * feature)
        dattn = dattn_t[eight, :]
        term = jnp.sum(dattn * attn_t[eight, :], axis=0, keepdims=True)
        moment = moments[h]
        raw = inner_rows(dattn, moment[2 * feature :]) - term * moment[0:feature]
        dquery[eight, :] = raw * inverse[eight, :] * feature**-0.5


def last_body(
    dquery,
    dkv_own,
    dkv_back,
    sn_t,
    dmid_t,
    mixed_t,
    lead_t,
    out_own,
    out_far,
    s_query,
    s_key,
    s_value,
    columns,
    early,
    side_out_far,
    state_own,
    far,
    keep,
    send,
    pack,
):
    side, tokens = sn_t.shape
    span = tokens // 2
    width = out_own.shape[1]
    dq = dquery[...].astype(bf16)
    dkv = (dkv_own[...].astype(bf16).astype(f32) + dkv_back[...].astype(f32)).astype(bf16)
    dk, dv = dkv[0:side], dkv[side : 2 * side]
    sn = sn_t[...]
    dnormed = nn(s_query[...], dq) + nn(s_key[...], dk) + nn(s_value[...], dv)
    mixed = mixed_t[...]
    mixed_scale = lax.rsqrt(jnp.mean(mixed * mixed, axis=0, keepdims=True) + EPS)
    unit = mixed * mixed_scale
    scaled = dnormed * columns[:, 1:2]
    dmixed = dmid_t[...] + mixed_scale * (
        scaled - unit * jnp.mean(scaled * unit, axis=0, keepdims=True)
    )
    gate_open = jax.nn.sigmoid(columns[:, 0:1])
    grad_gain = jnp.sum(dnormed * unit, axis=1, keepdims=True)
    grad_gate = jnp.sum(dmixed * lead_t[...], axis=1, keepdims=True) * gate_open * (1.0 - gate_open)
    state = (1.0 - gate_open) * dmixed
    state_own[...] = state[:, 0:span]
    far[0:side] = side_out_far[...]
    far[side : 2 * side] = state[:, span:tokens].astype(bf16)
    ddown = (gate_open * dmixed).astype(bf16)
    pack[:, 0:width] = nn(ddown[:, 0:span], out_own[...]) + nn(ddown[:, span:tokens], out_far[...])
    at = width
    blank = jnp.zeros((side, 128 - side), f32)
    for grad in (dq, dk, dv):
        pack[:, at : at + 128] = jnp.concatenate([nt(sn, grad), blank], axis=1)
        at += 128
    lane = iota((side, 128), 1)
    inner = early.shape[1] - 128
    vectors = early[:, inner : inner + 128]
    vectors = jnp.where(lane == side + 1, grad_gain, vectors)
    pack[:, at : at + 128] = jnp.where(lane == side + 2, grad_gate, vectors)
    pack[:, at + 128 : at + 128 + inner] = early[:, 0:inner]
    size = keep.shape[1]
    core = lax.axis_index("blk") % 2
    keep[...] = pack[:, pl.ds(pl.multiple_of(core * size, 128), size)].astype(bf16)
    send[...] = pack[:, pl.ds(pl.multiple_of((1 - core) * size, 128), size)].astype(bf16)


def quarter_index():
    return (lax.axis_index("blk") // 2) % 2 + 2 * (lax.axis_index("dp") % 2)


def spread_body(*refs):
    pieces, refs = refs[0:8], refs[8:]
    (
        grad_down,
        grad_gate,
        gain_in,
        grad_query,
        grad_key,
        grad_value,
        grad_out,
        gain_mid,
        grad_inner,
        grad_outer,
        pack,
    ) = refs
    side, width = grad_down.shape
    hidden = grad_inner.shape[1]
    size = pieces[0].shape[1]
    core, quarter = lax.axis_index("blk") % 2, quarter_index()
    for i, piece in enumerate(pieces):
        at = ((core ^ (i // 4)) * 4 + (quarter ^ (i % 4))) * size
        pack[:, pl.ds(pl.multiple_of(at, 128), size)] = piece[...].astype(f32)
    whole = pack[...]
    grad_down[...] = whole[:, 0:width]
    at = width
    for target in (grad_query, grad_key, grad_value):
        target[...] = whole[:, at : at + side]
        at += 128
    block = whole[:, at : at + 128]
    grad_out[...] = block[:, 0:side]
    rows = block.T
    gain_mid[...] = rows[side : side + 1]
    gain_in[...] = rows[side + 1 : side + 2]
    grad_gate[...] = rows[side + 2 : side + 3]
    at += 128
    grad_inner[...] = whole[:, at : at + hidden]
    grad_outer[...] = whole[:, at + hidden : at + 2 * hidden]


def per_device(
    hidden,
    side_state,
    doc_lengths,
    norm_in,
    w_query,
    w_key,
    w_value,
    w_out,
    norm_mid,
    w_inner,
    w_outer,
    w_down,
    gate,
    side_norm_in,
    s_query,
    s_key,
    s_value,
    s_out,
    side_norm_mid,
    s_inner,
    s_outer,
    cotangent,
):
    span, rows, width = hidden.shape
    side = side_state.shape[2]
    ff = w_inner.shape[1]
    sff = s_inner.shape[1]
    tokens = 2 * span
    feature = side // SHEADS
    blk_size, dp_size = lax.axis_size("blk"), lax.axis_size("dp")
    half = blk_size // 2
    place = lax.axis_index("blk")
    row = place // half

    def swap(value, axis, size, hop):
        return lax.ppermute(value, axis, [(i, i ^ hop) for i in range(size)])

    def across(value):
        return swap(value, "blk", blk_size, half)

    def beside(value):
        return swap(value, "blk", blk_size, 1)

    hidden = jnp.transpose(hidden, (1, 0, 2))
    hidden_far = across(lax.dynamic_index_in_dim(hidden, 1 - row, 0, keepdims=False))
    hidden_mate = beside(hidden)
    state, cot = (jnp.transpose(array, (1, 2, 0)) for array in (side_state, cotangent))
    side_far = across(
        lax.dynamic_index_in_dim(jnp.concatenate([state, cot], axis=1), 1 - row, 0, keepdims=False)
    )
    down_w, s_outer_t = w_down.T, s_outer.T

    value_t, gains, key_doc, query_doc, side_key_doc, side_query_doc = kernel_call(
        prepare_body,
        [
            ((width, width), bf16),
            ((2, width), f32),
            ((2 * tokens, 128), bf16),
            ((tokens, 128), bf16),
            ((2 * tokens, 128), bf16),
            ((16, tokens), bf16),
        ],
        [doc_lengths, w_value, norm_in, norm_mid],
        vmem=16,
        scalars=(0,),
        cost=(1000, 1000, 0),
    )
    head = width // HEADS
    stride = head + 16
    projections = (gains, w_query, w_key, value_t, key_doc, query_doc)

    def state_of(queries, keys, columns):
        return [
            ((queries, width), bf16),
            ((keys, width), bf16),
            ((HEADS * stride, keys), bf16),
            ((HEADS // 2, 2 * (head + 8), columns), f32),
        ]

    state_a = kernel_call(
        first_body,
        state_of(span, tokens, span),
        [hidden, hidden_mate, *projections],
        vmem=24,
        cost=(1000, 1000, 0),
    )
    small = (s_query, s_key, s_value, s_out, s_inner, gate, side_norm_in, side_norm_mid)
    hidden_far, small, *state_a = lax.optimization_barrier((hidden_far, small, *state_a))
    dup, dup_t, tall_t, columns, s_query_t = kernel_call(
        side_weights_body,
        [
            ((side, 128), bf16),
            ((6 * side, side), bf16),
            ((side + sff, side), bf16),
            ((side, 128), f32),
            ((side, side), bf16),
        ],
        small,
        vmem=8,
        scratch=[pltpu.VMEM((128, 128), f32)],
        cost=(1000, 1000, 0),
    )
    (attended,) = kernel_call(
        second_body,
        [((tokens, width), bf16)],
        [hidden_far, beside(hidden_far), *projections, *state_a],
        vmem=30,
        scratch=[
            pltpu.VMEM((span, width), bf16),
            pltpu.VMEM((tokens, width), bf16),
            pltpu.VMEM((HEADS * stride, tokens), bf16),
            pltpu.VMEM((HEADS * 8, tokens), f32),
        ],
        cost=(8 * 10**9, 8 * 10**6, 0),
    )
    side_far, attended = lax.optimization_barrier((side_far, attended))
    out_own, out_far, sn_rows, sn_t, mixed_t, lead_t = kernel_call(
        dense_body,
        [
            ((span, width), bf16),
            ((span, width), bf16),
            ((tokens, side), bf16),
            ((side, tokens), bf16),
            ((side, tokens), f32),
            ((side, tokens), f32),
        ],
        [
            hidden,
            hidden_far,
            attended,
            gains,
            w_out,
            w_inner,
            w_outer,
            down_w,
            columns,
            state,
            side_far,
        ],
        vmem=28,
        cost=(10 * 10**9, 14 * 10**6, 0),
    )
    sn_mate = beside(sn_rows)
    out_back = across(out_far)
    dkv_own, dkv_mate, dmid_t, *carried = kernel_call(
        side_body,
        [
            ((2 * side, tokens), f32),
            ((2 * side, tokens), bf16),
            ((side, tokens), f32),
            ((side, tokens), f32),
            ((side, tokens), f32),
            ((SHEADS, feature * (feature + 2), tokens), f32),
            ((side, tokens), f32),
            ((sff, tokens), f32),
            ((side, tokens), bf16),
            ((sff, tokens), bf16),
            ((side, tokens), f32),
            ((side, tokens), f32),
        ],
        [
            sn_rows,
            sn_mate,
            mixed_t,
            cot,
            side_far,
            dup,
            dup_t,
            tall_t,
            s_outer_t,
            s_out,
            s_inner,
            columns,
            side_key_doc,
            side_query_doc,
            s_query_t,
        ],
        vmem=36,
        scratch=[
            pltpu.VMEM((SHEADS, tokens, 2 * tokens), bf16),
            pltpu.VMEM((2 * tokens, 128), bf16),
            pltpu.VMEM((2 * side, 2 * tokens), bf16),
            pltpu.VMEM((2 * side, 2 * tokens), bf16),
            pltpu.VMEM((2 * side, tokens), bf16),
            pltpu.VMEM((128, tokens), bf16),
            pltpu.VMEM((side, tokens), f32),
            pltpu.VMEM((SHEADS, feature * (2 * feature + 4), tokens), bf16),
            pltpu.VMEM((2 * side, 2 * tokens), f32),
        ],
        cost=(30 * 10**9, 3 * 10**6, 0),
    )
    dkv_back = beside(dkv_mate)
    side_own, side_back, dquery, early = kernel_call(
        aside_body,
        [
            ((side, span), bf16),
            ((side, span), bf16),
            ((side, tokens), f32),
            ((side, 2 * sff + 128), f32),
        ],
        [*carried, dmid_t, cot, side_far, s_outer_t],
        vmem=12,
        cost=(10**9, 6 * 10**6, 0),
    )
    dkv_back, out_back = lax.optimization_barrier((dkv_back, out_back))
    packed = width + 4 * 128 + 2 * sff
    grad_own, far, keep, send = kernel_call(
        last_body,
        [
            ((side, span), f32),
            ((2 * side, span), bf16),
            ((side, packed // 2), bf16),
            ((side, packed // 2), bf16),
        ],
        [
            dquery,
            dkv_own,
            dkv_back,
            sn_t,
            dmid_t,
            mixed_t,
            lead_t,
            out_own,
            out_far,
            s_query,
            s_key,
            s_value,
            columns,
            early,
            side_back,
        ],
        vmem=16,
        scratch=[pltpu.VMEM((side, packed), f32)],
        cost=(10**9, 3 * 10**6, 0),
    )

    def add(*terms):
        total = terms[0].astype(f32)
        for term in terms[1:]:
            total = total + term.astype(f32)
        return total.astype(bf16)

    quarter = packed // 8
    mine = quarter_index()
    devices = dp_size * blk_size

    def between(value, chip):
        mask = 2 * (chip % 2) + blk_size * (chip // 2)
        return lax.ppermute(value, ("dp", "blk"), [(i, i ^ mask) for i in range(devices)])

    def part(value, index):
        return lax.dynamic_slice_in_dim(value, index * quarter, quarter, 1)

    total = add(keep, beside(send))
    total = add(part(total, mine), *[between(part(total, mine ^ chip), chip) for chip in (1, 2, 3)])
    total, far = lax.optimization_barrier((total, far))
    hop = 2
    while hop < dp_size:
        total = add(total, swap(total, "dp", dp_size, hop))
        hop *= 2
    pieces = [total] + [between(total, chip) for chip in (1, 2, 3)]
    pieces += [beside(piece) for piece in pieces]
    vector = ((1, side), f32)
    square = ((side, side), f32)
    grads = kernel_call(
        spread_body,
        [
            ((side, width), f32),
            vector,
            vector,
            square,
            square,
            square,
            square,
            vector,
            ((side, sff), f32),
            ((side, sff), f32),
        ],
        pieces,
        vmem=16,
        scratch=[pltpu.VMEM((side, packed), f32)],
        cost=(0, 2 * 10**6, 0),
    )
    grads = [grad.reshape(side) if grad.shape[0] == 1 else grad for grad in grads]
    grads[0], grads[-1] = grads[0].T, grads[-1].T

    def both_rows(own, back):
        first = jnp.where(row == 0, own, back)
        second = jnp.where(row == 0, back, own)
        return jnp.stack([first, second])

    far = across(far)
    return (
        jnp.transpose(both_rows(out_own, out_back), (1, 0, 2)),
        jnp.transpose(both_rows(side_own, far[0:side]), (2, 0, 1)),
        jnp.transpose(both_rows(grad_own, far[side : 2 * side].astype(f32)), (2, 0, 1)),
        *grads,
    )


def solution(mesh):
    split = P("blk", "dp", None)
    return jax.shard_map(
        per_device,
        mesh=mesh,
        in_specs=(split, split, P("dp", None)) + (P(),) * 18 + (split,),
        out_specs=(split,) * 3 + (P(),) * 10,
        check_vma=False,
    )
```

```python
import math

import jax
import jax.numpy as jnp
from jax import lax
from jax.experimental import pallas as pl
from jax.experimental.pallas import tpu as pltpu
from jax.sharding import PartitionSpec as P

HEADS = 12
SHEADS = 12
SPARE = 96
EPS = 1e-06
LOG2E = math.log2(math.e)
FAR = 2.0**100
LOW_TOTAL, HIGH_TOTAL = 2.0**-60, 2.0**60

f32, bf16, i32 = jnp.float32, jnp.bfloat16, jnp.int32


def nn(left, right):
    return jnp.dot(left, right, preferred_element_type=f32)


def nt(left, right):
    return lax.dot_general(left, right, (((1,), (1,)), ((), ())), preferred_element_type=f32)


def tn(left, right):
    return lax.dot_general(left, right, (((0,), (0,)), ((), ())), preferred_element_type=f32)


def ones_where(condition):
    return jnp.where(condition, 1.0, 0.0).astype(bf16)


def iota(shape, dim):
    return lax.broadcasted_iota(i32, shape, dim)


def eye(size):
    return ones_where(iota((size, size), 0) == iota((size, size), 1))


def norm_lanes(value, gain):
    return value * lax.rsqrt(jnp.mean(value * value, axis=1, keepdims=True) + EPS) * gain


def gelu(value):
    return 0.5 * value * (1.0 + lax.erf(value * math.sqrt(0.5)))


def gelu_slope(value):
    bell = jnp.exp2(value * value * (-0.5 * LOG2E)) * (1.0 / math.sqrt(2.0 * math.pi))
    return 0.5 * (1.0 + lax.erf(value * math.sqrt(0.5))) + value * bell


def kernel_call(body, outs, ins, *, vmem, scratch=(), whole=(), scalars=(), cost=(0, 0, 0)):
    specs = [
        pl.BlockSpec(
            memory_space=pl.ANY if i in whole else pltpu.SMEM if i in scalars else pltpu.VMEM
        )
        for i in range(len(ins))
    ]
    return pl.pallas_call(
        body,
        out_shape=[jax.ShapeDtypeStruct(shape, kind) for shape, kind in outs],
        in_specs=specs,
        out_specs=[pl.BlockSpec(memory_space=pltpu.VMEM)] * len(outs),
        scratch_shapes=list(scratch),
        compiler_params=pltpu.CompilerParams(vmem_limit_bytes=vmem * 2**20),
        cost_estimate=pl.CostEstimate(flops=cost[0], bytes_accessed=cost[1], transcendentals=cost[2]),
    )(*ins)


def doubled(rows, columns, feature):
    wide, thin = iota((rows, columns), 0), iota((rows, columns), 1)
    source = (wide // (2 * feature)) * feature + wide % feature
    return ones_where(source == thin)


def bounds(doc_lengths, row):
    starts, ends, at = [], [], jnp.int32(0)
    for d in range(doc_lengths.shape[1]):
        starts.append(at)
        at = at + doc_lengths[row, d]
        ends.append(at)
    return starts, ends


def in_doc(doc_lengths, row, runs, length, shape, token_dim):
    starts, ends = bounds(doc_lengths, row)
    parts = []
    part_shape = list(shape)
    part_shape[token_dim] = length
    number = iota(tuple(part_shape), 1 - token_dim)
    first = jnp.zeros(tuple(part_shape), i32)
    last = first
    for d, (start, end) in enumerate(zip(starts, ends)):
        first = jnp.where(number == d, start, first)
        last = jnp.where(number == d, end, last)
    for run in runs:
        position = iota(tuple(part_shape), token_dim) + run
        parts.append(jnp.where((position >= first) & (position < last), 1.0, 0.0))
    return jnp.concatenate(parts, axis=token_dim)


def side_weights_body(
    s_query, s_key, s_value, s_out, s_inner, gate, gain_in, gain_mid, dup, dup_t, tall_t, columns, query_t, lines
):
    side, hidden = s_inner.shape
    feature = side // SHEADS
    dup[...] = nn(s_key[...], ones_where(iota(dup.shape, 0) == iota(dup.shape, 1))).astype(bf16)
    query_t[...] = nt(eye(side), s_query[...]).astype(bf16)
    spread_t = doubled(2 * side, side, feature)
    for i, weight in enumerate((s_query, s_key, s_value)):
        dup_t[2 * side * i : 2 * side * (i + 1)] = nt(spread_t, weight[...]).astype(bf16)
    tall_t[0:side] = nt(eye(side), s_out[...]).astype(bf16)
    tall_t[side : side + hidden] = nt(eye(hidden), s_inner[...]).astype(bf16)
    lines[...] = jnp.zeros(lines.shape, f32)
    for i, line in enumerate((gate, gain_in, gain_mid)):
        lines[i : i + 1, 0:side] = line[...].reshape(1, side)
    columns[...] = lines[...].T[0:side]


def prepare_body(
    doc_lengths, w_value, norm_in, norm_mid, value_t, gains, bias, side_key_doc, side_query_doc
):
    value_t[...] = nt(eye(w_value.shape[0]), w_value[...]).astype(bf16)
    for i, line in enumerate((norm_in, norm_mid)):
        gains[i : i + 1] = line[...].astype(f32).reshape(1, line.shape[0])
    keys, tokens = bias.shape
    span = tokens // 2
    place, half = lax.axis_index("blk"), lax.axis_size("blk") // 2
    row = place // half
    own, mate = place * span, (place ^ 1) * span
    far, far_mate = (place ^ half) * span, (place ^ half ^ 1) * span
    found = in_doc(doc_lengths, row, (own, mate, far, far_mate), span, (keys, 128), 0)
    mine = jnp.concatenate([found[0:span], found[tokens : tokens + span]], axis=0)
    bias[...] = nt((found - 1.0).astype(bf16), (mine * FAR).astype(bf16))
    mates = jnp.concatenate([found[span:tokens], found[tokens + span : keys]], axis=0)
    spare = SPARE
    low = iota((keys, 128), 1) < spare
    ordered = pltpu.roll(jnp.concatenate([mine, mates], axis=0), spare, 1)
    side_key_doc[...] = jnp.where(low, 0.0, ordered - 1.0).astype(bf16)
    side_query_doc[...] = (in_doc(doc_lengths, row, (own, far), span, (16, tokens), 1) * FAR).astype(bf16)


def project(tokens, gain, w_query, w_key, value_t, queries):
    normed = norm_lanes(tokens.astype(f32), gain).astype(bf16)
    query = nn(normed[0:queries], w_query[...]).astype(bf16)
    return query, nn(normed, w_key[...]).astype(bf16), nt(value_t[...], normed).astype(bf16)


def padded(value_t, head):
    ones = jnp.ones((16, value_t.shape[1]), bf16)
    pieces = []
    for at in range(0, value_t.shape[0], head):
        pieces += [value_t[at : at + head], ones]
    return jnp.concatenate(pieces, axis=0)


def pair_lanes(j):
    return pl.ds(pl.multiple_of(j * 128, 128), 128)


def pair_sums(j, queries, keys, values, bias, shifted=False):
    width = queries[0].shape[1]
    head = width // HEADS
    stride = values[0].shape[0] // HEADS
    lanes = pair_lanes(j)
    key = jnp.concatenate([ref[:, lanes] for ref in keys], axis=0)
    query = jnp.concatenate([ref[:, lanes] for ref in queries], axis=0)
    rows = pl.ds(pl.multiple_of(j * 2 * stride, 16), 2 * stride)
    value = jnp.concatenate([ref[rows, :] for ref in values], axis=1)
    lane = iota((1, 128), 1) // head
    masked = [query * ones_where(lane == i) for i in range(2)]
    count = query.shape[0]

    scores = nt(key, jnp.concatenate(masked, axis=0)) * (LOG2E * head**-0.5)
    scores = scores + jnp.concatenate([bias, bias], axis=1)
    if shifted:
        scores = scores - jnp.max(scores, axis=0, keepdims=True)
    both = nn(value, jnp.exp2(scores).astype(bf16))
    return [both[i * stride : i * stride + head + 8, i * count : (i + 1) * count] for i in range(2)]


def first_body(own, mate, gains, w_query, w_key, value_t, bias, query, key, value, part):
    _, span, width = own.shape
    head = width // HEADS
    row = lax.axis_index("blk") // (lax.axis_size("blk") // 2)
    tokens = jnp.concatenate([own[row], mate[row]], axis=0)
    query[...], key[...], value_new = project(
        tokens, gains[0:1], w_query, w_key, value_t, span
    )
    value[...] = padded(value_new, head)

    def pair(j, carry):
        sums = pair_sums(j, [query], [key], [value], bias[0 : 2 * span, 0:span])
        part[j] = jnp.concatenate(sums, axis=0)
        return carry

    lax.fori_loop(0, HEADS // 2, pair, 0, unroll=6)


def out_of_range(totals):
    lowest, highest = jnp.min(totals), jnp.max(totals)
    return jnp.logical_not((lowest > LOW_TOTAL) & (highest < HIGH_TOTAL))


def far_body(far, gains, w_query, w_key, w_value, query, key, value):
    width = far.shape[1]
    head = width // HEADS
    normed = norm_lanes(far[...].astype(f32), gains[0:1]).astype(bf16)
    query[...] = nn(normed, w_query[...]).astype(bf16)
    key[...] = nn(normed, w_key[...]).astype(bf16)
    value[...] = padded(nn(normed, w_value[...]).astype(bf16).T, head)


def second_body(
    far_mate,
    gains,
    w_key,
    w_value,
    bias,
    query_a,
    key_a,
    value_a,
    part_a,
    query_b,
    key_b,
    value_b,
    attended,
    key,
    value,
    totals,
):
    span, width = far_mate.shape
    head = width // HEADS
    normed = norm_lanes(far_mate[...].astype(f32), gains[0:1]).astype(bf16)
    key[...] = nn(normed, w_key[...]).astype(bf16)
    value[...] = padded(nn(normed, w_value[...]).astype(bf16).T, head)
    keys, values, queries = [key_a, key_b, key], [value_a, value_b, value], [query_a, query_b]

    def finish(j, sums):
        results = []
        for i, summed in enumerate(sums):
            totals[pl.ds(pl.multiple_of((2 * j + i) * 8, 8), 8), :] = summed[head : head + 8]
            results.append(summed[0:head] * (1.0 / summed[head : head + 1]))
        attended[:, pair_lanes(j)] = jnp.concatenate(results, axis=0).T.astype(bf16)

    def pair(j, carry):
        old = pair_sums(j, [query_a], keys[1:], values[1:], bias[2 * span : 4 * span, 0:span])
        new = pair_sums(j, [query_b], keys, values, bias[:, span : 2 * span])
        sums = []
        for i in range(2):
            rows = slice(i * (head + 8), (i + 1) * (head + 8))
            sums.append(jnp.concatenate([old[i] + part_a[j, rows], new[i]], axis=1))
        finish(j, sums)
        return carry

    lax.fori_loop(0, HEADS // 2, pair, 0, unroll=6)

    @pl.when(out_of_range(totals[...]))
    def _():
        def again(j, carry):
            finish(j, pair_sums(j, queries, keys, values, bias[...], shifted=True))
            return carry

        lax.fori_loop(0, HEADS // 2, again, 0)


def dense_body(
    own, far, attended, gains, w_out, w_inner, w_outer, down_w, columns, state, side_far, out_own, out_far, sn_rows, sn_t, mixed_t, lead_t
):
    _, span, width = own.shape
    row = lax.axis_index("blk") // (lax.axis_size("blk") // 2)
    tokens = jnp.concatenate([own[row], far[...]], axis=0)
    after = tokens.astype(f32) + nn(attended[...], w_out[...])
    middle = norm_lanes(after, gains[1:2]).astype(bf16)
    result = after
    for at in range(0, w_inner.shape[1], width):
        act = gelu(nn(middle, w_inner[:, at : at + width])).astype(bf16)
        result = result + nn(act, w_outer[at : at + width, :])
    out = result.astype(bf16)
    out_own[...] = out[0:span]
    out_far[...] = out[span : 2 * span]

    side = state.shape[1]
    down_t = nt(down_w[...], out)
    state_t = jnp.concatenate([state[row], side_far[0:side]], axis=1).astype(f32)
    gate_open = jax.nn.sigmoid(columns[:, 0:1])
    mixed = gate_open * down_t + (1.0 - gate_open) * state_t
    normed = (
        mixed * lax.rsqrt(jnp.mean(mixed * mixed, axis=0, keepdims=True) + EPS) * columns[:, 1:2]
    )
    mixed_t[...] = mixed
    lead_t[...] = down_t - state_t
    sn_t[...] = normed.astype(bf16)
    sn_rows[...] = normed.T.astype(bf16)


def outer_rows(left, right):
    return jnp.concatenate([left[f : f + 1] * right for f in range(left.shape[0])], axis=0)


def inner_rows(left, products):
    count = left.shape[0]
    total = left[0:1] * products[0:count]
    for f in range(1, count):
        total = total + left[f : f + 1] * products[f * count : (f + 1) * count]
    return total


def two_parts(value):
    high = value.astype(bf16).astype(f32)
    return [high, value - high]


def side_body(
    sn_own,
    sn_mate,
    mixed_t,
    cot,
    side_far,
    dup,
    dup_t,
    tall_t,
    s_outer_t,
    s_out,
    s_inner,
    columns,
    key_doc,
    query_doc,
    thin_query,
    dkv_own,
    dkv_mate,
    dmid_t,
    attn_t,
    inverse,
    moments,
    mid_t,
    inner_t,
    normed_t,
    dinner_t,
    dnormed_t,
    dattn_t,
    weights,
    keys,
    key_t,
    value_t,
    query_t,
    query_s,
    totals,
    back_rows,
    dkv_t,
):
    tokens, side = sn_own.shape
    feature = side // SHEADS
    hidden = s_inner.shape[1]
    wide = 2 * side
    row = lax.axis_index("blk") // (lax.axis_size("blk") // 2)
    scale = feature**-0.5

    sn = jnp.concatenate([sn_own[...], sn_mate[...]], axis=0)
    keys[...] = nn(sn, dup[...]).astype(bf16) + key_doc[...]
    key_t[...] = nt(dup_t[wide : 2 * wide], sn).astype(bf16)
    second = iota((wide, 2 * tokens), 0) % (2 * feature) >= feature
    value_t[...] = jnp.where(second, 1.0, nt(dup_t[2 * wide : 3 * wide], sn)).astype(bf16)
    query = nt(dup_t[0:wide], sn_own[...]).astype(bf16)
    query_t[...] = query
    query_s[0:side] = nt(thin_query[...], sn_own[...]).astype(bf16)
    query_s[side : side + 16] = query_doc[...]
    query_s[side + 16 :] = jnp.zeros((128 - side - 16, tokens), bf16)
    owner = iota((128, 1), 0) // feature

    def head_rows(h, count):
        return pl.ds(pl.multiple_of(h * count, count), count)

    def attend(shifted, size):
        def group(j, carry):
            for i in range(size):
                h = size * j + i
                rows, eight = head_rows(h, 16), head_rows(h, 8)
                mine = ones_where((owner == h) | (owner >= SHEADS))
                scores = nn(keys[...], query_s[...] * mine) * (scale * LOG2E)
                if shifted:
                    scores = scores - jnp.max(scores, axis=0, keepdims=True)
                weight = jnp.exp2(scores).astype(bf16)
                weights[h] = weight.T
                value, key = value_t[rows, :], key_t[rows, :]
                products = outer_rows(value[0:feature].astype(f32), key[0:feature].astype(f32))
                products = jnp.concatenate(two_parts(products), axis=0).astype(bf16)
                summed = nn(jnp.concatenate([value, key, products], axis=0), weight)
                total = summed[feature : 2 * feature]
                totals[eight, :] = total
                invert = 1.0 / total
                inverse[eight, :] = invert
                attn_t[eight, :] = summed[0:feature] * invert
                at = 4 * feature + feature * feature
                moments[h] = jnp.concatenate(
                    [summed[2 * feature : 4 * feature], summed[4 * feature : at] + summed[at:]], axis=0
                )
            return carry

        lax.fori_loop(0, SHEADS // size, group, 0)

    attend(False, SHEADS)

    @pl.when(out_of_range(totals[...]))
    def _():
        attend(True, 2)

    attn = attn_t[...]
    attn_low = attn.astype(bf16)
    mid = mixed_t[...] + nn(tall_t[0:side], attn_low)
    mid_scale = lax.rsqrt(jnp.mean(mid * mid, axis=0, keepdims=True) + EPS)
    gain = columns[:, 2:3]
    unit = mid * mid_scale
    normed = (unit * gain).astype(bf16)
    inner = nn(tall_t[side : side + hidden], normed)
    dy_low = jnp.concatenate([cot[row], side_far[side : 2 * side]], axis=1)
    dinner = (gelu_slope(inner) * tn(s_outer_t[...], dy_low)).astype(bf16)
    dnormed = nn(s_inner[...], dinner)
    scaled = dnormed * gain
    dmid = dy_low.astype(f32) + mid_scale * (
        scaled - unit * jnp.mean(scaled * unit, axis=0, keepdims=True)
    )
    dmid_t[...] = dmid
    dattn = nn(s_out[...], dmid.astype(bf16)).astype(bf16).astype(f32)
    mid_t[...] = mid
    inner_t[...] = inner
    normed_t[...] = normed
    dinner_t[...] = dinner
    dnormed_t[...] = dnormed
    dattn_t[...] = dattn

    for h in range(SHEADS):
        eight = slice(h * feature, (h + 1) * feature)
        invert = inverse[eight, :]
        term = jnp.sum(dattn[eight] * attn[eight], axis=0, keepdims=True)
        query = query_t[2 * h * feature : 2 * (h + 1) * feature].astype(f32)[0:feature]
        share = dattn[eight] * invert
        back_rows[h] = jnp.concatenate(
            two_parts(share) + two_parts(term * invert * query) + two_parts(outer_rows(share, query)), axis=0
        ).astype(bf16)

    for h in range(SHEADS):
        eight = slice(h * feature, (h + 1) * feature)
        summed = nn(back_rows[h], weights[h])
        dkv_t[side + h * feature : side + (h + 1) * feature] = (
            summed[0:feature] + summed[feature : 2 * feature]
        )
        value = value_t[2 * h * feature : 2 * (h + 1) * feature].astype(f32)[0:feature]
        at = 4 * feature + feature * feature
        raw = inner_rows(value, summed[4 * feature : at] + summed[at:])
        raw = raw - (summed[2 * feature : 3 * feature] + summed[3 * feature : 4 * feature])
        dkv_t[eight] = raw * scale
    dkv_own[...] = dkv_t[:, 0:tokens]
    dkv_mate[...] = dkv_t[:, tokens : 2 * tokens].astype(bf16)


def aside_body(
    attn_t,
    inverse,
    moments,
    mid_t,
    inner_t,
    normed_t,
    dinner_t,
    dnormed_t,
    dattn_t,
    dmid_t,
    cot,
    side_far,
    s_outer_t,
    out_own,
    out_far,
    dquery,
    early,
):
    side, tokens = mid_t.shape
    span = tokens // 2
    feature = side // SHEADS
    hidden = inner_t.shape[0]
    row = lax.axis_index("blk") // (lax.axis_size("blk") // 2)
    mid = mid_t[...]
    act = gelu(inner_t[...]).astype(bf16)
    out = (mid + nn(s_outer_t[...], act)).astype(bf16)
    out_own[...] = out[:, 0:span]
    out_far[...] = out[:, span : 2 * span]
    dy_low = jnp.concatenate([cot[row], side_far[side : 2 * side]], axis=1)
    early[:, 0:hidden] = nt(normed_t[...], dinner_t[...])
    early[:, hidden : 2 * hidden] = nt(dy_low, act)
    unit = mid * lax.rsqrt(jnp.mean(mid * mid, axis=0, keepdims=True) + EPS)
    grad_gain = jnp.sum(dnormed_t[...] * unit, axis=1, keepdims=True)
    last = nt(attn_t[...].astype(bf16), dmid_t[...].astype(bf16))
    last = jnp.concatenate([last, jnp.zeros((side, 128 - side), f32)], axis=1)
    early[:, 2 * hidden : 2 * hidden + 128] = jnp.where(
        iota((side, 128), 1) == side, grad_gain, last
    )
    for h in range(SHEADS):
        eight = slice(h * feature, (h + 1) * feature)
        dattn = dattn_t[eight, :]
        term = jnp.sum(dattn * attn_t[eight, :], axis=0, keepdims=True)
        moment = moments[h]
        raw = inner_rows(dattn, moment[2 * feature :]) - term * moment[0:feature]
        dquery[eight, :] = raw * inverse[eight, :] * feature**-0.5


def last_body(
    dquery,
    dkv_own,
    dkv_back,
    sn_t,
    dmid_t,
    mixed_t,
    lead_t,
    out_own,
    out_far,
    s_query,
    s_key,
    s_value,
    columns,
    early,
    side_out_far,
    state_own,
    far,
    keep,
    send,
    pack,
):
    side, tokens = sn_t.shape
    span = tokens // 2
    width = out_own.shape[1]
    dq = dquery[...].astype(bf16)
    dkv = (dkv_own[...].astype(bf16).astype(f32) + dkv_back[...].astype(f32)).astype(bf16)
    dk, dv = dkv[0:side], dkv[side : 2 * side]
    sn = sn_t[...]
    dnormed = nn(s_query[...], dq) + nn(s_key[...], dk) + nn(s_value[...], dv)
    mixed = mixed_t[...]
    mixed_scale = lax.rsqrt(jnp.mean(mixed * mixed, axis=0, keepdims=True) + EPS)
    unit = mixed * mixed_scale
    scaled = dnormed * columns[:, 1:2]
    dmixed = dmid_t[...] + mixed_scale * (
        scaled - unit * jnp.mean(scaled * unit, axis=0, keepdims=True)
    )
    gate_open = jax.nn.sigmoid(columns[:, 0:1])
    grad_gain = jnp.sum(dnormed * unit, axis=1, keepdims=True)
    grad_gate = jnp.sum(dmixed * lead_t[...], axis=1, keepdims=True) * gate_open * (1.0 - gate_open)
    state = (1.0 - gate_open) * dmixed
    state_own[...] = state[:, 0:span]
    far[0:side] = side_out_far[...]
    far[side : 2 * side] = state[:, span:tokens].astype(bf16)
    ddown = (gate_open * dmixed).astype(bf16)
    pack[:, 0:width] = nn(ddown[:, 0:span], out_own[...]) + nn(ddown[:, span:tokens], out_far[...])
    at = width
    blank = jnp.zeros((side, 128 - side), f32)
    for grad in (dq, dk, dv):
        pack[:, at : at + 128] = jnp.concatenate([nt(sn, grad), blank], axis=1)
        at += 128
    lane = iota((side, 128), 1)
    inner = early.shape[1] - 128
    vectors = early[:, inner : inner + 128]
    vectors = jnp.where(lane == side + 1, grad_gain, vectors)
    pack[:, at : at + 128] = jnp.where(lane == side + 2, grad_gate, vectors)
    pack[:, at + 128 : at + 128 + inner] = early[:, 0:inner]
    size = keep.shape[1]
    core = lax.axis_index("blk") % 2
    keep[...] = pack[:, pl.ds(pl.multiple_of(core * size, 128), size)].astype(bf16)
    send[...] = pack[:, pl.ds(pl.multiple_of((1 - core) * size, 128), size)].astype(bf16)


def quarter_index():
    return (lax.axis_index("blk") // 2) % 2 + 2 * (lax.axis_index("dp") % 2)


def spread_body(*refs):
    pieces, refs = refs[0:8], refs[8:]
    (
        grad_down,
        grad_gate,
        gain_in,
        grad_query,
        grad_key,
        grad_value,
        grad_out,
        gain_mid,
        grad_inner,
        grad_outer,
        pack,
    ) = refs
    side, width = grad_down.shape
    hidden = grad_inner.shape[1]
    size = pieces[0].shape[1]
    core, quarter = lax.axis_index("blk") % 2, quarter_index()
    for i, piece in enumerate(pieces):
        at = ((core ^ (i // 4)) * 4 + (quarter ^ (i % 4))) * size
        pack[:, pl.ds(pl.multiple_of(at, 128), size)] = piece[...].astype(f32)
    whole = pack[...]
    grad_down[...] = whole[:, 0:width]
    at = width
    for target in (grad_query, grad_key, grad_value):
        target[...] = whole[:, at : at + side]
        at += 128
    block = whole[:, at : at + 128]
    grad_out[...] = block[:, 0:side]
    rows = block.T
    gain_mid[...] = rows[side : side + 1]
    gain_in[...] = rows[side + 1 : side + 2]
    grad_gate[...] = rows[side + 2 : side + 3]
    at += 128
    grad_inner[...] = whole[:, at : at + hidden]
    grad_outer[...] = whole[:, at + hidden : at + 2 * hidden]


def per_device(
    hidden,
    side_state,
    doc_lengths,
    norm_in,
    w_query,
    w_key,
    w_value,
    w_out,
    norm_mid,
    w_inner,
    w_outer,
    w_down,
    gate,
    side_norm_in,
    s_query,
    s_key,
    s_value,
    s_out,
    side_norm_mid,
    s_inner,
    s_outer,
    cotangent,
):
    span, rows, width = hidden.shape
    side = side_state.shape[2]
    ff = w_inner.shape[1]
    sff = s_inner.shape[1]
    tokens = 2 * span
    feature = side // SHEADS
    blk_size, dp_size = lax.axis_size("blk"), lax.axis_size("dp")
    half = blk_size // 2
    place = lax.axis_index("blk")
    row = place // half

    def swap(value, axis, size, hop):
        return lax.ppermute(value, axis, [(i, i ^ hop) for i in range(size)])

    def across(value):
        return swap(value, "blk", blk_size, half)

    def beside(value):
        return swap(value, "blk", blk_size, 1)

    hidden = jnp.transpose(hidden, (1, 0, 2))
    hidden_far = across(lax.dynamic_index_in_dim(hidden, 1 - row, 0, keepdims=False))
    hidden_mate = beside(hidden)
    state, cot = (jnp.transpose(array, (1, 2, 0)) for array in (side_state, cotangent))
    side_far = across(
        lax.dynamic_index_in_dim(jnp.concatenate([state, cot], axis=1), 1 - row, 0, keepdims=False)
    )
    down_w, s_outer_t = w_down.T, s_outer.T

    value_t, gains, bias, side_key_doc, side_query_doc = kernel_call(
        prepare_body,
        [
            ((width, width), bf16),
            ((2, width), f32),
            ((2 * tokens, tokens), f32),
            ((2 * tokens, 128), bf16),
            ((16, tokens), bf16),
        ],
        [doc_lengths, w_value, norm_in, norm_mid],
        vmem=16,
        scalars=(0,),
        cost=(1000, 1000, 0),
    )
    head = width // HEADS
    stride = head + 16
    projections = (gains, w_query, w_key, value_t, bias)

    def state_of(queries, keys, columns):
        return [
            ((queries, width), bf16),
            ((keys, width), bf16),
            ((HEADS * stride, keys), bf16),
            ((HEADS // 2, 2 * (head + 8), columns), f32),
        ]

    state_a = kernel_call(
        first_body,
        state_of(span, tokens, span),
        [hidden, hidden_mate, *projections],
        vmem=24,
        cost=(1000, 1000, 0),
    )
    small = (s_query, s_key, s_value, s_out, s_inner, gate, side_norm_in, side_norm_mid)
    hidden_far, small, *state_a = lax.optimization_barrier((hidden_far, small, *state_a))
    dup, dup_t, tall_t, columns, s_query_t = kernel_call(
        side_weights_body,
        [
            ((side, 128), bf16),
            ((6 * side, side), bf16),
            ((side + sff, side), bf16),
            ((side, 128), f32),
            ((side, side), bf16),
        ],
        small,
        vmem=8,
        scratch=[pltpu.VMEM((128, 128), f32)],
        cost=(1000, 1000, 0),
    )
    far_mate = beside(hidden_far)
    state_b = kernel_call(
        far_body,
        state_of(span, span, span)[0:3],
        [hidden_far, gains, w_query, w_key, w_value],
        vmem=16,
        cost=(5 * 10**9, 8 * 10**6, 0),
    )
    (attended,) = kernel_call(
        second_body,
        [((tokens, width), bf16)],
        [far_mate, gains, w_key, w_value, bias, *state_a, *state_b],
        vmem=26,
        scratch=[
            pltpu.VMEM((span, width), bf16),
            pltpu.VMEM((HEADS * stride, span), bf16),
            pltpu.VMEM((HEADS * 8, tokens), f32),
        ],
        cost=(8 * 10**9, 8 * 10**6, 0),
    )
    side_far, attended = lax.optimization_barrier((side_far, attended))
    out_own, out_far, sn_rows, sn_t, mixed_t, lead_t = kernel_call(
        dense_body,
        [
            ((span, width), bf16),
            ((span, width), bf16),
            ((tokens, side), bf16),
            ((side, tokens), bf16),
            ((side, tokens), f32),
            ((side, tokens), f32),
        ],
        [
            hidden,
            hidden_far,
            attended,
            gains,
            w_out,
            w_inner,
            w_outer,
            down_w,
            columns,
            state,
            side_far,
        ],
        vmem=28,
        cost=(10 * 10**9, 14 * 10**6, 0),
    )
    sn_mate = beside(sn_rows)
    out_back = across(out_far)
    dkv_own, dkv_mate, dmid_t, *carried = kernel_call(
        side_body,
        [
            ((2 * side, tokens), f32),
            ((2 * side, tokens), bf16),
            ((side, tokens), f32),
            ((side, tokens), f32),
            ((side, tokens), f32),
            ((SHEADS, feature * (feature + 2), tokens), f32),
            ((side, tokens), f32),
            ((sff, tokens), f32),
            ((side, tokens), bf16),
            ((sff, tokens), bf16),
            ((side, tokens), f32),
            ((side, tokens), f32),
        ],
        [
            sn_rows,
            sn_mate,
            mixed_t,
            cot,
            side_far,
            dup,
            dup_t,
            tall_t,
            s_outer_t,
            s_out,
            s_inner,
            columns,
            side_key_doc,
            side_query_doc,
            s_query_t,
        ],
        vmem=36,
        scratch=[
            pltpu.VMEM((SHEADS, tokens, 2 * tokens), bf16),
            pltpu.VMEM((2 * tokens, 128), bf16),
            pltpu.VMEM((2 * side, 2 * tokens), bf16),
            pltpu.VMEM((2 * side, 2 * tokens), bf16),
            pltpu.VMEM((2 * side, tokens), bf16),
            pltpu.VMEM((128, tokens), bf16),
            pltpu.VMEM((side, tokens), f32),
            pltpu.VMEM((SHEADS, feature * (2 * feature + 4), tokens), bf16),
            pltpu.VMEM((2 * side, 2 * tokens), f32),
        ],
        cost=(30 * 10**9, 3 * 10**6, 0),
    )
    dkv_back = beside(dkv_mate)
    side_own, side_back, dquery, early = kernel_call(
        aside_body,
        [
            ((side, span), bf16),
            ((side, span), bf16),
            ((side, tokens), f32),
            ((side, 2 * sff + 128), f32),
        ],
        [*carried, dmid_t, cot, side_far, s_outer_t],
        vmem=12,
        cost=(10**9, 6 * 10**6, 0),
    )
    dkv_back, out_back = lax.optimization_barrier((dkv_back, out_back))
    packed = width + 4 * 128 + 2 * sff
    grad_own, far, keep, send = kernel_call(
        last_body,
        [
            ((side, span), f32),
            ((2 * side, span), bf16),
            ((side, packed // 2), bf16),
            ((side, packed // 2), bf16),
        ],
        [
            dquery,
            dkv_own,
            dkv_back,
            sn_t,
            dmid_t,
            mixed_t,
            lead_t,
            out_own,
            out_far,
            s_query,
            s_key,
            s_value,
            columns,
            early,
            side_back,
        ],
        vmem=16,
        scratch=[pltpu.VMEM((side, packed), f32)],
        cost=(10**9, 3 * 10**6, 0),
    )

    def add(*terms):
        total = terms[0].astype(f32)
        for term in terms[1:]:
            total = total + term.astype(f32)
        return total.astype(bf16)

    quarter = packed // 8
    mine = quarter_index()
    devices = dp_size * blk_size

    def between(value, chip):
        mask = 2 * (chip % 2) + blk_size * (chip // 2)
        return lax.ppermute(value, ("dp", "blk"), [(i, i ^ mask) for i in range(devices)])

    def part(value, index):
        return lax.dynamic_slice_in_dim(value, index * quarter, quarter, 1)

    total = add(keep, beside(send))
    total = add(part(total, mine), *[between(part(total, mine ^ chip), chip) for chip in (1, 2, 3)])
    total, far = lax.optimization_barrier((total, far))
    hop = 2
    while hop < dp_size:
        total = add(total, swap(total, "dp", dp_size, hop))
        hop *= 2
    pieces = [total] + [between(total, chip) for chip in (1, 2, 3)]
    pieces += [beside(piece) for piece in pieces]
    vector = ((1, side), f32)
    square = ((side, side), f32)
    grads = kernel_call(
        spread_body,
        [
            ((side, width), f32),
            vector,
            vector,
            square,
            square,
            square,
            square,
            vector,
            ((side, sff), f32),
            ((side, sff), f32),
        ],
        pieces,
        vmem=16,
        scratch=[pltpu.VMEM((side, packed), f32)],
        cost=(0, 2 * 10**6, 0),
    )
    grads = [grad.reshape(side) if grad.shape[0] == 1 else grad for grad in grads]
    grads[0], grads[-1] = grads[0].T, grads[-1].T

    def both_rows(own, back):
        first = jnp.where(row == 0, own, back)
        second = jnp.where(row == 0, back, own)
        return jnp.stack([first, second])

    far = across(far)
    return (
        jnp.transpose(both_rows(out_own, out_back), (1, 0, 2)),
        jnp.transpose(both_rows(side_own, far[0:side]), (2, 0, 1)),
        jnp.transpose(both_rows(grad_own, far[side : 2 * side].astype(f32)), (2, 0, 1)),
        *grads,
    )


def solution(mesh):
    split = P("blk", "dp", None)
    return jax.shard_map(
        per_device,
        mesh=mesh,
        in_specs=(split, split, P("dp", None)) + (P(),) * 18 + (split,),
        out_specs=(split,) * 3 + (P(),) * 10,
        check_vma=False,
    )
```

```python
import math

import jax
import jax.numpy as jnp
from jax import lax
from jax.experimental import pallas as pl
from jax.experimental.pallas import tpu as pltpu
from jax.sharding import PartitionSpec as P

HEADS = 12
SHEADS = 12
SPARE = 96
EPS = 1e-06
LOG2E = math.log2(math.e)
FAR = 2.0**100
LOW_TOTAL, HIGH_TOTAL = 2.0**-60, 2.0**60

f32, bf16, i32 = jnp.float32, jnp.bfloat16, jnp.int32


def nn(left, right):
    return jnp.dot(left, right, preferred_element_type=f32)


def nt(left, right):
    return lax.dot_general(left, right, (((1,), (1,)), ((), ())), preferred_element_type=f32)


def tn(left, right):
    return lax.dot_general(left, right, (((0,), (0,)), ((), ())), preferred_element_type=f32)


def ones_where(condition):
    return jnp.where(condition, 1.0, 0.0).astype(bf16)


def iota(shape, dim):
    return lax.broadcasted_iota(i32, shape, dim)


def eye(size):
    return ones_where(iota((size, size), 0) == iota((size, size), 1))


def norm_lanes(value, gain):
    return value * lax.rsqrt(jnp.mean(value * value, axis=1, keepdims=True) + EPS) * gain


def gelu(value):
    return 0.5 * value * (1.0 + lax.erf(value * math.sqrt(0.5)))


def gelu_slope(value):
    bell = jnp.exp2(value * value * (-0.5 * LOG2E)) * (1.0 / math.sqrt(2.0 * math.pi))
    return 0.5 * (1.0 + lax.erf(value * math.sqrt(0.5))) + value * bell


def kernel_call(body, outs, ins, *, vmem, scratch=(), whole=(), scalars=(), cost=(0, 0, 0)):
    specs = [
        pl.BlockSpec(
            memory_space=pl.ANY if i in whole else pltpu.SMEM if i in scalars else pltpu.VMEM
        )
        for i in range(len(ins))
    ]
    return pl.pallas_call(
        body,
        out_shape=[jax.ShapeDtypeStruct(shape, kind) for shape, kind in outs],
        in_specs=specs,
        out_specs=[pl.BlockSpec(memory_space=pltpu.VMEM)] * len(outs),
        scratch_shapes=list(scratch),
        compiler_params=pltpu.CompilerParams(vmem_limit_bytes=vmem * 2**20),
        cost_estimate=pl.CostEstimate(flops=cost[0], bytes_accessed=cost[1], transcendentals=cost[2]),
    )(*ins)


def doubled(rows, columns, feature):
    wide, thin = iota((rows, columns), 0), iota((rows, columns), 1)
    source = (wide // (2 * feature)) * feature + wide % feature
    return ones_where(source == thin)


def bounds(doc_lengths, row):
    starts, ends, at = [], [], jnp.int32(0)
    for d in range(doc_lengths.shape[1]):
        starts.append(at)
        at = at + doc_lengths[row, d]
        ends.append(at)
    return starts, ends


def in_doc(doc_lengths, row, runs, length, shape, token_dim):
    starts, ends = bounds(doc_lengths, row)
    parts = []
    part_shape = list(shape)
    part_shape[token_dim] = length
    number = iota(tuple(part_shape), 1 - token_dim)
    first = jnp.zeros(tuple(part_shape), i32)
    last = first
    for d, (start, end) in enumerate(zip(starts, ends)):
        first = jnp.where(number == d, start, first)
        last = jnp.where(number == d, end, last)
    for run in runs:
        position = iota(tuple(part_shape), token_dim) + run
        parts.append(jnp.where((position >= first) & (position < last), 1.0, 0.0))
    return jnp.concatenate(parts, axis=token_dim)


def side_weights_body(
    s_query, s_key, s_value, s_out, s_inner, gate, gain_in, gain_mid, dup, dup_t, tall_t, columns, query_t, lines
):
    side, hidden = s_inner.shape
    feature = side // SHEADS
    dup[...] = nn(s_key[...], ones_where(iota(dup.shape, 0) == iota(dup.shape, 1))).astype(bf16)
    query_t[...] = nt(eye(side), s_query[...]).astype(bf16)
    spread_t = doubled(2 * side, side, feature)
    for i, weight in enumerate((s_query, s_key, s_value)):
        dup_t[2 * side * i : 2 * side * (i + 1)] = nt(spread_t, weight[...]).astype(bf16)
    tall_t[0:side] = nt(eye(side), s_out[...]).astype(bf16)
    tall_t[side : side + hidden] = nt(eye(hidden), s_inner[...]).astype(bf16)
    lines[...] = jnp.zeros(lines.shape, f32)
    for i, line in enumerate((gate, gain_in, gain_mid)):
        lines[i : i + 1, 0:side] = line[...].reshape(1, side)
    columns[...] = lines[...].T[0:side]


def prepare_body(
    doc_lengths, w_value, norm_in, norm_mid, value_t, gains, key_doc, query_doc, side_key_doc, side_query_doc
):
    value_t[...] = nt(eye(w_value.shape[0]), w_value[...]).astype(bf16)
    for i, line in enumerate((norm_in, norm_mid)):
        gains[i : i + 1] = line[...].astype(f32).reshape(1, line.shape[0])
    keys, tokens = key_doc.shape[0], query_doc.shape[0]
    span = tokens // 2
    place, half = lax.axis_index("blk"), lax.axis_size("blk") // 2
    row = place // half
    own, mate = place * span, (place ^ 1) * span
    far, far_mate = (place ^ half) * span, (place ^ half ^ 1) * span
    found = in_doc(doc_lengths, row, (own, mate, far, far_mate), span, (keys, 128), 0)
    key_doc[...] = (found - 1.0).astype(bf16)
    mine = jnp.concatenate([found[0:span], found[tokens : tokens + span]], axis=0)
    query_doc[...] = (mine * FAR).astype(bf16)
    mates = jnp.concatenate([found[span:tokens], found[tokens + span : keys]], axis=0)
    spare = SPARE
    low = iota((keys, 128), 1) < spare
    ordered = pltpu.roll(jnp.concatenate([mine, mates], axis=0), spare, 1)
    side_key_doc[...] = jnp.where(low, 0.0, ordered - 1.0).astype(bf16)
    side_query_doc[...] = (in_doc(doc_lengths, row, (own, far), span, (16, tokens), 1) * FAR).astype(bf16)


def project(tokens, gain, w_query, w_key, value_t, queries):
    normed = norm_lanes(tokens.astype(f32), gain).astype(bf16)
    query = nn(normed[0:queries], w_query[...]).astype(bf16)
    return query, nn(normed, w_key[...]).astype(bf16), nt(value_t[...], normed).astype(bf16)


def padded(value_t, head):
    ones = jnp.ones((16, value_t.shape[1]), bf16)
    pieces = []
    for at in range(0, value_t.shape[0], head):
        pieces += [value_t[at : at + head], ones]
    return jnp.concatenate(pieces, axis=0)


def pair_lanes(j):
    return pl.ds(pl.multiple_of(j * 128, 128), 128)


def pair_sums(j, queries, query_doc, keys, key_doc, values, shifted=False):
    width = queries[0].shape[1]
    head = width // HEADS
    stride = values[0].shape[0] // HEADS
    lanes = pair_lanes(j)
    key = jnp.concatenate([ref[:, lanes] for ref in keys], axis=0)
    key = jnp.concatenate([key, key_doc], axis=1)
    query = jnp.concatenate([ref[:, lanes] for ref in queries], axis=0)
    rows = pl.ds(pl.multiple_of(j * 2 * stride, 16), 2 * stride)
    value = jnp.concatenate([ref[rows, :] for ref in values], axis=1)
    lane = iota((1, 128), 1) // head
    masked = [jnp.concatenate([query * ones_where(lane == i), query_doc], axis=1) for i in range(2)]
    count = query.shape[0]

    scores = nt(key, jnp.concatenate(masked, axis=0)) * (LOG2E * head**-0.5)
    if shifted:
        scores = scores - jnp.max(scores, axis=0, keepdims=True)
    both = nn(value, jnp.exp2(scores).astype(bf16))
    return [both[i * stride : i * stride + head + 8, i * count : (i + 1) * count] for i in range(2)]


def first_body(own, mate, gains, w_query, w_key, value_t, key_doc, query_doc, query, key, value, part):
    _, span, width = own.shape
    head = width // HEADS
    row = lax.axis_index("blk") // (lax.axis_size("blk") // 2)
    tokens = jnp.concatenate([own[row], mate[row]], axis=0)
    query[...], key[...], value_new = project(
        tokens, gains[0:1], w_query, w_key, value_t, span
    )
    value[...] = padded(value_new, head)

    def pair(j, carry):
        sums = pair_sums(j, [query], query_doc[0:span], [key], key_doc[0 : 2 * span], [value])
        part[j] = jnp.concatenate(sums, axis=0)
        return carry

    lax.fori_loop(0, HEADS // 2, pair, 0, unroll=6)


def out_of_range(totals):
    lowest, highest = jnp.min(totals), jnp.max(totals)
    return jnp.logical_not((lowest > LOW_TOTAL) & (highest < HIGH_TOTAL))


def second_body(
    far,
    far_mate,
    gains,
    w_query,
    w_key,
    value_t,
    key_doc,
    query_doc,
    query_a,
    key_a,
    value_a,
    part_a,
    attended,
    query,
    key,
    value,
    totals,
):
    span, width = far.shape
    head = width // HEADS
    tokens = jnp.concatenate([far[...], far_mate[...]], axis=0)
    query[...], key[...], value_new = project(
        tokens, gains[0:1], w_query, w_key, value_t, span
    )
    value[...] = padded(value_new, head)
    keys, values, queries = [key_a, key], [value_a, value], [query_a, query]

    def finish(j, sums):
        results = []
        for i, summed in enumerate(sums):
            totals[pl.ds(pl.multiple_of((2 * j + i) * 8, 8), 8), :] = summed[head : head + 8]
            results.append(summed[0:head] * (1.0 / summed[head : head + 1]))
        attended[:, pair_lanes(j)] = jnp.concatenate(results, axis=0).T.astype(bf16)

    def pair(j, carry):
        old = pair_sums(j, [query_a], query_doc[0:span], [key], key_doc[2 * span : 4 * span], [value])
        new = pair_sums(j, [query], query_doc[span : 2 * span], keys, key_doc[...], values)
        sums = []
        for i in range(2):
            rows = slice(i * (head + 8), (i + 1) * (head + 8))
            sums.append(jnp.concatenate([old[i] + part_a[j, rows], new[i]], axis=1))
        finish(j, sums)
        return carry

    lax.fori_loop(0, HEADS // 2, pair, 0, unroll=6)

    @pl.when(out_of_range(totals[...]))
    def _():
        def again(j, carry):
            finish(j, pair_sums(j, queries, query_doc[...], keys, key_doc[...], values, shifted=True))
            return carry

        lax.fori_loop(0, HEADS // 2, again, 0)


def dense_body(
    own, far, attended, gains, w_out, w_inner, w_outer, down_w, columns, state, side_far, out_own, out_far, sn_rows, sn_t, mixed_t, lead_t
):
    _, span, width = own.shape
    row = lax.axis_index("blk") // (lax.axis_size("blk") // 2)
    tokens = jnp.concatenate([own[row], far[...]], axis=0)
    after = tokens.astype(f32) + nn(attended[...], w_out[...])
    middle = norm_lanes(after, gains[1:2]).astype(bf16)
    result = after
    for at in range(0, w_inner.shape[1], width):
        act = gelu(nn(middle, w_inner[:, at : at + width])).astype(bf16)
        result = result + nn(act, w_outer[at : at + width, :])
    out = result.astype(bf16)
    out_own[...] = out[0:span]
    out_far[...] = out[span : 2 * span]

    side = state.shape[1]
    down_t = nt(down_w[...], out)
    state_t = jnp.concatenate([state[row], side_far[0:side]], axis=1).astype(f32)
    gate_open = jax.nn.sigmoid(columns[:, 0:1])
    mixed = gate_open * down_t + (1.0 - gate_open) * state_t
    normed = (
        mixed * lax.rsqrt(jnp.mean(mixed * mixed, axis=0, keepdims=True) + EPS) * columns[:, 1:2]
    )
    mixed_t[...] = mixed
    lead_t[...] = down_t - state_t
    sn_t[...] = normed.astype(bf16)
    sn_rows[...] = normed.T.astype(bf16)


def outer_rows(left, right):
    return jnp.concatenate([left[f : f + 1] * right for f in range(left.shape[0])], axis=0)


def inner_rows(left, products):
    count = left.shape[0]
    total = left[0:1] * products[0:count]
    for f in range(1, count):
        total = total + left[f : f + 1] * products[f * count : (f + 1) * count]
    return total


def two_parts(value):
    high = value.astype(bf16).astype(f32)
    return [high, value - high]


def side_body(
    sn_own,
    sn_mate,
    mixed_t,
    cot,
    side_far,
    dup,
    dup_t,
    tall_t,
    s_outer_t,
    s_out,
    s_inner,
    columns,
    key_doc,
    query_doc,
    thin_query,
    dkv_own,
    dkv_mate,
    dmid_t,
    attn_t,
    inverse,
    moments,
    mid_t,
    inner_t,
    normed_t,
    dinner_t,
    dnormed_t,
    dattn_t,
    weights,
    keys,
    key_t,
    value_t,
    query_t,
    query_s,
    totals,
    back_rows,
    dkv_t,
):
    tokens, side = sn_own.shape
    feature = side // SHEADS
    hidden = s_inner.shape[1]
    wide = 2 * side
    row = lax.axis_index("blk") // (lax.axis_size("blk") // 2)
    scale = feature**-0.5

    sn = jnp.concatenate([sn_own[...], sn_mate[...]], axis=0)
    keys[...] = nn(sn, dup[...]).astype(bf16) + key_doc[...]
    key_t[...] = nt(dup_t[wide : 2 * wide], sn).astype(bf16)
    second = iota((wide, 2 * tokens), 0) % (2 * feature) >= feature
    value_t[...] = jnp.where(second, 1.0, nt(dup_t[2 * wide : 3 * wide], sn)).astype(bf16)
    query = nt(dup_t[0:wide], sn_own[...]).astype(bf16)
    query_t[...] = query
    query_s[0:side] = nt(thin_query[...], sn_own[...]).astype(bf16)
    query_s[side : side + 16] = query_doc[...]
    query_s[side + 16 :] = jnp.zeros((128 - side - 16, tokens), bf16)
    owner = iota((128, 1), 0) // feature

    def head_rows(h, count):
        return pl.ds(pl.multiple_of(h * count, count), count)

    def attend(shifted, size):
        def group(j, carry):
            for i in range(size):
                h = size * j + i
                rows, eight = head_rows(h, 16), head_rows(h, 8)
                mine = ones_where((owner == h) | (owner >= SHEADS))
                scores = nn(keys[...], query_s[...] * mine) * (scale * LOG2E)
                if shifted:
                    scores = scores - jnp.max(scores, axis=0, keepdims=True)
                weight = jnp.exp2(scores).astype(bf16)
                weights[h] = weight.T
                value, key = value_t[rows, :], key_t[rows, :]
                products = outer_rows(value[0:feature].astype(f32), key[0:feature].astype(f32))
                products = jnp.concatenate(two_parts(products), axis=0).astype(bf16)
                summed = nn(jnp.concatenate([value, key, products], axis=0), weight)
                total = summed[feature : 2 * feature]
                totals[eight, :] = total
                invert = 1.0 / total
                inverse[eight, :] = invert
                attn_t[eight, :] = summed[0:feature] * invert
                at = 4 * feature + feature * feature
                moments[h] = jnp.concatenate(
                    [summed[2 * feature : 4 * feature], summed[4 * feature : at] + summed[at:]], axis=0
                )
            return carry

        lax.fori_loop(0, SHEADS // size, group, 0)

    attend(False, SHEADS)

    @pl.when(out_of_range(totals[...]))
    def _():
        attend(True, 2)

    attn = attn_t[...]
    attn_low = attn.astype(bf16)
    mid = mixed_t[...] + nn(tall_t[0:side], attn_low)
    mid_scale = lax.rsqrt(jnp.mean(mid * mid, axis=0, keepdims=True) + EPS)
    gain = columns[:, 2:3]
    unit = mid * mid_scale
    normed = (unit * gain).astype(bf16)
    inner = nn(tall_t[side : side + hidden], normed)
    dy_low = jnp.concatenate([cot[row], side_far[side : 2 * side]], axis=1)
    dinner = (gelu_slope(inner) * tn(s_outer_t[...], dy_low)).astype(bf16)
    dnormed = nn(s_inner[...], dinner)
    scaled = dnormed * gain
    dmid = dy_low.astype(f32) + mid_scale * (
        scaled - unit * jnp.mean(scaled * unit, axis=0, keepdims=True)
    )
    dmid_t[...] = dmid
    dattn = nn(s_out[...], dmid.astype(bf16)).astype(bf16).astype(f32)
    mid_t[...] = mid
    inner_t[...] = inner
    normed_t[...] = normed
    dinner_t[...] = dinner
    dnormed_t[...] = dnormed
    dattn_t[...] = dattn

    for h in range(SHEADS):
        eight = slice(h * feature, (h + 1) * feature)
        invert = inverse[eight, :]
        term = jnp.sum(dattn[eight] * attn[eight], axis=0, keepdims=True)
        query = query_t[2 * h * feature : 2 * (h + 1) * feature].astype(f32)[0:feature]
        share = dattn[eight] * invert
        back_rows[h] = jnp.concatenate(
            two_parts(share) + two_parts(term * invert * query) + two_parts(outer_rows(share, query)), axis=0
        ).astype(bf16)

    for h in range(SHEADS):
        eight = slice(h * feature, (h + 1) * feature)
        summed = nn(back_rows[h], weights[h])
        dkv_t[side + h * feature : side + (h + 1) * feature] = (
            summed[0:feature] + summed[feature : 2 * feature]
        )
        value = value_t[2 * h * feature : 2 * (h + 1) * feature].astype(f32)[0:feature]
        at = 4 * feature + feature * feature
        raw = inner_rows(value, summed[4 * feature : at] + summed[at:])
        raw = raw - (summed[2 * feature : 3 * feature] + summed[3 * feature : 4 * feature])
        dkv_t[eight] = raw * scale
    dkv_own[...] = dkv_t[:, 0:tokens]
    dkv_mate[...] = dkv_t[:, tokens : 2 * tokens].astype(bf16)


def aside_body(
    attn_t,
    inverse,
    moments,
    mid_t,
    inner_t,
    normed_t,
    dinner_t,
    dnormed_t,
    dattn_t,
    dmid_t,
    cot,
    side_far,
    s_outer_t,
    out_own,
    out_far,
    dquery,
    early,
):
    side, tokens = mid_t.shape
    span = tokens // 2
    feature = side // SHEADS
    hidden = inner_t.shape[0]
    row = lax.axis_index("blk") // (lax.axis_size("blk") // 2)
    mid = mid_t[...]
    act = gelu(inner_t[...]).astype(bf16)
    out = (mid + nn(s_outer_t[...], act)).astype(bf16)
    out_own[...] = out[:, 0:span]
    out_far[...] = out[:, span : 2 * span]
    dy_low = jnp.concatenate([cot[row], side_far[side : 2 * side]], axis=1)
    early[:, 0:hidden] = nt(normed_t[...], dinner_t[...])
    early[:, hidden : 2 * hidden] = nt(dy_low, act)
    unit = mid * lax.rsqrt(jnp.mean(mid * mid, axis=0, keepdims=True) + EPS)
    grad_gain = jnp.sum(dnormed_t[...] * unit, axis=1, keepdims=True)
    last = nt(attn_t[...].astype(bf16), dmid_t[...].astype(bf16))
    last = jnp.concatenate([last, jnp.zeros((side, 128 - side), f32)], axis=1)
    early[:, 2 * hidden : 2 * hidden + 128] = jnp.where(
        iota((side, 128), 1) == side, grad_gain, last
    )
    for h in range(SHEADS):
        eight = slice(h * feature, (h + 1) * feature)
        dattn = dattn_t[eight, :]
        term = jnp.sum(dattn * attn_t[eight, :], axis=0, keepdims=True)
        moment = moments[h]
        raw = inner_rows(dattn, moment[2 * feature :]) - term * moment[0:feature]
        dquery[eight, :] = raw * inverse[eight, :] * feature**-0.5


def last_body(
    dquery,
    dkv_own,
    dkv_back,
    sn_t,
    dmid_t,
    mixed_t,
    lead_t,
    out_own,
    out_far,
    s_query,
    s_key,
    s_value,
    columns,
    early,
    side_out_far,
    state_own,
    far,
    keep,
    send,
    pack,
):
    side, tokens = sn_t.shape
    span = tokens // 2
    width = out_own.shape[1]
    dq = dquery[...].astype(bf16)
    dkv = (dkv_own[...].astype(bf16).astype(f32) + dkv_back[...].astype(f32)).astype(bf16)
    dk, dv = dkv[0:side], dkv[side : 2 * side]
    sn = sn_t[...]
    dnormed = nn(s_query[...], dq) + nn(s_key[...], dk) + nn(s_value[...], dv)
    mixed = mixed_t[...]
    mixed_scale = lax.rsqrt(jnp.mean(mixed * mixed, axis=0, keepdims=True) + EPS)
    unit = mixed * mixed_scale
    scaled = dnormed * columns[:, 1:2]
    dmixed = dmid_t[...] + mixed_scale * (
        scaled - unit * jnp.mean(scaled * unit, axis=0, keepdims=True)
    )
    gate_open = jax.nn.sigmoid(columns[:, 0:1])
    grad_gain = jnp.sum(dnormed * unit, axis=1, keepdims=True)
    grad_gate = jnp.sum(dmixed * lead_t[...], axis=1, keepdims=True) * gate_open * (1.0 - gate_open)
    state = (1.0 - gate_open) * dmixed
    state_own[...] = state[:, 0:span]
    far[0:side] = side_out_far[...]
    far[side : 2 * side] = state[:, span:tokens].astype(bf16)
    ddown = (gate_open * dmixed).astype(bf16)
    pack[:, 0:width] = nn(ddown[:, 0:span], out_own[...]) + nn(ddown[:, span:tokens], out_far[...])
    at = width
    blank = jnp.zeros((side, 128 - side), f32)
    for grad in (dq, dk, dv):
        pack[:, at : at + 128] = jnp.concatenate([nt(sn, grad), blank], axis=1)
        at += 128
    lane = iota((side, 128), 1)
    inner = early.shape[1] - 128
    vectors = early[:, inner : inner + 128]
    vectors = jnp.where(lane == side + 1, grad_gain, vectors)
    pack[:, at : at + 128] = jnp.where(lane == side + 2, grad_gate, vectors)
    pack[:, at + 128 : at + 128 + inner] = early[:, 0:inner]
    size = keep.shape[1]
    core = lax.axis_index("blk") % 2
    keep[...] = pack[:, pl.ds(pl.multiple_of(core * size, 128), size)].astype(bf16)
    send[...] = pack[:, pl.ds(pl.multiple_of((1 - core) * size, 128), size)].astype(bf16)


def quarter_index():
    return (lax.axis_index("blk") // 2) % 2 + 2 * (lax.axis_index("dp") % 2)


def spread_body(*refs):
    pieces, refs = refs[0:8], refs[8:]
    (
        grad_down,
        grad_gate,
        gain_in,
        grad_query,
        grad_key,
        grad_value,
        grad_out,
        gain_mid,
        grad_inner,
        grad_outer,
        pack,
    ) = refs
    side, width = grad_down.shape
    hidden = grad_inner.shape[1]
    size = pieces[0].shape[1]
    core, quarter = lax.axis_index("blk") % 2, quarter_index()
    for i, piece in enumerate(pieces):
        at = ((core ^ (i // 4)) * 4 + (quarter ^ (i % 4))) * size
        pack[:, pl.ds(pl.multiple_of(at, 128), size)] = piece[...]
    whole = pack[...].astype(f32)
    grad_down[...] = whole[:, 0:width]
    at = width
    for target in (grad_query, grad_key, grad_value):
        target[...] = whole[:, at : at + side]
        at += 128
    block = whole[:, at : at + 128]
    grad_out[...] = block[:, 0:side]
    rows = block.T
    gain_mid[...] = rows[side : side + 1]
    gain_in[...] = rows[side + 1 : side + 2]
    grad_gate[...] = rows[side + 2 : side + 3]
    at += 128
    grad_inner[...] = whole[:, at : at + hidden]
    grad_outer[...] = whole[:, at + hidden : at + 2 * hidden]


def per_device(
    hidden,
    side_state,
    doc_lengths,
    norm_in,
    w_query,
    w_key,
    w_value,
    w_out,
    norm_mid,
    w_inner,
    w_outer,
    w_down,
    gate,
    side_norm_in,
    s_query,
    s_key,
    s_value,
    s_out,
    side_norm_mid,
    s_inner,
    s_outer,
    cotangent,
):
    span, rows, width = hidden.shape
    side = side_state.shape[2]
    ff = w_inner.shape[1]
    sff = s_inner.shape[1]
    tokens = 2 * span
    feature = side // SHEADS
    blk_size, dp_size = lax.axis_size("blk"), lax.axis_size("dp")
    half = blk_size // 2
    place = lax.axis_index("blk")
    row = place // half

    def swap(value, axis, size, hop):
        return lax.ppermute(value, axis, [(i, i ^ hop) for i in range(size)])

    def across(value):
        return swap(value, "blk", blk_size, half)

    def beside(value):
        return swap(value, "blk", blk_size, 1)

    hidden = jnp.transpose(hidden, (1, 0, 2))
    hidden_far = across(lax.dynamic_index_in_dim(hidden, 1 - row, 0, keepdims=False))
    hidden_mate = beside(hidden)
    state, cot = (jnp.transpose(array, (1, 2, 0)) for array in (side_state, cotangent))
    side_far = across(
        lax.dynamic_index_in_dim(jnp.concatenate([state, cot], axis=1), 1 - row, 0, keepdims=False)
    )
    down_w, s_outer_t = w_down.T, s_outer.T

    value_t, gains, key_doc, query_doc, side_key_doc, side_query_doc = kernel_call(
        prepare_body,
        [
            ((width, width), bf16),
            ((2, width), f32),
            ((2 * tokens, 128), bf16),
            ((tokens, 128), bf16),
            ((2 * tokens, 128), bf16),
            ((16, tokens), bf16),
        ],
        [doc_lengths, w_value, norm_in, norm_mid],
        vmem=16,
        scalars=(0,),
        cost=(1000, 1000, 0),
    )
    head = width // HEADS
    stride = head + 16
    projections = (gains, w_query, w_key, value_t, key_doc, query_doc)

    def state_of(queries, keys, columns):
        return [
            ((queries, width), bf16),
            ((keys, width), bf16),
            ((HEADS * stride, keys), bf16),
            ((HEADS // 2, 2 * (head + 8), columns), f32),
        ]

    state_a = kernel_call(
        first_body,
        state_of(span, tokens, span),
        [hidden, hidden_mate, *projections],
        vmem=24,
        cost=(1000, 1000, 0),
    )
    small = (s_query, s_key, s_value, s_out, s_inner, gate, side_norm_in, side_norm_mid)
    hidden_far, small, *state_a = lax.optimization_barrier((hidden_far, small, *state_a))
    dup, dup_t, tall_t, columns, s_query_t = kernel_call(
        side_weights_body,
        [
            ((side, 128), bf16),
            ((6 * side, side), bf16),
            ((side + sff, side), bf16),
            ((side, 128), f32),
            ((side, side), bf16),
        ],
        small,
        vmem=8,
        scratch=[pltpu.VMEM((128, 128), f32)],
        cost=(1000, 1000, 0),
    )
    (attended,) = kernel_call(
        second_body,
        [((tokens, width), bf16)],
        [hidden_far, beside(hidden_far), *projections, *state_a],
        vmem=30,
        scratch=[
            pltpu.VMEM((span, width), bf16),
            pltpu.VMEM((tokens, width), bf16),
            pltpu.VMEM((HEADS * stride, tokens), bf16),
            pltpu.VMEM((HEADS * 8, tokens), f32),
        ],
        cost=(8 * 10**9, 8 * 10**6, 0),
    )
    side_far, attended = lax.optimization_barrier((side_far, attended))
    out_own, out_far, sn_rows, sn_t, mixed_t, lead_t = kernel_call(
        dense_body,
        [
            ((span, width), bf16),
            ((span, width), bf16),
            ((tokens, side), bf16),
            ((side, tokens), bf16),
            ((side, tokens), f32),
            ((side, tokens), f32),
        ],
        [
            hidden,
            hidden_far,
            attended,
            gains,
            w_out,
            w_inner,
            w_outer,
            down_w,
            columns,
            state,
            side_far,
        ],
        vmem=28,
        cost=(10 * 10**9, 14 * 10**6, 0),
    )
    sn_mate = beside(sn_rows)
    out_back = across(out_far)
    dkv_own, dkv_mate, dmid_t, *carried = kernel_call(
        side_body,
        [
            ((2 * side, tokens), f32),
            ((2 * side, tokens), bf16),
            ((side, tokens), f32),
            ((side, tokens), f32),
            ((side, tokens), f32),
            ((SHEADS, feature * (feature + 2), tokens), f32),
            ((side, tokens), f32),
            ((sff, tokens), f32),
            ((side, tokens), bf16),
            ((sff, tokens), bf16),
            ((side, tokens), f32),
            ((side, tokens), f32),
        ],
        [
            sn_rows,
            sn_mate,
            mixed_t,
            cot,
            side_far,
            dup,
            dup_t,
            tall_t,
            s_outer_t,
            s_out,
            s_inner,
            columns,
            side_key_doc,
            side_query_doc,
            s_query_t,
        ],
        vmem=36,
        scratch=[
            pltpu.VMEM((SHEADS, tokens, 2 * tokens), bf16),
            pltpu.VMEM((2 * tokens, 128), bf16),
            pltpu.VMEM((2 * side, 2 * tokens), bf16),
            pltpu.VMEM((2 * side, 2 * tokens), bf16),
            pltpu.VMEM((2 * side, tokens), bf16),
            pltpu.VMEM((128, tokens), bf16),
            pltpu.VMEM((side, tokens), f32),
            pltpu.VMEM((SHEADS, feature * (2 * feature + 4), tokens), bf16),
            pltpu.VMEM((2 * side, 2 * tokens), f32),
        ],
        cost=(30 * 10**9, 3 * 10**6, 0),
    )
    dkv_back = beside(dkv_mate)
    side_own, side_back, dquery, early = kernel_call(
        aside_body,
        [
            ((side, span), bf16),
            ((side, span), bf16),
            ((side, tokens), f32),
            ((side, 2 * sff + 128), f32),
        ],
        [*carried, dmid_t, cot, side_far, s_outer_t],
        vmem=12,
        cost=(10**9, 6 * 10**6, 0),
    )
    dkv_back, out_back = lax.optimization_barrier((dkv_back, out_back))
    packed = width + 4 * 128 + 2 * sff
    grad_own, far, keep, send = kernel_call(
        last_body,
        [
            ((side, span), f32),
            ((2 * side, span), bf16),
            ((side, packed // 2), bf16),
            ((side, packed // 2), bf16),
        ],
        [
            dquery,
            dkv_own,
            dkv_back,
            sn_t,
            dmid_t,
            mixed_t,
            lead_t,
            out_own,
            out_far,
            s_query,
            s_key,
            s_value,
            columns,
            early,
            side_back,
        ],
        vmem=16,
        scratch=[pltpu.VMEM((side, packed), f32)],
        cost=(10**9, 3 * 10**6, 0),
    )

    def add(*terms):
        total = terms[0].astype(f32)
        for term in terms[1:]:
            total = total + term.astype(f32)
        return total.astype(bf16)

    quarter = packed // 8
    mine = quarter_index()
    devices = dp_size * blk_size

    def between(value, chip):
        mask = 2 * (chip % 2) + blk_size * (chip // 2)
        return lax.ppermute(value, ("dp", "blk"), [(i, i ^ mask) for i in range(devices)])

    def part(value, index):
        return lax.dynamic_slice_in_dim(value, index * quarter, quarter, 1)

    total = add(keep, beside(send))
    total = add(part(total, mine), *[between(part(total, mine ^ chip), chip) for chip in (1, 2, 3)])
    total, far = lax.optimization_barrier((total, far))
    hop = 2
    while hop < dp_size:
        total = add(total, swap(total, "dp", dp_size, hop))
        hop *= 2
    pieces = [total] + [between(total, chip) for chip in (1, 2, 3)]
    pieces += [beside(piece) for piece in pieces]
    vector = ((1, side), f32)
    square = ((side, side), f32)
    grads = kernel_call(
        spread_body,
        [
            ((side, width), f32),
            vector,
            vector,
            square,
            square,
            square,
            square,
            vector,
            ((side, sff), f32),
            ((side, sff), f32),
        ],
        pieces,
        vmem=16,
        scratch=[pltpu.VMEM((side, packed), bf16)],
        cost=(0, 2 * 10**6, 0),
    )
    grads = [grad.reshape(side) if grad.shape[0] == 1 else grad for grad in grads]
    grads[0], grads[-1] = grads[0].T, grads[-1].T

    def both_rows(own, back):
        first = jnp.where(row == 0, own, back)
        second = jnp.where(row == 0, back, own)
        return jnp.stack([first, second])

    far = across(far)
    return (
        jnp.transpose(both_rows(out_own, out_back), (1, 0, 2)),
        jnp.transpose(both_rows(side_own, far[0:side]), (2, 0, 1)),
        jnp.transpose(both_rows(grad_own, far[side : 2 * side].astype(f32)), (2, 0, 1)),
        *grads,
    )


def solution(mesh):
    split = P("blk", "dp", None)
    return jax.shard_map(
        per_device,
        mesh=mesh,
        in_specs=(split, split, P("dp", None)) + (P(),) * 18 + (split,),
        out_specs=(split,) * 3 + (P(),) * 10,
        check_vma=False,
    )
```
